32 devices in a mesh: wide: 16 (over z, x, core), narrow: 2 (over y).
Axes of the slice: x: 2, y: 2, z: 4, core: 2. Of those that a mesh axis runs over, the one named last changes fastest.
Arguments:
- tokens: bfloat16 [32, 532, 1024], P('wide'), may hold values from -6 to 6
- cotangent: bfloat16 [32, 532, 1024], P('wide'), may hold values from -6 to 6
- doc_ids: int32 [32, 512], P('wide'), may hold values from 0 to 7, never falling along the last dimension, each value on 1 to 128 neighbouring positions
- reset_flags: int32 [32, 8], P('wide'), may hold values 0 or 1
- mem_live: int32 [32], P('wide'), may hold values from 1 to 10
- qkv_weight: float32 [3, 1024, 1024], P(None, 'wide', 'narrow'), may hold values from -0.1875 to 0.1875
- qkv_moment: float32 [3, 1024, 1024], P(None, 'wide', 'narrow'), may hold values from -0.66 to 0.66
- qkv_square: float32 [3, 1024, 1024], P(None, 'wide', 'narrow'), may hold values from 0.0102 to 0.163
- qkv_average: float32 [3, 1024, 1024], P(None, 'wide', 'narrow'), may hold values from -0.1875 to 0.1875
- out_weight: float32 [1024, 1024], P('narrow', 'wide'), may hold values from -1.5 to 1.5
- out_moment: float32 [1024, 1024], P('narrow', 'wide'), may hold values from -0.66 to 0.66
- out_square: float32 [1024, 1024], P('narrow', 'wide'), may hold values from 0.002 to 0.008
- out_average: float32 [1024, 1024], P('narrow', 'wide'), may hold values from -1.5 to 1.5
- up_weight: float32 [1024, 4096], P('wide', 'narrow'), may hold values from -0.1875 to 0.1875
- up_moment: float32 [1024, 4096], P('wide', 'narrow'), may hold values from -0.66 to 0.66
- up_square: float32 [1024, 4096], P('wide', 'narrow'), may hold values from 0.0102 to 0.163
- up_average: float32 [1024, 4096], P('wide', 'narrow'), may hold values from -0.1875 to 0.1875
- down_weight: float32 [4096, 1024], P('narrow', 'wide'), may hold values from -0.09375 to 0.09375
- down_moment: float32 [4096, 1024], P('narrow', 'wide'), may hold values from -0.66 to 0.66
- down_square: float32 [4096, 1024], P('narrow', 'wide'), may hold values from 0.0102 to 0.163
- down_average: float32 [4096, 1024], P('narrow', 'wide'), may hold values from -0.09375 to 0.09375
- norm_params: float32 [4, 1024], P(None, 'wide'), may hold values from -1.2 to 1.5
- norm_moment: float32 [4, 1024], P(None, 'wide'), may hold values from -2.64 to 2.64
- norm_square: float32 [4, 1024], P(None, 'wide'), may hold values from 0.16 to 2.6
- norm_average: float32 [4, 1024], P(None, 'wide'), may hold values from -1.2 to 1.5
Outputs:
- output: bfloat16 [32, 532, 1024], P('wide')
- input_grad: float32 [32, 532, 1024], P('wide')
- grad_norm: float32 [], replicated
- new_qkv: float32 [3, 1024, 1024], P(None, 'wide', 'narrow')
- new_qkv_moment: float32 [3, 1024, 1024], P(None, 'wide', 'narrow')
- new_qkv_square: float32 [3, 1024, 1024], P(None, 'wide', 'narrow')
- new_qkv_average: float32 [3, 1024, 1024], P(None, 'wide', 'narrow')
- new_out: float32 [1024, 1024], P('narrow', 'wide')
- new_out_moment: float32 [1024, 1024], P('narrow', 'wide')
- new_out_square: float32 [1024, 1024], P('narrow', 'wide')
- new_out_average: float32 [1024, 1024], P('narrow', 'wide')
- new_up: float32 [1024, 4096], P('wide', 'narrow')
- new_up_moment: float32 [1024, 4096], P('wide', 'narrow')
- new_up_square: float32 [1024, 4096], P('wide', 'narrow')
- new_up_average: float32 [1024, 4096], P('wide', 'narrow')
- new_down: float32 [4096, 1024], P('narrow', 'wide')
- new_down_moment: float32 [4096, 1024], P('narrow', 'wide')
- new_down_square: float32 [4096, 1024], P('narrow', 'wide')
- new_down_average: float32 [4096, 1024], P('narrow', 'wide')
- new_norms: float32 [4, 1024], P(None, 'wide')
- new_norm_moment: float32 [4, 1024], P(None, 'wide')
- new_norm_square: float32 [4, 1024], P(None, 'wide')
- new_norm_average: float32 [4, 1024], P(None, 'wide')
The draws below stay inside these ranges and needn't reach their ends.
Inputs may be any that keep to these rules, and one draw needn't show every extreme that they name: `doc_ids`: document numbers never fall along a segment; every document 0 to 7 has 1 to 128 tokens.
All inputs are finite; a program needn't handle non-finite values. No bound on the sum of `reset_flags` on one device may be relied on, other than what follows from the above.
Results may differ from the reference program's by a relative error of at most 0.01.
The reference program's roundings to bfloat16 on the way count: a program that leaves them out, or rounds other values in their place, can miss the bound.
Values may be sent and summed in bfloat16 or wider, within the bound.
No kernel may reach another device: no remote copies, remote signals or barrier semaphores. Data moves between devices by JAX's collectives and lax.ppermute only.
A program may use at most 192 MiB of HBM per device.

```python
import math
import jax
import jax.numpy as jnp
import numpy as np
from jax import lax

D = 1024
HEADS = 16
HEAD = 64
FF = 4096
MEM = 10
SEG_LEN = 512
DOCS = 8
DOC_MOST = 128
STEP = 10
ROWS = 532
SEGS = 32


def norm_rows(key):
    first_key, second_key = jax.random.split(key)
    gains = jax.random.uniform(first_key, (2, D), jnp.float32, 0.5, 1.5)
    shifts = jnp.clip(0.3 * jax.random.normal(second_key, (2, D), jnp.float32), -1.2, 1.2)
    return jnp.stack([gains[0], shifts[0], gains[1], shifts[1]])


def draw_norm_params(key, part):
    return norm_rows(jax.random.fold_in(key, 11))


def draw_norm_average(key, part):
    return norm_rows(jax.random.fold_in(key, 23))


def with_ends(drawn, key, least, largest):
    longest = drawn.shape.index(max(drawn.shape))
    spots = []
    for shift in (0, 1):
        where = [jax.random.randint(jax.random.fold_in(key, axis), (), 0, length) for axis, length in enumerate(drawn.shape)]
        where[longest] = (where[longest] + shift) % drawn.shape[longest]
        spots.append(tuple(where))
    return drawn.at[spots[0]].set(least).at[spots[1]].set(largest)


def levels(rng, extent, pieces, smallest, top_value):
    level, own = 1.0, jax.random.fold_in(rng, 6)
    for axis_at, blocks in pieces:
        steps = jnp.exp(jax.random.uniform(jax.random.fold_in(own, axis_at), (blocks,), jnp.float32, smallest / len(pieces), top_value / len(pieces)))
        level = level * jnp.repeat(steps, extent[axis_at] // blocks).reshape([-1 if axis == axis_at else 1 for axis in range(len(extent))])
    return level


def profile(amount, total, bound, skew):
    portions = [(1 << 20) // math.isqrt(standing ** skew) + 1 for standing in range(2, amount + 1)]
    surplus, holding = total - bound - (amount - 1), [1] * (amount - 1)
    while surplus > 0:
        candidates = [i for i in range(amount - 1) if holding[i] < bound]
        pool, remaining = sum([portions[i] for i in candidates]), surplus
        for i in candidates:
            extra = min(bound - holding[i], max(1, remaining * portions[i] // pool), surplus)
            holding[i] = holding[i] + extra
            surplus = surplus - extra
    return np.array([bound] + holding)


def ragged(own_key, count, total, reach, skew):
    if count == 2:
        one = jax.random.randint(own_key, (), max(1, total - reach), min(reach, total - 1) + 1)
        return jnp.stack([one, total - one])
    sizes = jnp.asarray(profile(count, total, reach, skew), jnp.int32)
    couples = (count - 1) // 2
    source_of, receiver = sizes[1:1 + 2 * couples:2], sizes[2:2 + 2 * couples:2]
    margin = jnp.minimum(source_of - 1, reach - receiver)
    passed = jax.random.randint(jax.random.fold_in(own_key, 1), (couples,), 0, 1 << 20) % (margin + 1)
    sizes = sizes.at[1:1 + 2 * couples:2].set(source_of - passed).at[2:2 + 2 * couples:2].set(receiver + passed)
    return sizes[jax.random.permutation(jax.random.fold_in(own_key, 2), count)]


def normal_values(key, dims, deviation, limit, pieces=(), kind=jnp.bfloat16):
    entries = jax.random.normal(key, dims, jnp.float32) * deviation
    if len(pieces) > 0:
        entries = levels(key, dims, pieces, -0.22, 0.18) * entries
    return jnp.clip(entries, min=-limit, max=limit).astype(kind)


def setup_inputs(seed: int = 0) -> dict:
    splits = jax.random.split(jax.random.key(seed), 26)
    return {
        "tokens": normal_values(splits[0], (SEGS, ROWS, D), 1.0, 6.0, ((0, 16),)),
        "cotangent": normal_values(splits[1], (SEGS, ROWS, D), 1.0, 6.0, ((0, 16),)),
        "doc_ids": jax.vmap(lambda own: jnp.searchsorted(jnp.cumsum(ragged(own, DOCS, SEG_LEN, DOC_MOST, 1)), jnp.arange(SEG_LEN), side="right"))(jax.random.split(splits[2], SEGS)).reshape((SEGS, SEG_LEN)).astype(jnp.int32),
        "reset_flags": with_ends((jax.random.randint(splits[3], (SEGS, DOCS), 0, 2) < 1).astype(jnp.int32), jax.random.fold_in(splits[3], 1), 0, 1),
        "mem_live": with_ends(jax.random.randint(splits[4], (SEGS,), 1, MEM + 1), jax.random.fold_in(splits[4], 1), 1, MEM).astype(jnp.int32),
        "qkv_weight": normal_values(splits[5], (3, D, D), D ** -0.5, 0.1875, ((1, 16), (2, 2)), jnp.float32),
        "qkv_moment": normal_values(splits[6], (3, D, D), 0.11, 0.66, ((1, 16), (2, 2)), jnp.float32),
        "qkv_square": jnp.clip(jnp.exp(math.log(0.163) - 2.7713625 * jax.random.uniform(splits[7], (3, D, D), jnp.float32) ** levels(splits[7], (3, D, D), ((1, 16), (2, 2)), -0.2, 0.2)), 0.0102, 0.163),
        "qkv_average": normal_values(splits[8], (3, D, D), D ** -0.5, 0.1875, ((1, 16), (2, 2)), jnp.float32),
        "out_weight": normal_values(splits[9], (D, D), (D // 64) ** -0.5, 1.5, ((0, 2), (1, 16)), jnp.float32),
        "out_moment": normal_values(splits[10], (D, D), 0.11, 0.66, ((0, 2), (1, 16)), jnp.float32),
        "out_square": jnp.clip(jnp.exp(math.log(0.008) - 1.3862944 * jax.random.uniform(splits[11], (D, D), jnp.float32) ** levels(splits[11], (D, D), ((0, 2), (1, 16)), -0.2, 0.2)), 0.002, 0.008),
        "out_average": normal_values(splits[12], (D, D), (D // 64) ** -0.5, 1.5, ((0, 2), (1, 16)), jnp.float32),
        "up_weight": normal_values(splits[13], (D, FF), D ** -0.5, 0.1875, ((0, 16), (1, 2)), jnp.float32),
        "up_moment": normal_values(splits[14], (D, FF), 0.11, 0.66, ((0, 16), (1, 2)), jnp.float32),
        "up_square": jnp.clip(jnp.exp(math.log(0.163) - 2.7713625 * jax.random.uniform(splits[15], (D, FF), jnp.float32) ** levels(splits[15], (D, FF), ((0, 16), (1, 2)), -0.2, 0.2)), 0.0102, 0.163),
        "up_average": normal_values(splits[16], (D, FF), D ** -0.5, 0.1875, ((0, 16), (1, 2)), jnp.float32),
        "down_weight": normal_values(splits[17], (FF, D), FF ** -0.5, 0.09375, ((0, 2), (1, 16)), jnp.float32),
        "down_moment": normal_values(splits[18], (FF, D), 0.11, 0.66, ((0, 2), (1, 16)), jnp.float32),
        "down_square": jnp.clip(jnp.exp(math.log(0.163) - 2.7713625 * jax.random.uniform(splits[19], (FF, D), jnp.float32) ** levels(splits[19], (FF, D), ((0, 2), (1, 16)), -0.2, 0.2)), 0.0102, 0.163),
        "down_average": normal_values(splits[20], (FF, D), FF ** -0.5, 0.09375, ((0, 2), (1, 16)), jnp.float32),
        "norm_params": draw_norm_params(jax.random.fold_in(splits[25], 71), 0),
        "norm_moment": normal_values(splits[22], (4, D), 0.44, 2.64, ((1, 16),), jnp.float32),
        "norm_square": jnp.clip(jnp.exp(math.log(2.6) - 2.7880929 * jax.random.uniform(splits[23], (4, D), jnp.float32) ** levels(splits[23], (4, D), ((1, 16),), -0.2, 0.2)), 0.16, 2.6),
        "norm_average": draw_norm_average(jax.random.fold_in(splits[25], 71), 0),
    }


@jax.custom_vjp
def low(v):
    return lax.optimization_barrier(v.astype(jnp.bfloat16)).astype(jnp.float32)

@jax.custom_vjp
def low_back(v):
    return v

def low_keep(v):
    return (low(v), None)

def low_pass(kept, grad):
    return (grad,)

def back_keep(v):
    return (v, None)

def back_low(kept, grad):
    return (low(grad),)
low.defvjp(low_keep, low_pass)
low_back.defvjp(back_keep, back_low)
HIGHEST = lax.Precision.HIGHEST
NORM_EPS = 1e-12
BETA_ONE = 0.9
BETA_TWO = 0.98
ADAM_EPS = 1e-06
AVERAGE_KEEP = 0.75

def matmul_high(left, right):
    return jnp.dot(left, right, precision=HIGHEST, preferred_element_type=jnp.float32)

def layer_norm(rows_in, gain, shift):
    center = rows_in - lax.optimization_barrier(jnp.mean(rows_in, axis=-1, keepdims=True))
    spread = lax.optimization_barrier(jnp.mean(center * center, axis=-1, keepdims=True))
    return center * lax.rsqrt(spread + NORM_EPS) * gain + shift

def allowed_mask(doc_row, reset_row, live_count):
    kinds = jnp.concatenate([jnp.full((MEM,), -1, jnp.int32), doc_row.astype(jnp.int32), jnp.full((MEM,), -2, jnp.int32)])
    place = jnp.arange(ROWS, dtype=jnp.int32)
    read_key = place < MEM
    live_key = place < live_count
    choose = kinds[:, None] == jnp.arange(DOCS, dtype=jnp.int32)[None, :]
    reset_query = lax.optimization_barrier(jnp.sum(jnp.where(choose, reset_row[None, :].astype(jnp.int32), 0), axis=1))
    memory_query = kinds < 0
    same_doc = kinds[:, None] == kinds[None, :]
    token_sees = same_doc | (read_key & live_key)[None, :] & (reset_query == 0)[:, None]
    memory_sees = jnp.broadcast_to((~read_key | live_key)[None, :], (ROWS, ROWS))
    return jnp.where(memory_query[:, None], memory_sees, token_sees)

def layer(rows_in, w_query, w_key, w_value, w_out, w_up, w_down, norms, allowed):
    score_scale = 1.0 / math.sqrt(HEAD)
    query = low_back(low(matmul_high(rows_in, w_query))).reshape(ROWS, HEADS, HEAD)
    keys = low_back(low(matmul_high(rows_in, w_key))).reshape(ROWS, HEADS, HEAD)
    values = low_back(low(matmul_high(rows_in, w_value))).reshape(ROWS, HEADS, HEAD)
    scores = low_back(jnp.einsum('qhd,khd->hqk', query, keys, precision=HIGHEST) * score_scale)
    scores = jnp.where(allowed[None], scores, jnp.float32(-1e+30))
    probs = low(jax.nn.softmax(scores, axis=-1))
    context = jnp.einsum('hqk,khd->qhd', probs, values, precision=HIGHEST).reshape(ROWS, D)
    context = low_back(low(context))
    branch = low_back(matmul_high(context, w_out))
    hidden = layer_norm(rows_in + branch, norms[0], norms[1])
    inner = low_back(matmul_high(low(hidden), w_up))
    active = low(jax.nn.gelu(inner, approximate=False))
    feed = low_back(matmul_high(active, w_down))
    return layer_norm(hidden + feed, norms[2], norms[3])

def adam_step(weight, moment, square, average, grad, rate, decay):
    moment = BETA_ONE * moment + (1.0 - BETA_ONE) * grad
    square = BETA_TWO * square + (1.0 - BETA_TWO) * grad * grad
    first_hat = moment / (1.0 - BETA_ONE ** STEP)
    second_hat = square / (1.0 - BETA_TWO ** STEP)
    weight = weight - rate * (first_hat / (jnp.sqrt(second_hat) + ADAM_EPS) + decay * weight)
    average = AVERAGE_KEEP * average + (1.0 - AVERAGE_KEEP) * weight
    return (weight, moment, square, average)

def reference(tokens, cotangent, doc_ids, reset_flags, mem_live, qkv_weight, qkv_moment, qkv_square, qkv_average, out_weight, out_moment, out_square, out_average, up_weight, up_moment, up_square, up_average, down_weight, down_moment, down_square, down_average, norm_params, norm_moment, norm_square, norm_average):

    def rounded(weight):
        return weight.astype(jnp.bfloat16).astype(jnp.float32)
    weights = (rounded(qkv_weight[0]), rounded(qkv_weight[1]), rounded(qkv_weight[2]), rounded(out_weight), rounded(up_weight), rounded(down_weight), rounded(norm_params))

    def per_segment(carry, inputs):
        rows_in, row_grad, doc_row, reset_row, live_count = inputs
        allowed = allowed_mask(doc_row, reset_row, live_count)

        def run(rows_value, w_query, w_key, w_value, w_out, w_up, w_down, norms):
            return layer(rows_value, w_query, w_key, w_value, w_out, w_up, w_down, norms, allowed)
        result, pull = jax.vjp(run, rows_in.astype(jnp.float32), *weights)
        grads = pull(row_grad.astype(jnp.float32))
        carry = tuple((total + grad for total, grad in zip(carry, grads[1:])))
        return (carry, (result.astype(jnp.bfloat16), grads[0]))
    zeros = tuple((jnp.zeros(weight.shape, jnp.float32) for weight in weights))
    sums, (output, input_grad) = lax.scan(per_segment, zeros, (tokens, cotangent, doc_ids, reset_flags, mem_live))
    grad_qkv = jnp.stack([sums[0], sums[1], sums[2]])
    grad_list = (grad_qkv, sums[3], sums[4], sums[5], sums[6])
    total = jnp.float32(0.0)
    for grad in grad_list:
        total = total + jnp.sum(grad * grad)
    grad_norm = jnp.sqrt(total)
    threshold = math.sqrt(4 * D * D + 2 * D * FF + 4 * D)
    factor = jnp.minimum(1.0, threshold / (grad_norm + 1e-06))
    new_qkv = adam_step(qkv_weight, qkv_moment, qkv_square, qkv_average, grad_qkv * factor, 0.02, 0.01)
    new_out = adam_step(out_weight, out_moment, out_square, out_average, sums[3] * factor, 0.06, 0.01)
    new_up = adam_step(up_weight, up_moment, up_square, up_average, sums[4] * factor, 0.02, 0.01)
    new_down = adam_step(down_weight, down_moment, down_square, down_average, sums[5] * factor, 0.02, 0.01)
    new_norm = adam_step(norm_params, norm_moment, norm_square, norm_average, sums[6] * factor, 0.4, 0.0)
    return (output, input_grad, grad_norm, new_qkv[0], new_qkv[1], new_qkv[2], new_qkv[3], new_out[0], new_out[1], new_out[2], new_out[3], new_up[0], new_up[1], new_up[2], new_up[3], new_down[0], new_down[1], new_down[2], new_down[3], new_norm[0], new_norm[1], new_norm[2], new_norm[3])
```

```python
import math

import jax
import jax.numpy as jnp
from jax import lax
from jax.sharding import PartitionSpec as P

D = 1024
HEAD = 64
FF = 4096
MEM = 10
STEP = 10


NORM_EPS = 1e-12
BETA_ONE = 0.9
BETA_TWO = 0.98
ADAM_EPS = 1e-06
AVERAGE_KEEP = 0.75
MASKED = -1e30


def allowed_mask(doc_row, reset_row, live_count):
    rows_all = doc_row.shape[0] + 2 * MEM
    kinds = jnp.concatenate(
        [jnp.full((MEM,), -1, jnp.int32), doc_row, jnp.full((MEM,), -2, jnp.int32)]
    )
    place = jnp.arange(rows_all, dtype=jnp.int32)
    read_key = place < MEM
    live_key = place < live_count
    choose = kinds[:, None] == jnp.arange(reset_row.shape[0], dtype=jnp.int32)[None, :]
    reset_query = jnp.sum(jnp.where(choose, reset_row[None, :], 0), axis=1)
    memory_query = kinds < 0
    same_doc = kinds[:, None] == kinds[None, :]
    token_sees = same_doc | (read_key & live_key)[None, :] & (reset_query == 0)[:, None]
    memory_sees = jnp.broadcast_to((~read_key | live_key)[None, :], (rows_all, rows_all))
    return jnp.where(memory_query[:, None], memory_sees, token_sees)


def norm_forward(rows_in, gain, shift):
    center = rows_in - jnp.mean(rows_in, axis=-1, keepdims=True)
    inverse = lax.rsqrt(jnp.mean(center * center, axis=-1, keepdims=True) + NORM_EPS)
    normed = center * inverse
    return (normed * gain + shift, normed, inverse)


def norm_backward(grad, normed, inverse, gain):
    scaled = grad * gain
    back = inverse * (
        scaled
        - jnp.mean(scaled, axis=-1, keepdims=True)
        - normed * jnp.mean(scaled * normed, axis=-1, keepdims=True)
    )
    return (back, jnp.stack([jnp.sum(grad * normed, axis=0), jnp.sum(grad, axis=0)]))


def masked_scores(query, keys, allowed):
    scores = jnp.einsum("qhd,khd->hqk", query, keys, preferred_element_type=jnp.float32) * (
        1.0 / math.sqrt(HEAD)
    )
    return jnp.where(allowed[None], scores, MASKED)


def attend(inputs):
    query, keys, values, allowed = inputs
    scores = masked_scores(query, keys, allowed)
    row_top = jnp.max(scores, axis=-1, keepdims=True)
    expo = jnp.exp(scores - row_top)
    row_total = jnp.sum(expo, axis=-1, keepdims=True)
    probs = (expo / row_total).astype(jnp.bfloat16)
    context = jnp.einsum("hqk,khd->qhd", probs, values, preferred_element_type=jnp.float32)
    return (context.astype(jnp.bfloat16), row_top + jnp.log(row_total))


def attend_back(inputs):
    query, keys, values, allowed, log_total, context_grad = inputs
    probs = jnp.exp(masked_scores(query, keys, allowed) - log_total)
    value_grad = jnp.einsum(
        "hqk,qhd->khd", probs.astype(jnp.bfloat16), context_grad, preferred_element_type=jnp.float32
    )
    prob_grad = jnp.einsum("qhd,khd->hqk", context_grad, values, preferred_element_type=jnp.float32)
    score_grad = probs * (prob_grad - jnp.sum(probs * prob_grad, axis=-1, keepdims=True))
    score_grad = score_grad.astype(jnp.bfloat16)
    scale_now = 1.0 / math.sqrt(HEAD)
    query_grad = (
        jnp.einsum("hqk,khd->qhd", score_grad, keys, preferred_element_type=jnp.float32) * scale_now
    )
    key_grad = (
        jnp.einsum("hqk,qhd->khd", score_grad, query, preferred_element_type=jnp.float32)
        * scale_now
    )
    return (
        query_grad.astype(jnp.bfloat16),
        key_grad.astype(jnp.bfloat16),
        value_grad.astype(jnp.bfloat16),
    )


def adam_step(weight, moment, square, average, grad, rate, decay):
    moment = BETA_ONE * moment + (1.0 - BETA_ONE) * grad
    square = BETA_TWO * square + (1.0 - BETA_TWO) * grad * grad
    first_hat = moment / (1.0 - BETA_ONE**STEP)
    second_hat = square / (1.0 - BETA_TWO**STEP)
    weight = weight - rate * (first_hat / (jnp.sqrt(second_hat) + ADAM_EPS) + decay * weight)
    average = AVERAGE_KEEP * average + (1.0 - AVERAGE_KEEP) * weight
    return (weight, moment, square, average)


def row_scatter(terms):
    return lax.psum_scatter(terms, "narrow", scatter_dimension=0, tiled=True)


def row_gather(piece):
    return lax.all_gather(piece, "narrow", axis=0, tiled=True)


def narrow_norm(grads):
    return lax.psum(grads, "narrow")


def shared_rows(
    tokens,
    cotangent,
    doc_ids,
    reset_flags,
    mem_live,
    qkv_weight,
    qkv_moment,
    qkv_square,
    qkv_average,
    out_weight,
    out_moment,
    out_square,
    out_average,
    up_weight,
    up_moment,
    up_square,
    up_average,
    down_weight,
    down_moment,
    down_square,
    down_average,
    norm_params,
    norm_moment,
    norm_square,
    norm_average,
):
    narrow_count = lax.axis_size("narrow")
    seg_count, rows_all, width = tokens.shape
    w_qkv, w_out, w_up, w_down, norms_low = (
        lax.all_gather(qkv_weight.astype(jnp.bfloat16), "wide", axis=1, tiled=True),
        lax.all_gather(out_weight.astype(jnp.bfloat16), "wide", axis=1, tiled=True),
        lax.all_gather(up_weight.astype(jnp.bfloat16), "wide", axis=0, tiled=True),
        lax.all_gather(down_weight.astype(jnp.bfloat16), "wide", axis=1, tiled=True),
        lax.all_gather(norm_params.astype(jnp.bfloat16), "wide", axis=1, tiled=True),
    )
    norms = norms_low.astype(jnp.float32)
    local_cols = w_qkv.shape[2]
    local_heads = local_cols // HEAD
    total_rows = seg_count * rows_all
    flat_in = tokens.reshape(total_rows, width)
    flat_cot = cotangent.reshape(total_rows, width)
    allowed = jax.vmap(allowed_mask)(doc_ids, reset_flags, mem_live)
    projected = jnp.einsum(
        "md,kdc->kmc", flat_in, w_qkv, preferred_element_type=jnp.float32
    ).astype(jnp.bfloat16)
    split_heads = projected.reshape(3, seg_count, rows_all, local_heads, HEAD)
    query, keys, values = (split_heads[0], split_heads[1], split_heads[2])
    context, log_total = lax.map(attend, (query, keys, values, allowed))
    context_flat = context.reshape(total_rows, local_cols)
    attention_terms = jnp.dot(context_flat, w_out, preferred_element_type=jnp.float32)
    share = total_rows // narrow_count
    row_start = lax.axis_index("narrow") * share
    own_in = lax.dynamic_slice_in_dim(flat_in, row_start, share, 0)
    own_cot = lax.dynamic_slice_in_dim(flat_cot, row_start, share, 0)
    first_sum = own_in.astype(jnp.float32) + row_scatter(attention_terms)
    hidden, normed_one, inverse_one = norm_forward(first_sum, norms[0], norms[1])
    hidden_low = row_gather(hidden.astype(jnp.bfloat16))
    inner = jnp.dot(hidden_low, w_up, preferred_element_type=jnp.float32)
    active, gelu_pull = jax.vjp(lambda value_in: jax.nn.gelu(value_in, approximate=False), inner)
    active_low = active.astype(jnp.bfloat16)
    feed_terms = jnp.dot(active_low, w_down, preferred_element_type=jnp.float32)
    feed = row_scatter(feed_terms)
    second_sum = hidden + feed
    result, normed_two, inverse_two = norm_forward(second_sum, norms[2], norms[3])
    result_low = result.astype(jnp.bfloat16)
    second_grad, norm_two_grads = norm_backward(
        own_cot.astype(jnp.float32), normed_two, inverse_two, norms[2]
    )
    norm_two_grads = narrow_norm(norm_two_grads)
    output = row_gather(result_low)
    feed_grad = row_gather(second_grad.astype(jnp.bfloat16))
    output = output.reshape(seg_count, rows_all, width)
    down_grad = jnp.einsum("mf,md->fd", active_low, feed_grad, preferred_element_type=jnp.float32)
    active_grad = jnp.einsum("md,fd->mf", feed_grad, w_down, preferred_element_type=jnp.float32)
    inner_grad = gelu_pull(active_grad)[0].astype(jnp.bfloat16)
    up_grad = jnp.einsum("md,mf->df", hidden_low, inner_grad, preferred_element_type=jnp.float32)
    hidden_terms = jnp.einsum("mf,df->md", inner_grad, w_up, preferred_element_type=jnp.float32)
    hidden_grad = second_grad + row_scatter(hidden_terms)
    first_grad, norm_one_grads = norm_backward(hidden_grad, normed_one, inverse_one, norms[0])
    norm_one_grads = narrow_norm(norm_one_grads)
    branch_grad = row_gather(first_grad.astype(jnp.bfloat16))
    out_grad_weight = jnp.einsum(
        "mc,md->cd", context_flat, branch_grad, preferred_element_type=jnp.float32
    )
    context_grad = jnp.einsum(
        "md,cd->mc", branch_grad, w_out, preferred_element_type=jnp.float32
    ).astype(jnp.bfloat16)
    context_grad = context_grad.reshape(seg_count, rows_all, local_heads, HEAD)
    query_grad, key_grad, value_grad = lax.map(
        attend_back, (query, keys, values, allowed, log_total, context_grad)
    )
    stacked_grad = jnp.stack([query_grad, key_grad, value_grad]).reshape(3, total_rows, local_cols)
    qkv_grad = jnp.einsum("md,kmc->kdc", flat_in, stacked_grad, preferred_element_type=jnp.float32)
    input_terms = jnp.einsum("kmc,kdc->md", stacked_grad, w_qkv, preferred_element_type=jnp.float32)
    input_grad = lax.all_gather(first_grad + row_scatter(input_terms), "narrow", axis=0, tiled=True)
    input_grad = input_grad.reshape(seg_count, rows_all, width)
    norm_grads = jnp.concatenate([norm_one_grads, norm_two_grads], axis=0)
    qkv_sum, out_sum, up_sum, down_sum, norm_sum = (
        lax.psum_scatter(qkv_grad, "wide", scatter_dimension=1, tiled=True),
        lax.psum_scatter(out_grad_weight, "wide", scatter_dimension=1, tiled=True),
        lax.psum_scatter(up_grad, "wide", scatter_dimension=0, tiled=True),
        lax.psum_scatter(down_grad, "wide", scatter_dimension=1, tiled=True),
        lax.psum_scatter(norm_grads, "wide", scatter_dimension=1, tiled=True),
    )
    local_squares = (
        jnp.sum(qkv_sum * qkv_sum)
        + jnp.sum(out_sum * out_sum)
        + jnp.sum(up_sum * up_sum)
        + jnp.sum(down_sum * down_sum)
        + jnp.sum(norm_sum * norm_sum) / narrow_count
    )
    grad_norm = jnp.sqrt(lax.psum(local_squares, ("wide", "narrow")))
    threshold = math.sqrt(4 * D * D + 2 * D * FF + 4 * D)
    factor = jnp.minimum(1.0, threshold / (grad_norm + 1e-06))
    new_qkv = adam_step(
        qkv_weight, qkv_moment, qkv_square, qkv_average, qkv_sum * factor, 0.02, 0.01
    )
    new_out = adam_step(
        out_weight, out_moment, out_square, out_average, out_sum * factor, 0.06, 0.01
    )
    new_up = adam_step(up_weight, up_moment, up_square, up_average, up_sum * factor, 0.02, 0.01)
    new_down = adam_step(
        down_weight, down_moment, down_square, down_average, down_sum * factor, 0.02, 0.01
    )
    new_norm = adam_step(
        norm_params, norm_moment, norm_square, norm_average, norm_sum * factor, 0.4, 0.0
    )
    return (
        output,
        input_grad,
        grad_norm,
        new_qkv[0],
        new_qkv[1],
        new_qkv[2],
        new_qkv[3],
        new_out[0],
        new_out[1],
        new_out[2],
        new_out[3],
        new_up[0],
        new_up[1],
        new_up[2],
        new_up[3],
        new_down[0],
        new_down[1],
        new_down[2],
        new_down[3],
        new_norm[0],
        new_norm[1],
        new_norm[2],
        new_norm[3],
    )


SWAP = ((0, 1), (1, 0))
RING = ((0, 1), (1, 3), (3, 2), (2, 0))
RING_BACK = tuple((b, a) for a, b in RING)


def send(block, axes, pairs):
    return lax.ppermute(block, axes, list(pairs))


def ring_place():
    x, y = lax.axis_index("x"), lax.axis_index("y")
    return jnp.where(x == 0, y, 3 - y)


def place_xy(place):
    place = lax.rem(place + 4, 4)
    x = place // 2
    return x, jnp.where(x == 0, place, 3 - place)


def line_gather(block):
    count = lax.axis_size("z")
    ups, downs = [block], [block]
    for step in range(1, count):
        pairs = [(i, i + 1) for i in range(step - 1, count - 1)]
        ups.append(send(ups[-1], "z", pairs))
        downs.append(send(downs[-1], "z", [(count - 1 - a, count - 1 - b) for a, b in pairs]))
    row = jnp.stack(ups[:0:-1] + downs)
    return lax.dynamic_slice_in_dim(row, count - 1 - lax.axis_index("z"), count, 0)


def ring_gather(block):
    left = send(block, ("x", "y"), RING)
    right = send(block, ("x", "y"), RING_BACK)
    half = block.shape[0] // 2
    far_one = send(left[:half], ("x", "y"), RING)
    far_two = send(right[half:], ("x", "y"), RING_BACK)
    return block, left, right, far_one, far_two


def ring_scatter(take, half_of):
    place = ring_place()
    far = half_of(take(*place_xy(place + 2)))
    from_left = send(far[0].astype(jnp.bfloat16), ("x", "y"), RING)
    from_right = send(far[1].astype(jnp.bfloat16), ("x", "y"), RING_BACK)
    right = half_of(take(*place_xy(place + 1)))
    left = half_of(take(*place_xy(place - 1)))
    to_right = jnp.concatenate([right[0] + from_left.astype(jnp.float32), right[1]]).astype(jnp.bfloat16)
    to_left = jnp.concatenate([left[0], left[1] + from_right.astype(jnp.float32)]).astype(jnp.bfloat16)
    from_left = send(to_right, ("x", "y"), RING)
    from_right = send(to_left, ("x", "y"), RING_BACK)
    return take(*place_xy(place)) + from_left.astype(jnp.float32) + from_right.astype(jnp.float32)


def line_scatter(take):
    count, z = lax.axis_size("z"), lax.axis_index("z")
    up = down = None
    for step in range(1, count):
        pairs = [(i, i + 1) for i in range(step)]
        above = take(jnp.minimum(z + count - step, count - 1))
        below = take(jnp.maximum(z - count + step, 0))
        if up is not None:
            above, below = above + up.astype(jnp.float32), below + down.astype(jnp.float32)
        up = send(above.astype(jnp.bfloat16), "z", pairs)
        down = send(below.astype(jnp.bfloat16), "z", [(count - 1 - a, count - 1 - b) for a, b in pairs])
    return take(z) + up.astype(jnp.float32) + down.astype(jnp.float32)


def core_terms(grad, rows):
    z, x, y = (lax.axis_size(a) for a in "zxy")
    blocks = grad.reshape(z, x, 2, rows, y, grad.shape[1] // y)
    core = lax.axis_index("c")
    own = lax.dynamic_index_in_dim(blocks, core, 2, keepdims=False)
    other = lax.dynamic_index_in_dim(blocks, 1 - core, 2, keepdims=False)
    return own, send(other, "c", SWAP)


def scatter_square_first(grad, rows):
    own, other = core_terms(grad, rows)

    def take(x, y):
        def pick(a):
            part = lax.dynamic_index_in_dim(a, x, 1, keepdims=False)
            return lax.dynamic_index_in_dim(part, y, 2, keepdims=False).astype(jnp.float32)

        return pick(own) + pick(other)

    half = own.shape[0] // 2
    column = ring_scatter(take, lambda a: (a[:half], a[half:]))
    return line_scatter(lambda z: lax.dynamic_index_in_dim(column, z, 0, keepdims=False))


def scatter_line_first(grad, rows):
    own, other = core_terms(grad, rows)

    def take_z(z):
        def pick(a):
            return lax.dynamic_index_in_dim(a, z, 0, keepdims=False).astype(jnp.float32)

        return pick(own) + pick(other)

    square = line_scatter(take_z)

    def take(x, y):
        part = lax.dynamic_index_in_dim(square, x, 0, keepdims=False)
        return lax.dynamic_index_in_dim(part, y, 1, keepdims=False)

    return ring_scatter(take, lambda a: (a[: rows // 2], a[rows // 2 :]))


def put(full, piece, z, x, c, y):
    piece = piece[:, None, None, :, None, :]
    return lax.dynamic_update_slice(full, piece, (z, x, c, 0, y, 0))


def gather_square_last(block):
    column = line_gather(block)
    pieces = ring_gather(column)
    others = tuple(send(p, "c", SWAP) for p in pieces)
    place, core = ring_place(), lax.axis_index("c")
    count = column.shape[0]
    full = jnp.zeros((count, lax.axis_size("x"), 2, block.shape[0], lax.axis_size("y"), block.shape[1]), block.dtype)
    for core_at, group in ((core, pieces), (1 - core, others)):
        for piece, shift, z in zip(group, (0, -1, 1, 2, 2), (0, 0, 0, 0, count // 2)):
            x, y = place_xy(place + shift)
            full = put(full, piece, z, x, core_at, y)
    return full


def gather_line_last(block):
    rows = block.shape[0]
    own, left, right, far_one, far_two = ring_gather(block)
    place, core = ring_place(), lax.axis_index("c")
    square = jnp.zeros((lax.axis_size("x"), rows, lax.axis_size("y"), block.shape[1]), block.dtype)
    for piece, shift, row in ((own, 0, 0), (left, -1, 0), (right, 1, 0), (far_one, 2, 0), (far_two, 2, rows // 2)):
        x, y = place_xy(place + shift)
        square = lax.dynamic_update_slice(square, piece[None, :, None, :], (x, row, y, 0))
    column = line_gather(square)
    other = send(column, "c", SWAP)
    full = jnp.zeros((column.shape[0], column.shape[1], 2) + column.shape[2:], block.dtype)
    full = lax.dynamic_update_slice(full, column[:, :, None], (0, 0, core, 0, 0, 0))
    return lax.dynamic_update_slice(full, other[:, :, None], (0, 0, 1 - core, 0, 0, 0))


def whole_segment(
    tokens,
    cotangent,
    doc_ids,
    reset_flags,
    mem_live,
    qkv_weight,
    qkv_moment,
    qkv_square,
    qkv_average,
    out_weight,
    out_moment,
    out_square,
    out_average,
    up_weight,
    up_moment,
    up_square,
    up_average,
    down_weight,
    down_moment,
    down_square,
    down_average,
    norm_params,
    norm_moment,
    norm_square,
    norm_average,
):
    low = jnp.bfloat16
    y = lax.axis_index("y")
    rows = up_weight.shape[0]
    halves, width = lax.axis_size("y"), tokens.shape[2]
    part, inner_part = qkv_weight.shape[2], up_weight.shape[1]
    heads = width // HEAD
    flat_in = lax.dynamic_index_in_dim(tokens, y, 0, keepdims=False)
    flat_cot = lax.dynamic_index_in_dim(cotangent, y, 0, keepdims=False)
    rows_all = flat_in.shape[0]

    def mine(a):
        return lax.dynamic_index_in_dim(a, y, 0, keepdims=False)

    allowed = allowed_mask(mine(doc_ids), mine(reset_flags), mine(mem_live))[None]

    qkv_block = jnp.concatenate([qkv_weight[k] for k in range(3)], axis=1).astype(low)
    norm_block = jnp.pad(norm_params.astype(low), ((0, rows - 4), (0, 128 - rows)))
    second_block = jnp.concatenate([out_weight.T.astype(low), up_weight.astype(low), norm_block], axis=1)
    down_block = down_weight.T.astype(low)

    w_qkv = gather_square_last(qkv_block).reshape(width, 3 * width)
    second = gather_square_last(second_block)
    w_out = second[..., :part].reshape(width, width)
    w_up = second[..., part : part + inner_part].reshape(width, halves * inner_part)
    norms = second[:, :, :, :4, 0, part + inner_part : part + inner_part + rows].reshape(-1, 4, rows)
    norms = norms.transpose(1, 0, 2).reshape(4, width).astype(jnp.float32)
    w_down = gather_line_last(down_block).reshape(width, halves * inner_part)

    projected = jnp.dot(flat_in, w_qkv, preferred_element_type=jnp.float32).astype(low)
    split = projected.reshape(rows_all, halves, 3, part // HEAD, HEAD)
    query, keys, values = (split[:, :, k].reshape(rows_all, heads, HEAD) for k in range(3))
    context, log_total = attend((query, keys, values, allowed[0]))
    context_flat = context.reshape(rows_all, width)
    nt = (((1,), (1,)), ((), ()))
    tn = (((0,), (0,)), ((), ()))

    def dot(a, b, dims=(((1,), (0,)), ((), ()))):
        return lax.dot_general(a, b, dims, preferred_element_type=jnp.float32)

    first_sum = flat_in.astype(jnp.float32) + dot(context_flat, w_out, nt)
    hidden, normed_one, inverse_one = norm_forward(first_sum, norms[0], norms[1])
    hidden_low = hidden.astype(low)
    inner = dot(hidden_low, w_up)
    active, gelu_pull = jax.vjp(lambda value_in: jax.nn.gelu(value_in, approximate=False), inner)
    active_low = active.astype(low)
    second_sum = hidden + dot(active_low, w_down, nt)
    result, normed_two, inverse_two = norm_forward(second_sum, norms[2], norms[3])
    second_grad, norm_two_grads = norm_backward(flat_cot.astype(jnp.float32), normed_two, inverse_two, norms[2])
    feed_grad = second_grad.astype(low)
    down_sum = scatter_line_first(dot(feed_grad, active_low, tn).astype(low), rows)
    inner_grad = gelu_pull(dot(feed_grad, w_down))[0].astype(low)
    up_sum = scatter_square_first(dot(hidden_low, inner_grad, tn).astype(low), rows)
    hidden_grad = second_grad + dot(inner_grad, w_up, nt)
    first_grad, norm_one_grads = norm_backward(hidden_grad, normed_one, inverse_one, norms[0])
    branch_grad = first_grad.astype(low)
    out_grad = dot(branch_grad, context_flat, tn).astype(low)
    context_grad = dot(branch_grad, w_out).astype(low).reshape(rows_all, heads, HEAD)
    grads = attend_back((query, keys, values, allowed[0], log_total, context_grad))
    grads = jnp.stack([g.reshape(rows_all, halves, part) for g in grads], axis=2)
    stacked_grad = grads.reshape(rows_all, 3 * width)
    qkv_grad = dot(flat_in, stacked_grad, tn).astype(low)
    norm_grads = jnp.concatenate([norm_one_grads, norm_two_grads], axis=0).astype(low)
    norm_grads = norm_grads.reshape(4, width // rows, rows).transpose(1, 0, 2)
    norm_grads = jnp.pad(norm_grads, ((0, 0), (0, rows - 4), (0, 128 - rows))).reshape(width, 128)
    last = []
    for k in range(halves):
        last += [qkv_grad[:, 3 * part * k : 3 * part * (k + 1)], out_grad[:, part * k : part * (k + 1)], norm_grads]
    last_sum = scatter_square_first(jnp.concatenate(last, axis=1), rows)

    own_grad = (first_grad + dot(stacked_grad, w_qkv, nt)).astype(low)
    own_out = result.astype(low)

    def both(own):
        other = send(own, "y", SWAP)
        return jnp.where(y == 0, jnp.stack([own, other]), jnp.stack([other, own]))

    output = both(own_out)
    input_grad = both(own_grad).astype(jnp.float32)

    qkv_sum = last_sum[:, : 3 * part].reshape(rows, 3, part).transpose(1, 0, 2)
    out_sum = last_sum[:, 3 * part : 4 * part].T
    norm_sum = last_sum[:4, 4 * part : 4 * part + rows]
    down_sum = down_sum.T
    local_squares = (
        jnp.sum(qkv_sum * qkv_sum)
        + jnp.sum(out_sum * out_sum)
        + jnp.sum(up_sum * up_sum)
        + jnp.sum(down_sum * down_sum)
        + jnp.sum(norm_sum * norm_sum) / halves
    )
    grad_norm = jnp.sqrt(lax.psum(local_squares, ("z", "x", "c", "y")))
    threshold = math.sqrt(4 * D * D + 2 * D * FF + 4 * D)
    factor = jnp.minimum(1.0, threshold / (grad_norm + 1e-06))
    new_qkv = adam_step(qkv_weight, qkv_moment, qkv_square, qkv_average, qkv_sum * factor, 0.02, 0.01)
    new_out = adam_step(out_weight, out_moment, out_square, out_average, out_sum * factor, 0.06, 0.01)
    new_up = adam_step(up_weight, up_moment, up_square, up_average, up_sum * factor, 0.02, 0.01)
    new_down = adam_step(down_weight, down_moment, down_square, down_average, down_sum * factor, 0.02, 0.01)
    new_norm = adam_step(norm_params, norm_moment, norm_square, norm_average, norm_sum * factor, 0.4, 0.0)
    return (output, input_grad, grad_norm) + new_qkv + new_out + new_up + new_down + new_norm


def solution(mesh):
    wide, narrow = mesh.shape["wide"], mesh.shape["narrow"]

    def placed(w, n):
        state = [P(None, w, n)] * 4 + [P(n, w)] * 4 + [P(w, n)] * 4 + [P(n, w)] * 4 + [P(None, w)] * 4
        return (
            tuple([P(w, None, None)] * 2 + [P(w, None)] * 2 + [P(w)] + state),
            tuple([P(w, None, None)] * 2 + [P()] + state),
        )

    def run(*args):
        if narrow == 2 and wide % 8 == 0 and args[0].shape[0] == wide * narrow:
            body = whole_segment
            grid = jax.sharding.Mesh(mesh.devices.reshape(wide // 4, 2, 2, 2), ("z", "x", "c", "y"))
            ins, outs = placed(("z", "x", "c"), "y")
        else:
            body, grid = shared_rows, mesh
            ins, outs = placed("wide", "narrow")
        return jax.shard_map(body, mesh=grid, in_specs=ins, out_specs=outs, check_vma=False)(*args)

    return run
```

```python
import functools
import math

import jax
import jax.numpy as jnp
from jax import lax
from jax.experimental import pallas as pl
from jax.experimental.pallas import tpu as pltpu
from jax.sharding import PartitionSpec as P

D = 1024
HEAD = 64
FF = 4096
MEM = 10
STEP = 10


NORM_EPS = 1e-12
BETA_ONE = 0.9
BETA_TWO = 0.98
ADAM_EPS = 1e-06
AVERAGE_KEEP = 0.75
MASKED = -1e30


def allowed_mask(doc_row, reset_row, live_count):
    rows_all = doc_row.shape[0] + 2 * MEM
    kinds = jnp.concatenate(
        [jnp.full((MEM,), -1, jnp.int32), doc_row, jnp.full((MEM,), -2, jnp.int32)]
    )
    place = jnp.arange(rows_all, dtype=jnp.int32)
    read_key = place < MEM
    live_key = place < live_count
    choose = kinds[:, None] == jnp.arange(reset_row.shape[0], dtype=jnp.int32)[None, :]
    reset_query = jnp.sum(jnp.where(choose, reset_row[None, :], 0), axis=1)
    memory_query = kinds < 0
    same_doc = kinds[:, None] == kinds[None, :]
    token_sees = same_doc | (read_key & live_key)[None, :] & (reset_query == 0)[:, None]
    memory_sees = jnp.broadcast_to((~read_key | live_key)[None, :], (rows_all, rows_all))
    return jnp.where(memory_query[:, None], memory_sees, token_sees)


def norm_forward(rows_in, gain, shift):
    center = rows_in - jnp.mean(rows_in, axis=-1, keepdims=True)
    inverse = lax.rsqrt(jnp.mean(center * center, axis=-1, keepdims=True) + NORM_EPS)
    normed = center * inverse
    return (normed * gain + shift, normed, inverse)


def norm_backward(grad, normed, inverse, gain):
    scaled = grad * gain
    back = inverse * (
        scaled
        - jnp.mean(scaled, axis=-1, keepdims=True)
        - normed * jnp.mean(scaled * normed, axis=-1, keepdims=True)
    )
    return (back, jnp.stack([jnp.sum(grad * normed, axis=0), jnp.sum(grad, axis=0)]))


def masked_scores(query, keys, allowed):
    scores = jnp.einsum("qhd,khd->hqk", query, keys, preferred_element_type=jnp.float32) * (
        1.0 / math.sqrt(HEAD)
    )
    return jnp.where(allowed[None], scores, MASKED)


def attend(inputs):
    query, keys, values, allowed = inputs
    scores = masked_scores(query, keys, allowed)
    row_top = jnp.max(scores, axis=-1, keepdims=True)
    expo = jnp.exp(scores - row_top)
    row_total = jnp.sum(expo, axis=-1, keepdims=True)
    probs = (expo / row_total).astype(jnp.bfloat16)
    context = jnp.einsum("hqk,khd->qhd", probs, values, preferred_element_type=jnp.float32)
    return (context.astype(jnp.bfloat16), row_top + jnp.log(row_total))


def attend_back(inputs):
    query, keys, values, allowed, log_total, context_grad = inputs
    probs = jnp.exp(masked_scores(query, keys, allowed) - log_total)
    value_grad = jnp.einsum(
        "hqk,qhd->khd", probs.astype(jnp.bfloat16), context_grad, preferred_element_type=jnp.float32
    )
    prob_grad = jnp.einsum("qhd,khd->hqk", context_grad, values, preferred_element_type=jnp.float32)
    score_grad = probs * (prob_grad - jnp.sum(probs * prob_grad, axis=-1, keepdims=True))
    score_grad = score_grad.astype(jnp.bfloat16)
    scale_now = 1.0 / math.sqrt(HEAD)
    query_grad = (
        jnp.einsum("hqk,khd->qhd", score_grad, keys, preferred_element_type=jnp.float32) * scale_now
    )
    key_grad = (
        jnp.einsum("hqk,qhd->khd", score_grad, query, preferred_element_type=jnp.float32)
        * scale_now
    )
    return (
        query_grad.astype(jnp.bfloat16),
        key_grad.astype(jnp.bfloat16),
        value_grad.astype(jnp.bfloat16),
    )


def adam_step(weight, moment, square, average, grad, rate, decay):
    moment = BETA_ONE * moment + (1.0 - BETA_ONE) * grad
    square = BETA_TWO * square + (1.0 - BETA_TWO) * grad * grad
    first_hat = moment / (1.0 - BETA_ONE**STEP)
    second_hat = square / (1.0 - BETA_TWO**STEP)
    weight = weight - rate * (first_hat / (jnp.sqrt(second_hat) + ADAM_EPS) + decay * weight)
    average = AVERAGE_KEEP * average + (1.0 - AVERAGE_KEEP) * weight
    return (weight, moment, square, average)


def row_scatter(terms):
    return lax.psum_scatter(terms, "narrow", scatter_dimension=0, tiled=True)


def row_gather(piece):
    return lax.all_gather(piece, "narrow", axis=0, tiled=True)


def narrow_norm(grads):
    return lax.psum(grads, "narrow")


def shared_rows(
    tokens,
    cotangent,
    doc_ids,
    reset_flags,
    mem_live,
    qkv_weight,
    qkv_moment,
    qkv_square,
    qkv_average,
    out_weight,
    out_moment,
    out_square,
    out_average,
    up_weight,
    up_moment,
    up_square,
    up_average,
    down_weight,
    down_moment,
    down_square,
    down_average,
    norm_params,
    norm_moment,
    norm_square,
    norm_average,
):
    narrow_count = lax.axis_size("narrow")
    seg_count, rows_all, width = tokens.shape
    w_qkv, w_out, w_up, w_down, norms_low = (
        lax.all_gather(qkv_weight.astype(jnp.bfloat16), "wide", axis=1, tiled=True),
        lax.all_gather(out_weight.astype(jnp.bfloat16), "wide", axis=1, tiled=True),
        lax.all_gather(up_weight.astype(jnp.bfloat16), "wide", axis=0, tiled=True),
        lax.all_gather(down_weight.astype(jnp.bfloat16), "wide", axis=1, tiled=True),
        lax.all_gather(norm_params.astype(jnp.bfloat16), "wide", axis=1, tiled=True),
    )
    norms = norms_low.astype(jnp.float32)
    local_cols = w_qkv.shape[2]
    local_heads = local_cols // HEAD
    total_rows = seg_count * rows_all
    flat_in = tokens.reshape(total_rows, width)
    flat_cot = cotangent.reshape(total_rows, width)
    allowed = jax.vmap(allowed_mask)(doc_ids, reset_flags, mem_live)
    projected = jnp.einsum(
        "md,kdc->kmc", flat_in, w_qkv, preferred_element_type=jnp.float32
    ).astype(jnp.bfloat16)
    split_heads = projected.reshape(3, seg_count, rows_all, local_heads, HEAD)
    query, keys, values = (split_heads[0], split_heads[1], split_heads[2])
    context, log_total = lax.map(attend, (query, keys, values, allowed))
    context_flat = context.reshape(total_rows, local_cols)
    attention_terms = jnp.dot(context_flat, w_out, preferred_element_type=jnp.float32)
    share = total_rows // narrow_count
    row_start = lax.axis_index("narrow") * share
    own_in = lax.dynamic_slice_in_dim(flat_in, row_start, share, 0)
    own_cot = lax.dynamic_slice_in_dim(flat_cot, row_start, share, 0)
    first_sum = own_in.astype(jnp.float32) + row_scatter(attention_terms)
    hidden, normed_one, inverse_one = norm_forward(first_sum, norms[0], norms[1])
    hidden_low = row_gather(hidden.astype(jnp.bfloat16))
    inner = jnp.dot(hidden_low, w_up, preferred_element_type=jnp.float32)
    active, gelu_pull = jax.vjp(lambda value_in: jax.nn.gelu(value_in, approximate=False), inner)
    active_low = active.astype(jnp.bfloat16)
    feed_terms = jnp.dot(active_low, w_down, preferred_element_type=jnp.float32)
    feed = row_scatter(feed_terms)
    second_sum = hidden + feed
    result, normed_two, inverse_two = norm_forward(second_sum, norms[2], norms[3])
    result_low = result.astype(jnp.bfloat16)
    second_grad, norm_two_grads = norm_backward(
        own_cot.astype(jnp.float32), normed_two, inverse_two, norms[2]
    )
    norm_two_grads = narrow_norm(norm_two_grads)
    output = row_gather(result_low)
    feed_grad = row_gather(second_grad.astype(jnp.bfloat16))
    output = output.reshape(seg_count, rows_all, width)
    down_grad = jnp.einsum("mf,md->fd", active_low, feed_grad, preferred_element_type=jnp.float32)
    active_grad = jnp.einsum("md,fd->mf", feed_grad, w_down, preferred_element_type=jnp.float32)
    inner_grad = gelu_pull(active_grad)[0].astype(jnp.bfloat16)
    up_grad = jnp.einsum("md,mf->df", hidden_low, inner_grad, preferred_element_type=jnp.float32)
    hidden_terms = jnp.einsum("mf,df->md", inner_grad, w_up, preferred_element_type=jnp.float32)
    hidden_grad = second_grad + row_scatter(hidden_terms)
    first_grad, norm_one_grads = norm_backward(hidden_grad, normed_one, inverse_one, norms[0])
    norm_one_grads = narrow_norm(norm_one_grads)
    branch_grad = row_gather(first_grad.astype(jnp.bfloat16))
    out_grad_weight = jnp.einsum(
        "mc,md->cd", context_flat, branch_grad, preferred_element_type=jnp.float32
    )
    context_grad = jnp.einsum(
        "md,cd->mc", branch_grad, w_out, preferred_element_type=jnp.float32
    ).astype(jnp.bfloat16)
    context_grad = context_grad.reshape(seg_count, rows_all, local_heads, HEAD)
    query_grad, key_grad, value_grad = lax.map(
        attend_back, (query, keys, values, allowed, log_total, context_grad)
    )
    stacked_grad = jnp.stack([query_grad, key_grad, value_grad]).reshape(3, total_rows, local_cols)
    qkv_grad = jnp.einsum("md,kmc->kdc", flat_in, stacked_grad, preferred_element_type=jnp.float32)
    input_terms = jnp.einsum("kmc,kdc->md", stacked_grad, w_qkv, preferred_element_type=jnp.float32)
    input_grad = lax.all_gather(first_grad + row_scatter(input_terms), "narrow", axis=0, tiled=True)
    input_grad = input_grad.reshape(seg_count, rows_all, width)
    norm_grads = jnp.concatenate([norm_one_grads, norm_two_grads], axis=0)
    qkv_sum, out_sum, up_sum, down_sum, norm_sum = (
        lax.psum_scatter(qkv_grad, "wide", scatter_dimension=1, tiled=True),
        lax.psum_scatter(out_grad_weight, "wide", scatter_dimension=1, tiled=True),
        lax.psum_scatter(up_grad, "wide", scatter_dimension=0, tiled=True),
        lax.psum_scatter(down_grad, "wide", scatter_dimension=1, tiled=True),
        lax.psum_scatter(norm_grads, "wide", scatter_dimension=1, tiled=True),
    )
    local_squares = (
        jnp.sum(qkv_sum * qkv_sum)
        + jnp.sum(out_sum * out_sum)
        + jnp.sum(up_sum * up_sum)
        + jnp.sum(down_sum * down_sum)
        + jnp.sum(norm_sum * norm_sum) / narrow_count
    )
    grad_norm = jnp.sqrt(lax.psum(local_squares, ("wide", "narrow")))
    threshold = math.sqrt(4 * D * D + 2 * D * FF + 4 * D)
    factor = jnp.minimum(1.0, threshold / (grad_norm + 1e-06))
    new_qkv = adam_step(
        qkv_weight, qkv_moment, qkv_square, qkv_average, qkv_sum * factor, 0.02, 0.01
    )
    new_out = adam_step(
        out_weight, out_moment, out_square, out_average, out_sum * factor, 0.06, 0.01
    )
    new_up = adam_step(up_weight, up_moment, up_square, up_average, up_sum * factor, 0.02, 0.01)
    new_down = adam_step(
        down_weight, down_moment, down_square, down_average, down_sum * factor, 0.02, 0.01
    )
    new_norm = adam_step(
        norm_params, norm_moment, norm_square, norm_average, norm_sum * factor, 0.4, 0.0
    )
    return (
        output,
        input_grad,
        grad_norm,
        new_qkv[0],
        new_qkv[1],
        new_qkv[2],
        new_qkv[3],
        new_out[0],
        new_out[1],
        new_out[2],
        new_out[3],
        new_up[0],
        new_up[1],
        new_up[2],
        new_up[3],
        new_down[0],
        new_down[1],
        new_down[2],
        new_down[3],
        new_norm[0],
        new_norm[1],
        new_norm[2],
        new_norm[3],
    )


SWAP = ((0, 1), (1, 0))
RING = ((0, 1), (1, 3), (3, 2), (2, 0))
RING_BACK = tuple((b, a) for a, b in RING)


def send(block, axes, pairs):
    return lax.ppermute(block, axes, list(pairs))


def ring_place():
    x, y = lax.axis_index("x"), lax.axis_index("y")
    return jnp.where(x == 0, y, 3 - y)


def place_xy(place):
    place = lax.rem(place + 4, 4)
    x = place // 2
    return x, jnp.where(x == 0, place, 3 - place)


def ring_gather(block):
    left = send(block, ("x", "y"), RING)
    right = send(block, ("x", "y"), RING_BACK)
    half = block.shape[0] // 2
    far_one = send(left[:half], ("x", "y"), RING)
    far_two = send(right[half:], ("x", "y"), RING_BACK)
    return block, left, right, far_one, far_two


def ring_scatter(take, half_of):
    place = ring_place()
    far = half_of(take(*place_xy(place + 2)))
    from_left = send(far[0].astype(jnp.bfloat16), ("x", "y"), RING)
    from_right = send(far[1].astype(jnp.bfloat16), ("x", "y"), RING_BACK)
    right = half_of(take(*place_xy(place + 1)))
    left = half_of(take(*place_xy(place - 1)))
    to_right = jnp.concatenate([right[0] + from_left.astype(jnp.float32), right[1]]).astype(jnp.bfloat16)
    to_left = jnp.concatenate([left[0], left[1] + from_right.astype(jnp.float32)]).astype(jnp.bfloat16)
    from_left = send(to_right, ("x", "y"), RING)
    from_right = send(to_left, ("x", "y"), RING_BACK)
    return take(*place_xy(place)) + from_left.astype(jnp.float32) + from_right.astype(jnp.float32)


def line_scatter(take):
    count, z = lax.axis_size("z"), lax.axis_index("z")
    up = down = None
    for step in range(1, count):
        pairs = [(i, i + 1) for i in range(step)]
        above = take(jnp.minimum(z + count - step, count - 1))
        below = take(jnp.maximum(z - count + step, 0))
        if up is not None:
            above, below = above + up.astype(jnp.float32), below + down.astype(jnp.float32)
        up = send(above.astype(jnp.bfloat16), "z", pairs)
        down = send(below.astype(jnp.bfloat16), "z", [(count - 1 - a, count - 1 - b) for a, b in pairs])
    return take(z) + up.astype(jnp.float32) + down.astype(jnp.float32)


STEP_WIDTH = 512
RING_SHIFTS = (0, -1, 1, 2, 2)
NT = (((1,), (1,)), ((), ()))
TN = (((0,), (0,)), ((), ()))
NN = (((1,), (0,)), ((), ()))
F32, LOW = jnp.float32, jnp.bfloat16
ANYWHERE = pl.BlockSpec(memory_space=pl.ANY)


def params(mib):
    return pltpu.CompilerParams(vmem_limit_bytes=mib << 20)


def shaped(shape, dtype):
    return jax.ShapeDtypeStruct(shape, dtype)


def full(shape):
    return pl.BlockSpec(shape, lambda *_: (0,) * len(shape))


def mm(a, b, dims=NN):
    return lax.dot_general(a, b, dims, preferred_element_type=F32)


def join_column_kernel(count, *refs):
    own, ups, downs = refs[0], refs[1:count], refs[count : 2 * count - 1]
    out, sem = refs[-2:]
    z = lax.axis_index("z")
    moves = [(None, own, z)]
    for k in range(1, count):
        moves += [(z >= k, ups[k - 1], z - k), (z + k < count, downs[k - 1], z + k)]
    for end in (False, True):
        for i, (here, ref, at) in enumerate(moves):
            copy = pltpu.make_async_copy(ref, out.at[at], sem.at[i])
            act = copy.wait if end else copy.start
            act() if here is None else pl.when(here)(act)


def line_pieces(block):
    count = lax.axis_size("z")
    ups, downs = [block], [block]
    for step in range(1, count):
        pairs = [(i, i + 1) for i in range(step - 1, count - 1)]
        ups.append(send(ups[-1], "z", pairs))
        downs.append(send(downs[-1], "z", [(count - 1 - a, count - 1 - b) for a, b in pairs]))
    return [block] + ups[1:] + downs[1:]


def join_column(pieces):
    count = (len(pieces) + 1) // 2
    shape = (count,) + pieces[0].shape
    return pl.pallas_call(
        functools.partial(join_column_kernel, count),
        in_specs=[ANYWHERE] * len(pieces),
        out_specs=pl.BlockSpec(memory_space=pltpu.VMEM),
        out_shape=shaped(shape, pieces[0].dtype),
        scratch_shapes=[pltpu.SemaphoreType.DMA((len(pieces),))],
        name="join_column",
    )(*pieces)


def join_square_kernel(own, left, right, far_one, far_two, out, sem):
    place = ring_place()
    half = far_one.shape[0]
    copies = []
    for i, (ref, shift) in enumerate(zip((own, left, right, far_one, far_two), RING_SHIFTS)):
        x, y = place_xy(place + shift)
        to = out.at[x, y] if i < 3 else out.at[x, y, pl.ds(half * (i - 3), half)]
        copies.append(pltpu.make_async_copy(ref, to, sem.at[i]))
    for copy in copies:
        copy.start()
    for copy in copies:
        copy.wait()


def join_square(pieces):
    return pl.pallas_call(
        join_square_kernel,
        in_specs=[ANYWHERE] * 5,
        out_specs=pl.BlockSpec(memory_space=pltpu.VMEM),
        out_shape=shaped((2, 2) + pieces[0].shape, pieces[0].dtype),
        scratch_shapes=[pltpu.SemaphoreType.DMA((5,))],
        name="join_square",
    )(*pieces)


def both_cores(pieces):
    return list(pieces) + [send(p, "c", SWAP) for p in pieces]


def weights_square_last(block):
    return both_cores(ring_gather(join_column(line_pieces(block))))


def weights_line_last(block):
    return both_cores(line_pieces(join_square(ring_gather(block))))


def load_square_last(pieces, w, sem, column, width, per_side):
    place, core = ring_place(), lax.axis_index("c")
    rows = w.shape[4]
    for k in range(per_side):
        for group, core_at in ((pieces[:5], core), (pieces[5:], 1 - core)):
            for i, (ref, shift) in enumerate(zip(group, RING_SHIFTS)):
                x, y = place_xy(place + shift)
                chunk = y * per_side + k
                first = ref.shape[0] if i == 4 else 0
                pltpu.make_async_copy(
                    ref.at[:, pl.ds(0, rows), pl.ds(column + k * width, width)],
                    w.at[chunk, pl.ds(first, ref.shape[0]), x, core_at],
                    sem.at[chunk],
                ).start()


def load_line_last(pieces, w, sem, width, per_side):
    z, core = lax.axis_index("z"), lax.axis_index("c")
    group_size = len(pieces) // 2
    count = (group_size + 1) // 2
    for k in range(per_side):
        for group, core_at in ((pieces[:group_size], core), (pieces[group_size:], 1 - core)):
            places = [(None, z)] + [(z >= s, z - s) for s in range(1, count)]
            places += [(z + s < count, z + s) for s in range(1, count)]
            for ref, (here, at) in zip(group, places):

                def begin(ref=ref, at=at, core_at=core_at):
                    for y in range(2):
                        chunk = y * per_side + k
                        pltpu.make_async_copy(
                            ref.at[:, y, :, pl.ds(k * width, width)], w.at[chunk, at, :, core_at], sem.at[chunk]
                        ).start()

                begin() if here is None else pl.when(here)(begin)


def ready(w, sem, chunk):
    pltpu.make_async_copy(w.at[chunk], w.at[chunk], sem.at[chunk]).wait()


def matrix(w, chunk):
    block = w[chunk]
    return block.reshape(-1, block.shape[-1])


def chunk_buffer(shapes, chunks, width):
    z, rows = shapes
    return [pltpu.VMEM((chunks, z, 2, 2, rows, width), LOW), pltpu.SemaphoreType.DMA((chunks,))]


def alternate(per_side):
    return lambda j: (j % 2) * per_side + j // 2


def project_kernel(per_side, x_ref, *refs):
    pieces, (o_ref, w, sem) = refs[:10], refs[10:]
    j = pl.program_id(0)

    @pl.when(j == 0)
    def _():
        load_square_last(pieces, w, sem, 0, o_ref.shape[2], per_side)

    chunk = alternate(per_side)(j)
    ready(w, sem, chunk)
    o_ref[0] = mm(x_ref[...], matrix(w, chunk)).astype(LOW)


def project(x, pieces, rows):
    count, width = pieces[0].shape[0], STEP_WIDTH
    per_side = pieces[0].shape[2] // width
    at = alternate(per_side)
    return pl.pallas_call(
        functools.partial(project_kernel, per_side),
        grid=(2 * per_side,),
        in_specs=[full(x.shape)] + [ANYWHERE] * 10,
        out_specs=pl.BlockSpec((1, x.shape[0], width), lambda j: (at(j), 0, 0)),
        out_shape=shaped((2 * per_side, x.shape[0], width), LOW),
        scratch_shapes=chunk_buffer((count, rows), 2 * per_side, width),
        compiler_params=params(32),
        name="project",
    )(x, *pieces)


def head_parts(a, lane, scale=None):
    a = a if scale is None else a * jnp.asarray(scale, a.dtype)
    none = jnp.zeros_like(a)
    return jnp.where(lane < HEAD, a, none), jnp.where(lane < HEAD, none, a)


def attend_kernel(q_ref, k_ref, v_ref, bias_ref, o_ref, l_ref):
    k, v = k_ref[0], v_ref[0]
    lane = lax.broadcasted_iota(jnp.int32, k.shape, 1)
    outs, logs = [], []
    for q in head_parts(q_ref[0], lane, HEAD**-0.5):
        scores = mm(q, k, NT) + bias_ref[...].astype(F32)
        top = jnp.max(scores, axis=-1, keepdims=True)
        expo = jnp.exp(scores - top)
        total = jnp.sum(expo, axis=-1, keepdims=True)
        outs.append(mm((expo * (1.0 / total)).astype(LOW), v))
        logs.append(top + jnp.log(total))
    o_ref[...] = jnp.where(lane < HEAD, outs[0], outs[1]).astype(LOW)
    l_ref[...] = jnp.where(lane < HEAD, logs[0], logs[1])


def pair_specs(total, per_side):
    def spec(k):
        return pl.BlockSpec((1, total, 128), lambda g: ((g // per_side) * 3 + k, 0, g % per_side))

    return [spec(k) for k in range(3)]


def attention(qkv, bias):
    total, width = qkv.shape[1], qkv.shape[2] * 2
    pairs = width // 128
    return pl.pallas_call(
        attend_kernel,
        grid=(pairs,),
        in_specs=pair_specs(total, pairs // 2) + [full(bias.shape)],
        out_specs=[pl.BlockSpec((total, 128), lambda g: (0, g))] * 2,
        out_shape=[shaped((total, width), LOW), shaped((total, width), F32)],
        compiler_params=params(48),
        name="attention",
    )(qkv, qkv, qkv, bias)


ROWS_AT_ONCE = 32


def by_rows(total, body, carry=0):
    def step(i, held):
        return body(pl.ds(pl.multiple_of(i * ROWS_AT_ONCE, ROWS_AT_ONCE), ROWS_AT_ONCE), held)

    return lax.fori_loop(0, total // ROWS_AT_ONCE, step, carry)


def normalize(v):
    center = v - jnp.mean(v, axis=-1, keepdims=True)
    inverse = lax.rsqrt(jnp.mean(center * center, axis=-1, keepdims=True) + NORM_EPS)
    return center * inverse, inverse


def unnormalize(scaled, normed, inverse):
    return inverse * (
        scaled
        - jnp.mean(scaled, axis=-1, keepdims=True)
        - normed * jnp.mean(scaled * normed, axis=-1, keepdims=True)
    )


def fold(a):
    return jnp.sum(a.reshape(-1, 8, a.shape[-1]), axis=0)


def gelu_parts(u):
    expo = jnp.exp(-0.5 * (u * u))
    t = 1.0 / (1.0 + 0.3275911 * 0.7071067811865476 * jnp.abs(u))
    poly = ((((1.061405429 * t - 1.453152027) * t + 1.421413741) * t - 0.284496736) * t + 0.254829592) * t
    tail = 0.5 * poly * expo
    phi = jnp.where(u < 0, tail, 1.0 - tail)
    return u * phi, phi + u * expo * 0.3989422804014327


def up_kernel(per_side, x_ref, ctx_ref, *refs):
    pieces = refs[:10]
    h_ref, n_ref, i_ref, norms_ref, g_ref, d_ref, wu, us, wo, os, nw, ns, acc = refs[10:]
    j = pl.program_id(0)
    width = g_ref.shape[2]

    @pl.when(j == 0)
    def _():
        first = 2 * per_side // 2 * width
        load_square_last(pieces, nw, ns, first + width, 128, 1)
        load_square_last(pieces, wo, os, first, width, 1)
        load_square_last(pieces, wu, us, 0, width, per_side)
        ready(nw, ns, 0)
        ready(nw, ns, 1)
        cells = nw[0].reshape(-1, nw.shape[4], 128).astype(F32)
        side = x_ref.shape[1] // cells.shape[0]
        norms_ref[...] = jnp.concatenate([cells[i, :8, :side] for i in range(cells.shape[0])], axis=1)
        ready(wo, os, 0)
        acc[...] = mm(ctx_ref[:, :width], matrix(wo, 0), NT)
        ready(wo, os, 1)
        acc[...] += mm(ctx_ref[:, width:], matrix(wo, 1), NT)
        gain, shift = norms_ref[0:1], norms_ref[1:2]

        def rows(r, held):
            normed, inverse = normalize(x_ref[r].astype(F32) + acc[r])
            n_ref[r] = normed
            i_ref[r] = jnp.broadcast_to(inverse, (ROWS_AT_ONCE, 128))
            h_ref[r] = (normed * gain + shift).astype(LOW)
            return held

        by_rows(x_ref.shape[0], rows)

    chunk = alternate(per_side)(j)
    ready(wu, us, chunk)
    active, slope = gelu_parts(mm(h_ref[...], matrix(wu, chunk)))
    g_ref[0] = active.astype(LOW)
    d_ref[0] = slope.astype(LOW)


def up(x, context, pieces, rows, inner_part):
    count, width = pieces[0].shape[0], STEP_WIDTH
    per_side = inner_part // width
    at = alternate(per_side)
    total, model = x.shape
    chunks = pl.BlockSpec((1, total, width), lambda j: (at(j), 0, 0))
    return pl.pallas_call(
        functools.partial(up_kernel, per_side),
        grid=(2 * per_side,),
        in_specs=[full(x.shape)] * 2 + [ANYWHERE] * 10,
        out_specs=[full(x.shape), full(x.shape), full((total, 128)), full((8, model)), chunks, chunks],
        out_shape=[
            shaped(x.shape, LOW),
            shaped(x.shape, F32),
            shaped((total, 128), F32),
            shaped((8, model), F32),
            shaped((2 * per_side, total, width), LOW),
            shaped((2 * per_side, total, width), LOW),
        ],
        scratch_shapes=chunk_buffer((count, rows), 2 * per_side, width)
        + chunk_buffer((count, rows), 2, width)
        + chunk_buffer((count, 16), 2, 128)
        + [pltpu.VMEM(x.shape, F32)],
        compiler_params=params(56),
        name="up",
    )(x, context, *pieces)


def down_kernel(per_side, pieces_count, g_ref, n_ref, norms_ref, cot_ref, *refs):
    pieces = refs[:pieces_count]
    o_ref, d_ref, f_ref, ng_ref, w, sem, acc = refs[pieces_count:]
    j = pl.program_id(0)

    @pl.when(j == 0)
    def _():
        load_line_last(pieces, w, sem, g_ref.shape[2], per_side)
        acc[...] = jnp.zeros_like(acc)

    chunk = alternate(per_side)(j)
    ready(w, sem, chunk)
    acc[...] += mm(g_ref[0], matrix(w, chunk), NT)

    @pl.when(j == 2 * per_side - 1)
    def _():
        gain_one, shift_one, gain, shift = (norms_ref[i : i + 1] for i in range(4))

        def rows(r, held):
            normed, inverse = normalize(n_ref[r] * gain_one + shift_one + acc[r])
            o_ref[r] = (normed * gain + shift).astype(LOW)
            dy = cot_ref[r].astype(F32)
            back = unnormalize(dy * gain, normed, inverse)
            d_ref[r] = back
            f_ref[r] = back.astype(LOW)
            return held[0] + fold(dy * normed), held[1] + fold(dy)

        none = jnp.zeros((8, acc.shape[1]), F32)
        gains, shifts = by_rows(acc.shape[0], rows, (none, none))
        ng_ref[...] = jnp.concatenate(
            [jnp.sum(gains, axis=0, keepdims=True), jnp.sum(shifts, axis=0, keepdims=True), none[:6]], axis=0
        )


def down(active, normed, norms, cot, pieces, rows):
    width = STEP_WIDTH
    chunks, total = active.shape[0], active.shape[1]
    at = alternate(chunks // 2)
    shape = normed.shape
    count = (len(pieces) // 2 + 1) // 2
    return pl.pallas_call(
        functools.partial(down_kernel, chunks // 2, len(pieces)),
        grid=(chunks,),
        in_specs=[pl.BlockSpec((1, total, width), lambda j: (at(j), 0, 0)), full(shape), full(norms.shape), full(shape)]
        + [ANYWHERE] * len(pieces),
        out_specs=[full(shape), full(shape), full(shape), full(norms.shape)],
        out_shape=[shaped(shape, LOW), shaped(shape, F32), shaped(shape, LOW), shaped(norms.shape, F32)],
        scratch_shapes=chunk_buffer((count, rows), chunks, width) + [pltpu.VMEM(shape, F32)],
        compiler_params=params(56),
        name="down",
    )(active, normed, norms, cot, *pieces)


def share_out(value, own_ref, other_ref):
    core = lax.axis_index("c")
    z, x, _, rows, width = own_ref.shape
    value = value.reshape(z, x, 2, rows, width)
    for parity in range(2):
        part = value[:, :, parity]

        @pl.when(core == parity)
        def _(part=part):
            own_ref[:, :, 0] = part

        @pl.when(core != parity)
        def _(part=part):
            other_ref[:, :, 0] = part


def share_specs(count, rows, per_side, columns):
    spec = pl.BlockSpec((count, 2, 1, rows, STEP_WIDTH), lambda j: (0, 0, j // per_side, 0, j % per_side))
    return [spec] * 2, [shaped((count, 2, 2, rows, columns), LOW)] * 2


def weight_grad_kernel(a_ref, b_ref, own_ref, other_ref):
    share_out(mm(a_ref[...], b_ref[0], TN).astype(LOW), own_ref, other_ref)


def weight_grad(a, b, spec, chunks, count, rows, name):
    out_specs, out_shape = share_specs(count, rows, chunks // 2, chunks // 2 * STEP_WIDTH)
    return pl.pallas_call(
        weight_grad_kernel,
        grid=(chunks,),
        in_specs=[full(a.shape), spec],
        out_specs=out_specs,
        out_shape=out_shape,
        compiler_params=params(32),
        name=name,
    )(a, b)


def inner_kernel(per_side, down_count, f_ref, d_ref, h_ref, r_ref, n_ref, i_ref, norms_ref, *refs):
    downs, ups = refs[:down_count], refs[down_count : down_count + 10]
    own_ref, other_ref, g_ref, a_ref, ng_ref, wd, ds, wu, us, acc = refs[down_count + 10 :]
    j = pl.program_id(0)
    width = d_ref.shape[2]

    @pl.when(j == 0)
    def _():
        load_line_last(downs, wd, ds, width, per_side)
        load_square_last(ups, wu, us, 0, width, per_side)
        acc[...] = r_ref[...]

    ready(wd, ds, j)
    grad = (mm(f_ref[...], matrix(wd, j)) * d_ref[0].astype(F32)).astype(LOW)
    share_out(mm(h_ref[...], grad, TN).astype(LOW), own_ref, other_ref)
    ready(wu, us, j)
    acc[...] += mm(grad, matrix(wu, j), NT)

    @pl.when(j == 2 * per_side - 1)
    def _():
        gain = norms_ref[0:1]

        def rows(r, held):
            dy, normed = acc[r], n_ref[r]
            back = unnormalize(dy * gain, normed, i_ref[r][:, :1])
            g_ref[r] = back
            a_ref[r] = back.astype(LOW)
            return held[0] + fold(dy * normed), held[1] + fold(dy)

        none = jnp.zeros((8, acc.shape[1]), F32)
        gains, shifts = by_rows(acc.shape[0], rows, (none, none))
        ng_ref[...] = jnp.concatenate(
            [jnp.sum(gains, axis=0, keepdims=True), jnp.sum(shifts, axis=0, keepdims=True), none[:6]], axis=0
        )


def inner_back(feed_grad, slope, hidden, second_grad, normed, inverse, norms, downs, ups, rows, columns):
    chunks, total, width = slope.shape
    shape = normed.shape
    count = ups[0].shape[0]
    out_specs, out_shape = share_specs(count, rows, chunks // 2, columns)
    once = pl.Buffered(1)

    def held(a):
        return pl.BlockSpec(a.shape, lambda j: (0,) * a.ndim, pipeline_mode=once)

    return pl.pallas_call(
        functools.partial(inner_kernel, chunks // 2, len(downs)),
        grid=(chunks,),
        in_specs=[held(feed_grad), pl.BlockSpec((1, total, width), lambda j: (j, 0, 0))]
        + [held(a) for a in (hidden, second_grad, normed, inverse, norms)]
        + [ANYWHERE] * (len(downs) + 10),
        out_specs=out_specs + [full(shape), full(shape), full(norms.shape)],
        out_shape=out_shape + [shaped(shape, F32), shaped(shape, LOW), shaped(norms.shape, F32)],
        scratch_shapes=chunk_buffer((count, rows), chunks, width) * 2 + [pltpu.VMEM(shape, F32)],
        compiler_params=params(58),
        name="inner_back",
    )(feed_grad, slope, hidden, second_grad, normed, inverse, norms, *downs, *ups)


def out_kernel(column, a_ref, ctx_ref, one_ref, two_ref, own_in, other_in, *refs):
    pieces = refs[:10]
    own_ref, other_ref, o_ref, w, sem, tiles, out_sem = refs[10:]
    _, _, z, x, rows, _ = tiles.shape
    width = w.shape[5]
    core = lax.axis_index("c")
    load_square_last(pieces, w, sem, column, width, 1)
    norm_grads = jnp.concatenate([one_ref[0:2], two_ref[0:2], one_ref[2:6]], axis=0)
    for y in range(2):
        grad = mm(a_ref[...], ctx_ref[:, y * width : (y + 1) * width], TN).astype(LOW).reshape(z, x, 2, rows, width)
        for parity in range(2):
            slot = (parity + core) % 2
            tiles[slot, y, :, :, :, :width] = grad[:, :, parity]
            for at in range(z * x):
                cell = norm_grads[:, (at * 2 + parity) * rows : (at * 2 + parity + 1) * rows]
                cell = jnp.concatenate([cell, jnp.zeros((8, 128 - rows), F32)], axis=1)
                cell = jnp.concatenate([cell, jnp.zeros((rows - 8, 128), F32)], axis=0)
                tiles[slot, y, at // x, at % x, :, width:] = cell.astype(LOW)
    copies = []
    for slot, ref in enumerate((own_ref, other_ref)):
        for y in range(2):
            copies.append(
                pltpu.make_async_copy(
                    tiles.at[slot, y], ref.at[:, :, y, :, pl.ds(column, width + 128)], out_sem.at[slot, y]
                )
            )
    for copy in copies:
        copy.start()
    for y in range(2):
        ready(w, sem, y)
        o_ref[:, y * width : (y + 1) * width] = mm(a_ref[...], matrix(w, y)).astype(LOW)
    for copy in copies:
        copy.wait()


def out_back(branch_grad, context, one, two, own, other, pieces, rows, column):
    count, width = pieces[0].shape[0], STEP_WIDTH
    inside = pl.BlockSpec(memory_space=pltpu.VMEM)
    return pl.pallas_call(
        functools.partial(out_kernel, column),
        in_specs=[inside] * 4 + [ANYWHERE] * 12,
        out_specs=[ANYWHERE, ANYWHERE, inside],
        out_shape=[shaped(own.shape, LOW), shaped(other.shape, LOW), shaped(context.shape, LOW)],
        scratch_shapes=chunk_buffer((count, rows), 2, width)
        + [pltpu.VMEM((2, 2, count, 2, rows, width + 128), LOW), pltpu.SemaphoreType.DMA((2, 2))],
        input_output_aliases={4: 0, 5: 1},
        compiler_params=params(40),
        name="out_back",
    )(branch_grad, context, one, two, own, other, *pieces)


def attend_back_kernel(q_ref, k_ref, v_ref, bias_ref, l_ref, g_ref, o_ref):
    k, v, grad = k_ref[0], v_ref[0], g_ref[...]
    lane = lax.broadcasted_iota(jnp.int32, k.shape, 1)
    scale = HEAD**-0.5
    queries = q_ref[0]
    outs = []
    for h, (q, own_grad) in enumerate(zip(head_parts(queries, lane, scale), head_parts(grad, lane))):
        log_total = l_ref[:, h * HEAD : h * HEAD + 1]
        probs = jnp.exp(mm(q, k, NT) + bias_ref[...].astype(F32) - log_total)
        prob_grad = mm(own_grad, v, NT)
        score_grad = probs * (prob_grad - jnp.sum(probs * prob_grad, axis=-1, keepdims=True))
        score_grad = score_grad.astype(LOW)
        outs.append(
            (mm(score_grad, k) * scale, mm(score_grad, queries, TN) * scale, mm(probs.astype(LOW), grad, TN))
        )
    for i in range(3):
        o_ref[i] = jnp.where(lane < HEAD, outs[0][i], outs[1][i]).astype(LOW)


def attention_back(qkv, bias, logs, grad):
    total, width = grad.shape
    pairs = width // 128
    column = pl.BlockSpec((total, 128), lambda g: (0, g))
    return pl.pallas_call(
        attend_back_kernel,
        grid=(pairs,),
        in_specs=pair_specs(total, pairs // 2) + [full(bias.shape), column, column],
        out_specs=pl.BlockSpec((3, total, 128), lambda g: (0, 0, g)),
        out_shape=shaped((3, total, width), LOW),
        compiler_params=params(48),
        name="attention_back",
    )(qkv, qkv, qkv, bias, logs, grad)


def input_kernel(per_side, g_ref, r_ref, *refs):
    pieces, (o_ref, w, sem, acc) = refs[:10], refs[10:]
    j = pl.program_id(0)

    @pl.when(j == 0)
    def _():
        load_square_last(pieces, w, sem, 0, g_ref.shape[2], per_side)
        acc[...] = r_ref[...]

    chunk = alternate(per_side)(j)
    ready(w, sem, chunk)
    acc[...] += mm(g_ref[0], matrix(w, chunk), NT)

    @pl.when(j == 2 * per_side - 1)
    def _():
        o_ref[...] = acc[...].astype(LOW)


def input_back(grads, first_grad, pieces, rows):
    count, width = pieces[0].shape[0], STEP_WIDTH
    per_side = grads.shape[0]
    shape = first_grad.shape
    return pl.pallas_call(
        functools.partial(input_kernel, per_side),
        grid=(2 * per_side,),
        in_specs=[pl.BlockSpec((1, shape[0], width), lambda j: (j // 2, 0, j % 2)), full(shape)] + [ANYWHERE] * 10,
        out_specs=full(shape),
        out_shape=shaped(shape, LOW),
        scratch_shapes=chunk_buffer((count, rows), 2 * per_side, width) + [pltpu.VMEM(shape, F32)],
        compiler_params=params(40),
        name="input_back",
    )(grads, first_grad, *pieces)


def at(a, index, axis):
    return lax.dynamic_index_in_dim(a, index, axis, keepdims=False)


def sum_square_first(own, other):
    def take(x, y):
        return at(at(own, x, 1), y, 1).astype(F32) + at(at(other, x, 1), y, 1).astype(F32)

    half = own.shape[0] // 2
    column = ring_scatter(take, lambda a: (a[:half], a[half:]))
    return line_scatter(lambda z: at(column, z, 0))


def sum_line_first(own, other):
    square = line_scatter(lambda z: at(own, z, 0).astype(F32) + at(other, z, 0).astype(F32))
    half = own.shape[3] // 2
    return ring_scatter(lambda x, y: at(at(square, x, 0), y, 0), lambda a: (a[:half], a[half:]))


def sum_over_all(value):
    value = value + send(value, "c", SWAP)
    square = [send(value, ("x", "y"), tuple((i, i ^ k) for i in range(4))) for k in (1, 2, 3)]
    value = (value + square[0]) + (square[1] + square[2])
    count, k = lax.axis_size("z"), 1
    while k < count:
        value = value + send(value, "z", tuple((i, i ^ k) for i in range(count)))
        k *= 2
    return value


def pad_rows(a, total):
    return jnp.pad(a, ((0, total - a.shape[0]), (0, 0)))


def mask_bias(doc_row, reset_row, live, total):
    kinds = jnp.concatenate([jnp.full((MEM,), -1, jnp.int32), doc_row, jnp.full((MEM,), -2, jnp.int32)])
    real = kinds.shape[0]
    kinds = jnp.pad(kinds, (0, total - real), constant_values=-3)
    place = jnp.arange(total, dtype=jnp.int32)
    choose = kinds[:, None] == jnp.arange(reset_row.shape[0], dtype=jnp.int32)[None, :]
    reset_query = jnp.sum(jnp.where(choose, reset_row[None, :], 0), axis=1)
    same = kinds[:, None] == kinds[None, :]
    live_key = place < jnp.minimum(live, MEM)
    token_sees = same | (live_key[None, :] & (reset_query == 0)[:, None])
    memory_sees = ((place >= MEM) | live_key)[None, :]
    sees = jnp.where((kinds < 0)[:, None], memory_sees, token_sees) & (place < real)[None, :]
    return jnp.where(sees, 0.0, MASKED).astype(LOW)


def whole_segment(
    tokens,
    cotangent,
    doc_ids,
    reset_flags,
    mem_live,
    qkv_weight,
    qkv_moment,
    qkv_square,
    qkv_average,
    out_weight,
    out_moment,
    out_square,
    out_average,
    up_weight,
    up_moment,
    up_square,
    up_average,
    down_weight,
    down_moment,
    down_square,
    down_average,
    norm_params,
    norm_moment,
    norm_square,
    norm_average,
):
    y = lax.axis_index("y")
    rows, inner_part = up_weight.shape
    count = lax.axis_size("z")
    width = tokens.shape[2]
    part = qkv_weight.shape[2]
    real = tokens.shape[1]
    total = -(-real // ROWS_AT_ONCE) * ROWS_AT_ONCE

    def mine(a):
        return lax.dynamic_index_in_dim(a, y, 0, keepdims=False)

    qkv_block = jnp.concatenate([qkv_weight[k] for k in range(3)], axis=1).astype(LOW)
    norm_block = jnp.pad(norm_params.astype(LOW), ((0, rows - 4), (0, 128 - rows)))
    second_block = jnp.concatenate([up_weight.astype(LOW), out_weight.T.astype(LOW), norm_block], axis=1)
    down_block = down_weight.T.astype(LOW)

    x = pad_rows(mine(tokens), total)
    cot = pad_rows(mine(cotangent), total)
    bias = mask_bias(mine(doc_ids), mine(reset_flags), mine(mem_live), total)

    w_qkv = weights_square_last(qkv_block)
    w_second = weights_square_last(second_block)
    w_down = weights_line_last(down_block)

    qkv = project(x, w_qkv, rows)
    context, logs = attention(qkv, bias)
    hidden, normed, inverse, norms, active, slope = up(x, context, w_second, rows, inner_part)
    result, second_grad, feed_grad, norm_two = down(active, normed, norms, cot, w_down, rows)

    chunks = active.shape[0]
    own, other = weight_grad(
        feed_grad,
        active,
        pl.BlockSpec((1, total, STEP_WIDTH), lambda j: (j, 0, 0)),
        chunks,
        count,
        rows,
        "down_grad",
    )
    down_sum = sum_line_first(own, send(other, "c", SWAP))
    columns = inner_part + part + 128
    own, other, first_grad, branch_grad, norm_one = inner_back(
        feed_grad, slope, hidden, second_grad, normed, inverse, norms, w_down, w_second, rows, columns
    )
    own, other, context_grad = out_back(
        branch_grad, context, norm_one, norm_two, own, other, w_second, rows, inner_part
    )
    second_sum = sum_square_first(own, send(other, "c", SWAP))
    grads = attention_back(qkv, bias, logs, context_grad)
    own, other = weight_grad(
        x,
        grads,
        pl.BlockSpec((1, total, STEP_WIDTH), lambda j: (j % 3, 0, j // 3)),
        6,
        count,
        rows,
        "qkv_grad",
    )
    qkv_sum = sum_square_first(own, send(other, "c", SWAP))
    own_grad = input_back(grads, first_grad, w_qkv, rows)

    def both(own):
        own = own[:real]
        other = send(own, "y", SWAP)
        return jnp.where(y == 0, jnp.stack([own, other]), jnp.stack([other, own]))

    output = both(result)
    input_grad = both(own_grad).astype(F32)

    qkv_sum = qkv_sum.reshape(rows, 3, part).transpose(1, 0, 2)
    up_sum = second_sum[:, :inner_part]
    out_sum = second_sum[:, inner_part : inner_part + part].T
    norm_sum = second_sum[:4, inner_part + part : inner_part + part + rows]
    down_sum = down_sum.T
    local_squares = (
        jnp.sum(qkv_sum * qkv_sum)
        + jnp.sum(out_sum * out_sum)
        + jnp.sum(up_sum * up_sum)
        + jnp.sum(down_sum * down_sum)
        + jnp.sum(norm_sum * norm_sum) / lax.axis_size("y")
    )
    grad_norm = jnp.sqrt(sum_over_all(jnp.full((8, 128), local_squares))[0, 0])
    threshold = math.sqrt(4 * D * D + 2 * D * FF + 4 * D)
    factor = jnp.minimum(1.0, threshold / (grad_norm + 1e-06))
    new_qkv = adam_step(qkv_weight, qkv_moment, qkv_square, qkv_average, qkv_sum * factor, 0.02, 0.01)
    new_out = adam_step(out_weight, out_moment, out_square, out_average, out_sum * factor, 0.06, 0.01)
    new_up = adam_step(up_weight, up_moment, up_square, up_average, up_sum * factor, 0.02, 0.01)
    new_down = adam_step(down_weight, down_moment, down_square, down_average, down_sum * factor, 0.02, 0.01)
    new_norm = adam_step(norm_params, norm_moment, norm_square, norm_average, norm_sum * factor, 0.4, 0.0)
    return (output, input_grad, grad_norm) + new_qkv + new_out + new_up + new_down + new_norm


def solution(mesh):
    wide, narrow = mesh.shape["wide"], mesh.shape["narrow"]

    def placed(w, n):
        state = [P(None, w, n)] * 4 + [P(n, w)] * 4 + [P(w, n)] * 4 + [P(n, w)] * 4 + [P(None, w)] * 4
        return (
            tuple([P(w, None, None)] * 2 + [P(w, None)] * 2 + [P(w)] + state),
            tuple([P(w, None, None)] * 2 + [P()] + state),
        )

    def run(*args):
        if narrow == 2 and wide % 8 == 0 and args[0].shape[0] == wide * narrow:
            body = whole_segment
            grid = jax.sharding.Mesh(mesh.devices.reshape(wide // 4, 2, 2, 2), ("z", "x", "c", "y"))
            ins, outs = placed(("z", "x", "c"), "y")
        else:
            body, grid = shared_rows, mesh
            ins, outs = placed("wide", "narrow")
        return jax.shard_map(body, mesh=grid, in_specs=ins, out_specs=outs, check_vma=False)(*args)

    return run
```

```python
import functools
import math

import jax
import jax.numpy as jnp
from jax import lax
from jax.experimental import pallas as pl
from jax.experimental.pallas import tpu as pltpu
from jax.sharding import PartitionSpec as P

D = 1024
HEAD = 64
FF = 4096
MEM = 10
STEP = 10


NORM_EPS = 1e-12
BETA_ONE = 0.9
BETA_TWO = 0.98
ADAM_EPS = 1e-06
AVERAGE_KEEP = 0.75
MASKED = -1e30


def allowed_mask(doc_row, reset_row, live_count):
    rows_all = doc_row.shape[0] + 2 * MEM
    kinds = jnp.concatenate(
        [jnp.full((MEM,), -1, jnp.int32), doc_row, jnp.full((MEM,), -2, jnp.int32)]
    )
    place = jnp.arange(rows_all, dtype=jnp.int32)
    read_key = place < MEM
    live_key = place < live_count
    choose = kinds[:, None] == jnp.arange(reset_row.shape[0], dtype=jnp.int32)[None, :]
    reset_query = jnp.sum(jnp.where(choose, reset_row[None, :], 0), axis=1)
    memory_query = kinds < 0
    same_doc = kinds[:, None] == kinds[None, :]
    token_sees = same_doc | (read_key & live_key)[None, :] & (reset_query == 0)[:, None]
    memory_sees = jnp.broadcast_to((~read_key | live_key)[None, :], (rows_all, rows_all))
    return jnp.where(memory_query[:, None], memory_sees, token_sees)


def norm_forward(rows_in, gain, shift):
    center = rows_in - jnp.mean(rows_in, axis=-1, keepdims=True)
    inverse = lax.rsqrt(jnp.mean(center * center, axis=-1, keepdims=True) + NORM_EPS)
    normed = center * inverse
    return (normed * gain + shift, normed, inverse)


def norm_backward(grad, normed, inverse, gain):
    scaled = grad * gain
    back = inverse * (
        scaled
        - jnp.mean(scaled, axis=-1, keepdims=True)
        - normed * jnp.mean(scaled * normed, axis=-1, keepdims=True)
    )
    return (back, jnp.stack([jnp.sum(grad * normed, axis=0), jnp.sum(grad, axis=0)]))


def masked_scores(query, keys, allowed):
    scores = jnp.einsum("qhd,khd->hqk", query, keys, preferred_element_type=jnp.float32) * (
        1.0 / math.sqrt(HEAD)
    )
    return jnp.where(allowed[None], scores, MASKED)


def attend(inputs):
    query, keys, values, allowed = inputs
    scores = masked_scores(query, keys, allowed)
    row_top = jnp.max(scores, axis=-1, keepdims=True)
    expo = jnp.exp(scores - row_top)
    row_total = jnp.sum(expo, axis=-1, keepdims=True)
    probs = (expo / row_total).astype(jnp.bfloat16)
    context = jnp.einsum("hqk,khd->qhd", probs, values, preferred_element_type=jnp.float32)
    return (context.astype(jnp.bfloat16), row_top + jnp.log(row_total))


def attend_back(inputs):
    query, keys, values, allowed, log_total, context_grad = inputs
    probs = jnp.exp(masked_scores(query, keys, allowed) - log_total)
    value_grad = jnp.einsum(
        "hqk,qhd->khd", probs.astype(jnp.bfloat16), context_grad, preferred_element_type=jnp.float32
    )
    prob_grad = jnp.einsum("qhd,khd->hqk", context_grad, values, preferred_element_type=jnp.float32)
    score_grad = probs * (prob_grad - jnp.sum(probs * prob_grad, axis=-1, keepdims=True))
    score_grad = score_grad.astype(jnp.bfloat16)
    scale_now = 1.0 / math.sqrt(HEAD)
    query_grad = (
        jnp.einsum("hqk,khd->qhd", score_grad, keys, preferred_element_type=jnp.float32) * scale_now
    )
    key_grad = (
        jnp.einsum("hqk,qhd->khd", score_grad, query, preferred_element_type=jnp.float32)
        * scale_now
    )
    return (
        query_grad.astype(jnp.bfloat16),
        key_grad.astype(jnp.bfloat16),
        value_grad.astype(jnp.bfloat16),
    )


def adam_step(weight, moment, square, average, grad, rate, decay):
    moment = BETA_ONE * moment + (1.0 - BETA_ONE) * grad
    square = BETA_TWO * square + (1.0 - BETA_TWO) * grad * grad
    first_hat = moment / (1.0 - BETA_ONE**STEP)
    second_hat = square / (1.0 - BETA_TWO**STEP)
    weight = weight - rate * (first_hat / (jnp.sqrt(second_hat) + ADAM_EPS) + decay * weight)
    average = AVERAGE_KEEP * average + (1.0 - AVERAGE_KEEP) * weight
    return (weight, moment, square, average)


def row_scatter(terms):
    return lax.psum_scatter(terms, "narrow", scatter_dimension=0, tiled=True)


def row_gather(piece):
    return lax.all_gather(piece, "narrow", axis=0, tiled=True)


def narrow_norm(grads):
    return lax.psum(grads, "narrow")


def shared_rows(
    tokens,
    cotangent,
    doc_ids,
    reset_flags,
    mem_live,
    qkv_weight,
    qkv_moment,
    qkv_square,
    qkv_average,
    out_weight,
    out_moment,
    out_square,
    out_average,
    up_weight,
    up_moment,
    up_square,
    up_average,
    down_weight,
    down_moment,
    down_square,
    down_average,
    norm_params,
    norm_moment,
    norm_square,
    norm_average,
):
    narrow_count = lax.axis_size("narrow")
    seg_count, rows_all, width = tokens.shape
    w_qkv, w_out, w_up, w_down, norms_low = (
        lax.all_gather(qkv_weight.astype(jnp.bfloat16), "wide", axis=1, tiled=True),
        lax.all_gather(out_weight.astype(jnp.bfloat16), "wide", axis=1, tiled=True),
        lax.all_gather(up_weight.astype(jnp.bfloat16), "wide", axis=0, tiled=True),
        lax.all_gather(down_weight.astype(jnp.bfloat16), "wide", axis=1, tiled=True),
        lax.all_gather(norm_params.astype(jnp.bfloat16), "wide", axis=1, tiled=True),
    )
    norms = norms_low.astype(jnp.float32)
    local_cols = w_qkv.shape[2]
    local_heads = local_cols // HEAD
    total_rows = seg_count * rows_all
    flat_in = tokens.reshape(total_rows, width)
    flat_cot = cotangent.reshape(total_rows, width)
    allowed = jax.vmap(allowed_mask)(doc_ids, reset_flags, mem_live)
    projected = jnp.einsum(
        "md,kdc->kmc", flat_in, w_qkv, preferred_element_type=jnp.float32
    ).astype(jnp.bfloat16)
    split_heads = projected.reshape(3, seg_count, rows_all, local_heads, HEAD)
    query, keys, values = (split_heads[0], split_heads[1], split_heads[2])
    context, log_total = lax.map(attend, (query, keys, values, allowed))
    context_flat = context.reshape(total_rows, local_cols)
    attention_terms = jnp.dot(context_flat, w_out, preferred_element_type=jnp.float32)
    share = total_rows // narrow_count
    row_start = lax.axis_index("narrow") * share
    own_in = lax.dynamic_slice_in_dim(flat_in, row_start, share, 0)
    own_cot = lax.dynamic_slice_in_dim(flat_cot, row_start, share, 0)
    first_sum = own_in.astype(jnp.float32) + row_scatter(attention_terms)
    hidden, normed_one, inverse_one = norm_forward(first_sum, norms[0], norms[1])
    hidden_low = row_gather(hidden.astype(jnp.bfloat16))
    inner = jnp.dot(hidden_low, w_up, preferred_element_type=jnp.float32)
    active, gelu_pull = jax.vjp(lambda value_in: jax.nn.gelu(value_in, approximate=False), inner)
    active_low = active.astype(jnp.bfloat16)
    feed_terms = jnp.dot(active_low, w_down, preferred_element_type=jnp.float32)
    feed = row_scatter(feed_terms)
    second_sum = hidden + feed
    result, normed_two, inverse_two = norm_forward(second_sum, norms[2], norms[3])
    result_low = result.astype(jnp.bfloat16)
    second_grad, norm_two_grads = norm_backward(
        own_cot.astype(jnp.float32), normed_two, inverse_two, norms[2]
    )
    norm_two_grads = narrow_norm(norm_two_grads)
    output = row_gather(result_low)
    feed_grad = row_gather(second_grad.astype(jnp.bfloat16))
    output = output.reshape(seg_count, rows_all, width)
    down_grad = jnp.einsum("mf,md->fd", active_low, feed_grad, preferred_element_type=jnp.float32)
    active_grad = jnp.einsum("md,fd->mf", feed_grad, w_down, preferred_element_type=jnp.float32)
    inner_grad = gelu_pull(active_grad)[0].astype(jnp.bfloat16)
    up_grad = jnp.einsum("md,mf->df", hidden_low, inner_grad, preferred_element_type=jnp.float32)
    hidden_terms = jnp.einsum("mf,df->md", inner_grad, w_up, preferred_element_type=jnp.float32)
    hidden_grad = second_grad + row_scatter(hidden_terms)
    first_grad, norm_one_grads = norm_backward(hidden_grad, normed_one, inverse_one, norms[0])
    norm_one_grads = narrow_norm(norm_one_grads)
    branch_grad = row_gather(first_grad.astype(jnp.bfloat16))
    out_grad_weight = jnp.einsum(
        "mc,md->cd", context_flat, branch_grad, preferred_element_type=jnp.float32
    )
    context_grad = jnp.einsum(
        "md,cd->mc", branch_grad, w_out, preferred_element_type=jnp.float32
    ).astype(jnp.bfloat16)
    context_grad = context_grad.reshape(seg_count, rows_all, local_heads, HEAD)
    query_grad, key_grad, value_grad = lax.map(
        attend_back, (query, keys, values, allowed, log_total, context_grad)
    )
    stacked_grad = jnp.stack([query_grad, key_grad, value_grad]).reshape(3, total_rows, local_cols)
    qkv_grad = jnp.einsum("md,kmc->kdc", flat_in, stacked_grad, preferred_element_type=jnp.float32)
    input_terms = jnp.einsum("kmc,kdc->md", stacked_grad, w_qkv, preferred_element_type=jnp.float32)
    input_grad = lax.all_gather(first_grad + row_scatter(input_terms), "narrow", axis=0, tiled=True)
    input_grad = input_grad.reshape(seg_count, rows_all, width)
    norm_grads = jnp.concatenate([norm_one_grads, norm_two_grads], axis=0)
    qkv_sum, out_sum, up_sum, down_sum, norm_sum = (
        lax.psum_scatter(qkv_grad, "wide", scatter_dimension=1, tiled=True),
        lax.psum_scatter(out_grad_weight, "wide", scatter_dimension=1, tiled=True),
        lax.psum_scatter(up_grad, "wide", scatter_dimension=0, tiled=True),
        lax.psum_scatter(down_grad, "wide", scatter_dimension=1, tiled=True),
        lax.psum_scatter(norm_grads, "wide", scatter_dimension=1, tiled=True),
    )
    local_squares = (
        jnp.sum(qkv_sum * qkv_sum)
        + jnp.sum(out_sum * out_sum)
        + jnp.sum(up_sum * up_sum)
        + jnp.sum(down_sum * down_sum)
        + jnp.sum(norm_sum * norm_sum) / narrow_count
    )
    grad_norm = jnp.sqrt(lax.psum(local_squares, ("wide", "narrow")))
    threshold = math.sqrt(4 * D * D + 2 * D * FF + 4 * D)
    factor = jnp.minimum(1.0, threshold / (grad_norm + 1e-06))
    new_qkv = adam_step(
        qkv_weight, qkv_moment, qkv_square, qkv_average, qkv_sum * factor, 0.02, 0.01
    )
    new_out = adam_step(
        out_weight, out_moment, out_square, out_average, out_sum * factor, 0.06, 0.01
    )
    new_up = adam_step(up_weight, up_moment, up_square, up_average, up_sum * factor, 0.02, 0.01)
    new_down = adam_step(
        down_weight, down_moment, down_square, down_average, down_sum * factor, 0.02, 0.01
    )
    new_norm = adam_step(
        norm_params, norm_moment, norm_square, norm_average, norm_sum * factor, 0.4, 0.0
    )
    return (
        output,
        input_grad,
        grad_norm,
        new_qkv[0],
        new_qkv[1],
        new_qkv[2],
        new_qkv[3],
        new_out[0],
        new_out[1],
        new_out[2],
        new_out[3],
        new_up[0],
        new_up[1],
        new_up[2],
        new_up[3],
        new_down[0],
        new_down[1],
        new_down[2],
        new_down[3],
        new_norm[0],
        new_norm[1],
        new_norm[2],
        new_norm[3],
    )


SWAP = ((0, 1), (1, 0))
RING = ((0, 1), (1, 3), (3, 2), (2, 0))
RING_BACK = tuple((b, a) for a, b in RING)


def send(block, axes, pairs):
    return lax.ppermute(block, axes, list(pairs))


def ring_place():
    x, y = lax.axis_index("x"), lax.axis_index("y")
    return jnp.where(x == 0, y, 3 - y)


def place_xy(place):
    place = lax.rem(place + 4, 4)
    x = place // 2
    return x, jnp.where(x == 0, place, 3 - place)


def ring_near(block):
    return send(block, ("x", "y"), RING), send(block, ("x", "y"), RING_BACK)


def ring_far(left, right):
    half = left.shape[0] // 2
    return send(left[:half], ("x", "y"), RING), send(right[half:], ("x", "y"), RING_BACK)


def after(value, *others):
    return lax.optimization_barrier((value,) + others)[0]


STEP_WIDTH = 512
RING_SHIFTS = (0, -1, 1, 2, 2)
NT = (((1,), (1,)), ((), ()))
TN = (((0,), (0,)), ((), ()))
NN = (((1,), (0,)), ((), ()))
F32, LOW = jnp.float32, jnp.bfloat16
ANYWHERE = pl.BlockSpec(memory_space=pl.ANY)


def params(mib):
    return pltpu.CompilerParams(vmem_limit_bytes=mib << 20)


def cost(flops, moved):
    return pl.CostEstimate(flops=int(flops), bytes_accessed=int(moved), transcendentals=0)


def shaped(shape, dtype):
    return jax.ShapeDtypeStruct(shape, dtype)


def full(shape):
    return pl.BlockSpec(shape, lambda *_: (0,) * len(shape))


def mm(a, b, dims=NN):
    return lax.dot_general(a, b, dims, preferred_element_type=F32)


def join_column_kernel(count, *refs):
    out, sem = refs[-2:]
    z = lax.axis_index("z")
    copies = [pltpu.make_async_copy(ref, out.at[z ^ k], sem.at[k]) for k, ref in enumerate(refs[:count])]
    for copy in copies:
        copy.start()
    for copy in copies:
        copy.wait()


def partners(k):
    return tuple((i, i ^ k) for i in range(lax.axis_size("z")))


def line_pieces(block):
    return [block] + [send(block, "z", partners(k)) for k in range(1, lax.axis_size("z"))]


def join_column(pieces):
    count = len(pieces)
    shape = (count,) + pieces[0].shape
    return pl.pallas_call(
        functools.partial(join_column_kernel, count),
        in_specs=[ANYWHERE] * count,
        out_specs=pl.BlockSpec(memory_space=pltpu.VMEM),
        out_shape=shaped(shape, pieces[0].dtype),
        scratch_shapes=[pltpu.SemaphoreType.DMA((count,))],
        name="join_column",
    )(*pieces)


def both_cores(pieces):
    return list(pieces) + [send(p, "c", SWAP) for p in pieces]


def load_weights(pieces, w, sem, column, width, per_side):
    place, core = ring_place(), lax.axis_index("c")
    rows = w.shape[4]
    for k in range(per_side):
        for group, core_at in ((pieces[:5], core), (pieces[5:], 1 - core)):
            for i, (ref, shift) in enumerate(zip(group, RING_SHIFTS)):
                x, y = place_xy(place + shift)
                chunk = y * per_side + k
                first = ref.shape[0] if i == 4 else 0
                pltpu.make_async_copy(
                    ref.at[:, pl.ds(0, rows), pl.ds(column + k * width, width)],
                    w.at[chunk, pl.ds(first, ref.shape[0]), x, core_at],
                    sem.at[chunk],
                ).start()


def ready(w, sem, chunk):
    pltpu.make_async_copy(w.at[chunk], w.at[chunk], sem.at[chunk]).wait()


def matrix(w, chunk):
    block = w[chunk]
    return block.reshape(-1, block.shape[-1])


def chunk_buffer(shapes, chunks, width):
    z, rows = shapes
    return [pltpu.VMEM((chunks, z, 2, 2, rows, width), LOW), pltpu.SemaphoreType.DMA((chunks,))]


def alternate(per_side):
    return lambda j: (j % 2) * per_side + j // 2


def project_kernel(per_side, x_ref, *refs):
    pieces, (o_ref, w, sem) = refs[:10], refs[10:]
    j = pl.program_id(0)

    @pl.when(j == 0)
    def _():
        load_weights(pieces, w, sem, 0, o_ref.shape[2], per_side)

    chunk = alternate(per_side)(j)
    ready(w, sem, chunk)
    o_ref[0] = mm(x_ref[...], matrix(w, chunk)).astype(LOW)


def project(x, pieces, rows):
    count, width = pieces[0].shape[0], STEP_WIDTH
    per_side = pieces[0].shape[2] // width
    at = alternate(per_side)
    return pl.pallas_call(
        functools.partial(project_kernel, per_side),
        grid=(2 * per_side,),
        in_specs=[full(x.shape)] + [ANYWHERE] * 10,
        out_specs=pl.BlockSpec((1, x.shape[0], width), lambda j: (at(j), 0, 0)),
        out_shape=shaped((2 * per_side, x.shape[0], width), LOW),
        scratch_shapes=chunk_buffer((count, rows), 2 * per_side, width),
        compiler_params=params(32),
        cost_estimate=cost(6 * 1.1e9, 6 * 2e6),
        name="project",
    )(x, *pieces)


def head_parts(a, lane, scale=None):
    a = a if scale is None else a * jnp.asarray(scale, a.dtype)
    none = jnp.zeros_like(a)
    return jnp.where(lane < HEAD, a, none), jnp.where(lane < HEAD, none, a)


def attend_kernel(q_ref, k_ref, v_ref, bias_ref, o_ref, l_ref):
    k, v = k_ref[0], v_ref[0]
    lane = lax.broadcasted_iota(jnp.int32, k.shape, 1)
    outs, logs = [], []
    for q in head_parts(q_ref[0], lane, HEAD**-0.5):
        scores = mm(q, k, NT) + bias_ref[...].astype(F32)
        top = jnp.max(scores, axis=-1, keepdims=True)
        expo = jnp.exp(scores - top)
        total = jnp.sum(expo, axis=-1, keepdims=True)
        outs.append(mm((expo * (1.0 / total)).astype(LOW), v))
        logs.append(top + jnp.log(total))
    o_ref[...] = jnp.where(lane < HEAD, outs[0], outs[1]).astype(LOW)
    l_ref[...] = jnp.where(lane < HEAD, logs[0], logs[1])


def pair_specs(total, per_side):
    def spec(k):
        return pl.BlockSpec((1, total, 128), lambda g: ((g // per_side) * 3 + k, 0, g % per_side))

    return [spec(k) for k in range(3)]


def attention(qkv, bias):
    total, width = qkv.shape[1], qkv.shape[2] * 2
    pairs = width // 128
    return pl.pallas_call(
        attend_kernel,
        grid=(pairs,),
        in_specs=pair_specs(total, pairs // 2) + [full(bias.shape)],
        out_specs=[pl.BlockSpec((total, 128), lambda g: (0, g))] * 2,
        out_shape=[shaped((total, width), LOW), shaped((total, width), F32)],
        compiler_params=params(48),
        cost_estimate=cost(17 * 1.1e9, 17 * 2e6),
        name="attention",
    )(qkv, qkv, qkv, bias)


ROWS_AT_ONCE = 32


def by_rows(total, body, carry=0):
    def step(i, held):
        return body(pl.ds(pl.multiple_of(i * ROWS_AT_ONCE, ROWS_AT_ONCE), ROWS_AT_ONCE), held)

    return lax.fori_loop(0, total // ROWS_AT_ONCE, step, carry)


def normalize(v):
    center = v - jnp.mean(v, axis=-1, keepdims=True)
    inverse = lax.rsqrt(jnp.mean(center * center, axis=-1, keepdims=True) + NORM_EPS)
    return center * inverse, inverse


def unnormalize(scaled, normed, inverse):
    return inverse * (
        scaled
        - jnp.mean(scaled, axis=-1, keepdims=True)
        - normed * jnp.mean(scaled * normed, axis=-1, keepdims=True)
    )


def fold(a):
    return jnp.sum(a.reshape(-1, 8, a.shape[-1]), axis=0)


def gelu_parts(u):
    expo = jnp.exp(-0.5 * (u * u))
    t = 1.0 / (1.0 + 0.3275911 * 0.7071067811865476 * jnp.abs(u))
    poly = ((((1.061405429 * t - 1.453152027) * t + 1.421413741) * t - 0.284496736) * t + 0.254829592) * t
    tail = 0.5 * poly * expo
    phi = jnp.where(u < 0, tail, 1.0 - tail)
    return u * phi, phi + u * expo * 0.3989422804014327


def up_kernel(per_side, x_ref, ctx_ref, *refs):
    pieces = refs[:10]
    h_ref, n_ref, i_ref, norms_ref, g_ref, d_ref, wu, us, wo, os, nw, ns, acc = refs[10:]
    j = pl.program_id(0)
    width = g_ref.shape[2]

    @pl.when(j == 0)
    def _():
        first = 2 * per_side // 2 * width
        load_weights(pieces, nw, ns, first + width, 128, 1)
        load_weights(pieces, wo, os, first, width, 1)
        load_weights(pieces, wu, us, 0, width, per_side)
        ready(nw, ns, 0)
        ready(nw, ns, 1)
        cells = nw[0].reshape(-1, nw.shape[4], 128).astype(F32)
        side = x_ref.shape[1] // cells.shape[0]
        norms_ref[...] = jnp.concatenate([cells[i, :8, :side] for i in range(cells.shape[0])], axis=1)
        ready(wo, os, 0)
        acc[...] = mm(ctx_ref[:, :width], matrix(wo, 0), NT)
        ready(wo, os, 1)
        acc[...] += mm(ctx_ref[:, width:], matrix(wo, 1), NT)
        gain, shift = norms_ref[0:1], norms_ref[1:2]

        def rows(r, held):
            normed, inverse = normalize(x_ref[r].astype(F32) + acc[r])
            n_ref[r] = normed
            i_ref[r] = jnp.broadcast_to(inverse, (ROWS_AT_ONCE, 128))
            h_ref[r] = (normed * gain + shift).astype(LOW)
            return held

        by_rows(x_ref.shape[0], rows)

    chunk = alternate(per_side)(j)
    ready(wu, us, chunk)
    active, slope = gelu_parts(mm(h_ref[...], matrix(wu, chunk)))
    g_ref[0] = active.astype(LOW)
    d_ref[0] = slope.astype(LOW)


def up(x, context, pieces, rows, inner_part):
    count, width = pieces[0].shape[0], STEP_WIDTH
    per_side = inner_part // width
    at = alternate(per_side)
    total, model = x.shape
    chunks = pl.BlockSpec((1, total, width), lambda j: (at(j), 0, 0))
    return pl.pallas_call(
        functools.partial(up_kernel, per_side),
        grid=(2 * per_side,),
        in_specs=[full(x.shape)] * 2 + [ANYWHERE] * 10,
        out_specs=[full(x.shape), full(x.shape), full((total, 128)), full((8, model)), chunks, chunks],
        out_shape=[
            shaped(x.shape, LOW),
            shaped(x.shape, F32),
            shaped((total, 128), F32),
            shaped((8, model), F32),
            shaped((2 * per_side, total, width), LOW),
            shaped((2 * per_side, total, width), LOW),
        ],
        scratch_shapes=chunk_buffer((count, rows), 2 * per_side, width)
        + chunk_buffer((count, rows), 2, width)
        + chunk_buffer((count, 16), 2, 128)
        + [pltpu.VMEM(x.shape, F32)],
        compiler_params=params(56),
        cost_estimate=cost(22 * 1.1e9, 22 * 2e6),
        name="up",
    )(x, context, *pieces)


def down_kernel(per_side, pieces_count, g_ref, n_ref, norms_ref, cot_ref, *refs):
    pieces = refs[:pieces_count]
    o_ref, d_ref, f_ref, ng_ref, w, sem, acc = refs[pieces_count:]
    j = pl.program_id(0)

    @pl.when(j == 0)
    def _():
        load_weights(pieces, w, sem, 0, g_ref.shape[2], per_side)
        acc[...] = jnp.zeros_like(acc)

    chunk = alternate(per_side)(j)
    ready(w, sem, chunk)
    acc[...] += mm(g_ref[0], matrix(w, chunk), NT)

    @pl.when(j == 2 * per_side - 1)
    def _():
        gain_one, shift_one, gain, shift = (norms_ref[i : i + 1] for i in range(4))

        def rows(r, held):
            normed, inverse = normalize(n_ref[r] * gain_one + shift_one + acc[r])
            o_ref[r] = (normed * gain + shift).astype(LOW)
            dy = cot_ref[r].astype(F32)
            back = unnormalize(dy * gain, normed, inverse)
            d_ref[r] = back
            f_ref[r] = back.astype(LOW)
            return held[0] + fold(dy * normed), held[1] + fold(dy)

        none = jnp.zeros((8, acc.shape[1]), F32)
        gains, shifts = by_rows(acc.shape[0], rows, (none, none))
        ng_ref[...] = jnp.concatenate(
            [jnp.sum(gains, axis=0, keepdims=True), jnp.sum(shifts, axis=0, keepdims=True), none[:6]], axis=0
        )


def down(active, normed, norms, cot, pieces, rows):
    width = STEP_WIDTH
    chunks, total = active.shape[0], active.shape[1]
    at = alternate(chunks // 2)
    shape = normed.shape
    count = pieces[0].shape[0]
    return pl.pallas_call(
        functools.partial(down_kernel, chunks // 2, len(pieces)),
        grid=(chunks,),
        in_specs=[pl.BlockSpec((1, total, width), lambda j: (at(j), 0, 0)), full(shape), full(norms.shape), full(shape)]
        + [ANYWHERE] * len(pieces),
        out_specs=[full(shape), full(shape), full(shape), full(norms.shape)],
        out_shape=[shaped(shape, LOW), shaped(shape, F32), shaped(shape, LOW), shaped(norms.shape, F32)],
        scratch_shapes=chunk_buffer((count, rows), chunks, width) + [pltpu.VMEM(shape, F32)],
        compiler_params=params(56),
        cost_estimate=cost(17 * 1.1e9, 17 * 2e6),
        name="down",
    )(active, normed, norms, cot, *pieces)


def share_out(value, own_ref, other_ref):
    core = lax.axis_index("c")
    z, x, _, rows, width = own_ref.shape
    value = value.reshape(z, x, 2, rows, width)
    for parity in range(2):
        part = value[:, :, parity]

        @pl.when(core == parity)
        def _(part=part):
            own_ref[:, :, 0] = part

        @pl.when(core != parity)
        def _(part=part):
            other_ref[:, :, 0] = part


def share_specs(count, rows, per_side, columns):
    spec = pl.BlockSpec((count, 2, 1, rows, STEP_WIDTH), lambda j: (0, 0, j // per_side, 0, j % per_side))
    return [spec] * 2, [shaped((count, 2, 2, rows, columns), LOW)] * 2


def weight_grad_kernel(a_ref, b_ref, own_ref, other_ref):
    share_out(mm(a_ref[...], b_ref[0], TN).astype(LOW), own_ref, other_ref)


def weight_grad(a, b, spec, chunks, count, rows, name):
    out_specs, out_shape = share_specs(count, rows, chunks // 2, chunks // 2 * STEP_WIDTH)
    return pl.pallas_call(
        weight_grad_kernel,
        grid=(chunks,),
        in_specs=[full(a.shape), spec],
        out_specs=out_specs,
        out_shape=out_shape,
        compiler_params=params(32),
        cost_estimate=cost(9 * 1.1e9, 9 * 2e6),
        name=name,
    )(a, b)


def inner_kernel(per_side, down_count, f_ref, d_ref, h_ref, r_ref, n_ref, i_ref, norms_ref, *refs):
    downs, ups = refs[:down_count], refs[down_count : down_count + 10]
    own_ref, other_ref, g_ref, a_ref, ng_ref, wd, ds, wu, us, acc = refs[down_count + 10 :]
    j = pl.program_id(0)
    width = d_ref.shape[2]

    @pl.when(j == 0)
    def _():
        load_weights(downs, wd, ds, 0, width, per_side)
        load_weights(ups, wu, us, 0, width, per_side)
        acc[...] = r_ref[...]

    ready(wd, ds, j)
    grad = (mm(f_ref[...], matrix(wd, j)) * d_ref[0].astype(F32)).astype(LOW)
    share_out(mm(h_ref[...], grad, TN).astype(LOW), own_ref, other_ref)
    ready(wu, us, j)
    acc[...] += mm(grad, matrix(wu, j), NT)

    @pl.when(j == 2 * per_side - 1)
    def _():
        gain = norms_ref[0:1]

        def rows(r, held):
            dy, normed = acc[r], n_ref[r]
            back = unnormalize(dy * gain, normed, i_ref[r][:, :1])
            g_ref[r] = back
            a_ref[r] = back.astype(LOW)
            return held[0] + fold(dy * normed), held[1] + fold(dy)

        none = jnp.zeros((8, acc.shape[1]), F32)
        gains, shifts = by_rows(acc.shape[0], rows, (none, none))
        ng_ref[...] = jnp.concatenate(
            [jnp.sum(gains, axis=0, keepdims=True), jnp.sum(shifts, axis=0, keepdims=True), none[:6]], axis=0
        )


def inner_back(feed_grad, slope, hidden, second_grad, normed, inverse, norms, downs, ups, rows, columns):
    chunks, total, width = slope.shape
    shape = normed.shape
    count = ups[0].shape[0]
    out_specs, out_shape = share_specs(count, rows, chunks // 2, columns)
    once = pl.Buffered(1)

    def held(a):
        return pl.BlockSpec(a.shape, lambda j: (0,) * a.ndim, pipeline_mode=once)

    return pl.pallas_call(
        functools.partial(inner_kernel, chunks // 2, len(downs)),
        grid=(chunks,),
        in_specs=[held(feed_grad), pl.BlockSpec((1, total, width), lambda j: (j, 0, 0))]
        + [held(a) for a in (hidden, second_grad, normed, inverse, norms)]
        + [ANYWHERE] * (len(downs) + 10),
        out_specs=out_specs + [full(shape), full(shape), full(norms.shape)],
        out_shape=out_shape + [shaped(shape, F32), shaped(shape, LOW), shaped(norms.shape, F32)],
        scratch_shapes=chunk_buffer((count, rows), chunks, width) * 2 + [pltpu.VMEM(shape, F32)],
        compiler_params=params(58),
        cost_estimate=cost(32 * 1.1e9, 32 * 2e6),
        name="inner_back",
    )(feed_grad, slope, hidden, second_grad, normed, inverse, norms, *downs, *ups)


def out_kernel(column, a_ref, ctx_ref, one_ref, two_ref, own_in, other_in, *refs):
    pieces = refs[:10]
    own_ref, other_ref, o_ref, w, sem, tiles, out_sem = refs[10:]
    _, _, z, x, rows, _ = tiles.shape
    width = w.shape[5]
    core = lax.axis_index("c")
    load_weights(pieces, w, sem, column, width, 1)
    norm_grads = jnp.concatenate([one_ref[0:2], two_ref[0:2], one_ref[2:6]], axis=0)
    for y in range(2):
        grad = mm(a_ref[...], ctx_ref[:, y * width : (y + 1) * width], TN).astype(LOW).reshape(z, x, 2, rows, width)
        for parity in range(2):
            slot = (parity + core) % 2
            tiles[slot, y, :, :, :, :width] = grad[:, :, parity]
            for at in range(z * x):
                cell = norm_grads[:, (at * 2 + parity) * rows : (at * 2 + parity + 1) * rows]
                cell = jnp.concatenate([cell, jnp.zeros((8, 128 - rows), F32)], axis=1)
                cell = jnp.concatenate([cell, jnp.zeros((rows - 8, 128), F32)], axis=0)
                tiles[slot, y, at // x, at % x, :, width:] = cell.astype(LOW)
    copies = []
    for slot, ref in enumerate((own_ref, other_ref)):
        for y in range(2):
            copies.append(
                pltpu.make_async_copy(
                    tiles.at[slot, y], ref.at[:, :, y, :, pl.ds(column, width + 128)], out_sem.at[slot, y]
                )
            )
    for copy in copies:
        copy.start()
    for y in range(2):
        ready(w, sem, y)
        o_ref[:, y * width : (y + 1) * width] = mm(a_ref[...], matrix(w, y)).astype(LOW)
    for copy in copies:
        copy.wait()


def out_back(branch_grad, context, one, two, own, other, pieces, rows, column):
    count, width = pieces[0].shape[0], STEP_WIDTH
    inside = pl.BlockSpec(memory_space=pltpu.VMEM)
    return pl.pallas_call(
        functools.partial(out_kernel, column),
        in_specs=[inside] * 4 + [ANYWHERE] * 12,
        out_specs=[ANYWHERE, ANYWHERE, inside],
        out_shape=[shaped(own.shape, LOW), shaped(other.shape, LOW), shaped(context.shape, LOW)],
        scratch_shapes=chunk_buffer((count, rows), 2, width)
        + [pltpu.VMEM((2, 2, count, 2, rows, width + 128), LOW), pltpu.SemaphoreType.DMA((2, 2))],
        input_output_aliases={4: 0, 5: 1},
        compiler_params=params(40),
        cost_estimate=cost(4 * 1.1e9, 4 * 2e6),
        name="out_back",
    )(branch_grad, context, one, two, own, other, *pieces)


def attend_back_kernel(q_ref, k_ref, v_ref, bias_ref, l_ref, g_ref, o_ref):
    k, v, grad = k_ref[0], v_ref[0], g_ref[...]
    lane = lax.broadcasted_iota(jnp.int32, k.shape, 1)
    scale = HEAD**-0.5
    queries = q_ref[0]
    outs = []
    for h, (q, own_grad) in enumerate(zip(head_parts(queries, lane, scale), head_parts(grad, lane))):
        log_total = l_ref[:, h * HEAD : h * HEAD + 1]
        probs = jnp.exp(mm(q, k, NT) + bias_ref[...].astype(F32) - log_total)
        prob_grad = mm(own_grad, v, NT)
        score_grad = probs * (prob_grad - jnp.sum(probs * prob_grad, axis=-1, keepdims=True))
        score_grad = score_grad.astype(LOW)
        outs.append(
            (mm(score_grad, k) * scale, mm(score_grad, queries, TN) * scale, mm(probs.astype(LOW), grad, TN))
        )
    for i in range(3):
        o_ref[i] = jnp.where(lane < HEAD, outs[0][i], outs[1][i]).astype(LOW)


def attention_back(qkv, bias, logs, grad):
    total, width = grad.shape
    pairs = width // 128
    column = pl.BlockSpec((total, 128), lambda g: (0, g))
    return pl.pallas_call(
        attend_back_kernel,
        grid=(pairs,),
        in_specs=pair_specs(total, pairs // 2) + [full(bias.shape), column, column],
        out_specs=pl.BlockSpec((3, total, 128), lambda g: (0, 0, g)),
        out_shape=shaped((3, total, width), LOW),
        compiler_params=params(48),
        cost_estimate=cost(25 * 1.1e9, 25 * 2e6),
        name="attention_back",
    )(qkv, qkv, qkv, bias, logs, grad)


def input_kernel(per_side, g_ref, r_ref, *refs):
    pieces, (o_ref, w, sem, acc) = refs[:10], refs[10:]
    j = pl.program_id(0)

    @pl.when(j == 0)
    def _():
        load_weights(pieces, w, sem, 0, g_ref.shape[2], per_side)
        acc[...] = r_ref[...]

    chunk = alternate(per_side)(j)
    ready(w, sem, chunk)
    acc[...] += mm(g_ref[0], matrix(w, chunk), NT)

    @pl.when(j == 2 * per_side - 1)
    def _():
        o_ref[...] = acc[...].astype(LOW)


def input_back(grads, first_grad, pieces, rows):
    count, width = pieces[0].shape[0], STEP_WIDTH
    per_side = grads.shape[0]
    shape = first_grad.shape
    return pl.pallas_call(
        functools.partial(input_kernel, per_side),
        grid=(2 * per_side,),
        in_specs=[pl.BlockSpec((1, shape[0], width), lambda j: (j // 2, 0, j % 2)), full(shape)] + [ANYWHERE] * 10,
        out_specs=full(shape),
        out_shape=shaped(shape, LOW),
        scratch_shapes=chunk_buffer((count, rows), 2 * per_side, width) + [pltpu.VMEM(shape, F32)],
        compiler_params=params(40),
        cost_estimate=cost(7 * 1.1e9, 7 * 2e6),
        name="input_back",
    )(grads, first_grad, *pieces)


def at(a, index, axis):
    return lax.dynamic_index_in_dim(a, index, axis, keepdims=False)


def chip_term(own, other, shift):
    x, y = place_xy(ring_place() + shift)
    return at(at(own, x, 1), y, 1).astype(F32) + at(at(other, x, 1), y, 1).astype(F32)


def ring_pair(to_right, to_left):
    return send(to_right, ("x", "y"), RING), send(to_left, ("x", "y"), RING_BACK)


def far_terms(own, other):
    far = chip_term(own, other, 2).astype(LOW)
    half = far.shape[0] // 2
    return far[:half], far[half:]


def near_terms(own, other, from_left, from_right):
    half = from_left.shape[0]
    right, left = chip_term(own, other, 1), chip_term(own, other, -1)
    to_right = jnp.concatenate([right[:half] + from_left.astype(F32), right[half:]]).astype(LOW)
    to_left = jnp.concatenate([left[:half], left[half:] + from_right.astype(F32)]).astype(LOW)
    return to_right, to_left


def line_terms(own, other, from_left, from_right):
    column = chip_term(own, other, 0) + from_left.astype(F32) + from_right.astype(F32)
    z = lax.axis_index("z")
    return [at(column, z, 0)] + [at(column, z ^ k, 0).astype(LOW) for k in range(1, column.shape[0])]


def line_send(terms):
    return [send(term, "z", partners(k + 1)) for k, term in enumerate(terms[1:])]


def total_of(own, others):
    for other in others:
        own = own + other.astype(F32)
    return own


def sum_over_all(value):
    value = value + send(value, "c", SWAP)
    square = [send(value, ("x", "y"), tuple((i, i ^ k) for i in range(4))) for k in (1, 2, 3)]
    value = (value + square[0]) + (square[1] + square[2])
    count, k = lax.axis_size("z"), 1
    while k < count:
        value = value + send(value, "z", tuple((i, i ^ k) for i in range(count)))
        k *= 2
    return value


def pad_rows(a, total):
    return jnp.pad(a, ((0, total - a.shape[0]), (0, 0)))


def mask_bias(doc_row, reset_row, live, total):
    kinds = jnp.concatenate([jnp.full((MEM,), -1, jnp.int32), doc_row, jnp.full((MEM,), -2, jnp.int32)])
    real = kinds.shape[0]
    kinds = jnp.pad(kinds, (0, total - real), constant_values=-3)
    place = jnp.arange(total, dtype=jnp.int32)
    choose = kinds[:, None] == jnp.arange(reset_row.shape[0], dtype=jnp.int32)[None, :]
    reset_query = jnp.sum(jnp.where(choose, reset_row[None, :], 0), axis=1)
    same = kinds[:, None] == kinds[None, :]
    live_key = place < jnp.minimum(live, MEM)
    token_sees = same | (live_key[None, :] & (reset_query == 0)[:, None])
    memory_sees = ((place >= MEM) | live_key)[None, :]
    sees = jnp.where((kinds < 0)[:, None], memory_sees, token_sees) & (place < real)[None, :]
    return jnp.where(sees, 0.0, MASKED).astype(LOW)


def whole_segment(
    tokens,
    cotangent,
    doc_ids,
    reset_flags,
    mem_live,
    qkv_weight,
    qkv_moment,
    qkv_square,
    qkv_average,
    out_weight,
    out_moment,
    out_square,
    out_average,
    up_weight,
    up_moment,
    up_square,
    up_average,
    down_weight,
    down_moment,
    down_square,
    down_average,
    norm_params,
    norm_moment,
    norm_square,
    norm_average,
):
    y = lax.axis_index("y")
    rows, inner_part = up_weight.shape
    count = lax.axis_size("z")
    width = tokens.shape[2]
    part = qkv_weight.shape[2]
    real = tokens.shape[1]
    total = -(-real // ROWS_AT_ONCE) * ROWS_AT_ONCE

    def mine(a):
        return lax.dynamic_index_in_dim(a, y, 0, keepdims=False)

    qkv_block = jnp.concatenate([qkv_weight[k] for k in range(3)], axis=1).astype(LOW)
    norm_block = jnp.pad(norm_params.astype(LOW), ((0, rows - 4), (0, 128 - rows)))
    second_block = jnp.concatenate([up_weight.astype(LOW), out_weight.T.astype(LOW), norm_block], axis=1)
    down_block = down_weight.T.astype(LOW)

    x = pad_rows(mine(tokens), total)
    cot = pad_rows(mine(cotangent), total)
    bias = mask_bias(mine(doc_ids), mine(reset_flags), mine(mem_live), total)

    z_qkv = line_pieces(qkv_block)
    z_second = line_pieces(after(second_block, *z_qkv))
    column_qkv = join_column(z_qkv)
    near_qkv = ring_near(column_qkv)
    far_qkv = ring_far(*near_qkv)
    w_qkv = both_cores((column_qkv,) + near_qkv + far_qkv)
    z_down = line_pieces(after(down_block, *z_second))
    column_second = after(join_column(z_second), *far_qkv)
    near_second = ring_near(column_second)

    qkv = project(after(x, column_second), w_qkv, rows)
    context, logs = attention(qkv, bias)

    near_second = after(near_second, context)
    far_second = ring_far(*near_second)
    w_second = both_cores((column_second,) + near_second + far_second)
    column_down = after(join_column([after(z_down[0], context)] + z_down[1:]), *far_second)
    near_down = ring_near(column_down)

    hidden, normed, inverse, norms, active, slope = up(x, after(context, column_down), w_second, rows, inner_part)

    near_down = after(near_down, active)
    far_down = ring_far(*near_down)
    w_down = both_cores((column_down,) + near_down + far_down)
    result, second_grad, feed_grad, norm_two = down(active, normed, norms, cot, w_down, rows)

    chunks = active.shape[0]
    own_down, other = weight_grad(
        feed_grad,
        active,
        pl.BlockSpec((1, total, STEP_WIDTH), lambda j: (j, 0, 0)),
        chunks,
        count,
        rows,
        "down_grad",
    )
    other_down = send(other, "c", SWAP)
    far = far_terms(own_down, other_down)
    far_down = ring_pair(*far)
    columns = inner_part + part + 128
    own, other, first_grad, branch_grad, norm_one = inner_back(
        after(feed_grad, *far),
        slope,
        hidden,
        second_grad,
        normed,
        inverse,
        norms,
        w_down,
        w_second,
        rows,
        columns,
    )
    far_down = after(far_down, branch_grad)
    near = near_terms(own_down, other_down, *far_down)
    near_down = ring_pair(*near)
    own_second, other, context_grad = out_back(
        after(branch_grad, *near), context, norm_one, norm_two, own, other, w_second, rows, inner_part
    )
    other_second = send(other, "c", SWAP)
    near_down = after(near_down, context_grad, other_second)
    line_down = line_terms(own_down, other_down, *near_down)
    others_down = line_send(line_down)
    far = far_terms(own_second, after(other_second, *near_down))
    far_second = ring_pair(*far)

    grads = attention_back(qkv, bias, logs, after(context_grad, *far, *line_down))

    far_second = after(far_second, grads)
    near = near_terms(own_second, other_second, *far_second)
    near_second = ring_pair(*near)
    own_qkv, other = weight_grad(
        after(x, *near),
        grads,
        pl.BlockSpec((1, total, STEP_WIDTH), lambda j: (j % 3, 0, j // 3)),
        6,
        count,
        rows,
        "qkv_grad",
    )
    other_qkv = send(other, "c", SWAP)
    own_grad = input_back(after(grads, own_qkv), first_grad, w_qkv, rows)
    near_second = after(near_second, own_grad)
    line_second = line_terms(own_second, other_second, *near_second)
    others_second = line_send(line_second)
    far = far_terms(own_qkv, after(other_qkv, *near_second))
    far_qkv = ring_pair(*far)
    near = near_terms(own_qkv, after(other_qkv, *line_second), *far_qkv)
    near_qkv = ring_pair(*near)
    line_qkv = line_terms(own_qkv, other_qkv, *near_qkv)
    others_qkv = line_send(line_qkv)
    down_sum = total_of(line_down[0], others_down)
    second_sum = total_of(line_second[0], others_second)
    qkv_sum = total_of(line_qkv[0], others_qkv)

    def both(own):
        own = own[:real]
        other = send(own, "y", SWAP)
        return jnp.where(y == 0, jnp.stack([own, other]), jnp.stack([other, own]))

    output = both(result)
    input_grad = both(own_grad).astype(F32)

    qkv_sum = qkv_sum.reshape(rows, 3, part).transpose(1, 0, 2)
    up_sum = second_sum[:, :inner_part]
    out_sum = second_sum[:, inner_part : inner_part + part].T
    norm_sum = second_sum[:4, inner_part + part : inner_part + part + rows]
    down_sum = down_sum.T
    local_squares = (
        jnp.sum(qkv_sum * qkv_sum)
        + jnp.sum(out_sum * out_sum)
        + jnp.sum(up_sum * up_sum)
        + jnp.sum(down_sum * down_sum)
        + jnp.sum(norm_sum * norm_sum) / lax.axis_size("y")
    )
    grad_norm = jnp.sqrt(sum_over_all(jnp.full((8, 128), local_squares))[0, 0])
    threshold = math.sqrt(4 * D * D + 2 * D * FF + 4 * D)
    factor = jnp.minimum(1.0, threshold / (grad_norm + 1e-06))
    new_qkv = adam_step(qkv_weight, qkv_moment, qkv_square, qkv_average, qkv_sum * factor, 0.02, 0.01)
    new_out = adam_step(out_weight, out_moment, out_square, out_average, out_sum * factor, 0.06, 0.01)
    new_up = adam_step(up_weight, up_moment, up_square, up_average, up_sum * factor, 0.02, 0.01)
    new_down = adam_step(down_weight, down_moment, down_square, down_average, down_sum * factor, 0.02, 0.01)
    new_norm = adam_step(norm_params, norm_moment, norm_square, norm_average, norm_sum * factor, 0.4, 0.0)
    return (output, input_grad, grad_norm) + new_qkv + new_out + new_up + new_down + new_norm


def solution(mesh):
    wide, narrow = mesh.shape["wide"], mesh.shape["narrow"]

    def placed(w, n):
        state = [P(None, w, n)] * 4 + [P(n, w)] * 4 + [P(w, n)] * 4 + [P(n, w)] * 4 + [P(None, w)] * 4
        return (
            tuple([P(w, None, None)] * 2 + [P(w, None)] * 2 + [P(w)] + state),
            tuple([P(w, None, None)] * 2 + [P()] + state),
        )

    def run(*args):
        if narrow == 2 and wide % 8 == 0 and args[0].shape[0] == wide * narrow:
            body = whole_segment
            grid = jax.sharding.Mesh(mesh.devices.reshape(wide // 4, 2, 2, 2), ("z", "x", "c", "y"))
            ins, outs = placed(("z", "x", "c"), "y")
        else:
            body, grid = shared_rows, mesh
            ins, outs = placed("wide", "narrow")
        return jax.shard_map(body, mesh=grid, in_specs=ins, out_specs=outs, check_vma=False)(*args)

    return run
```

```python
import functools
import math

import jax
import jax.numpy as jnp
from jax import lax
from jax.experimental import pallas as pl
from jax.experimental.pallas import tpu as pltpu
from jax.sharding import PartitionSpec as P

D = 1024
HEAD = 64
FF = 4096
MEM = 10
STEP = 10


NORM_EPS = 1e-12
BETA_ONE = 0.9
BETA_TWO = 0.98
ADAM_EPS = 1e-06
AVERAGE_KEEP = 0.75
MASKED = -1e30


def allowed_mask(doc_row, reset_row, live_count):
    rows_all = doc_row.shape[0] + 2 * MEM
    kinds = jnp.concatenate(
        [jnp.full((MEM,), -1, jnp.int32), doc_row, jnp.full((MEM,), -2, jnp.int32)]
    )
    place = jnp.arange(rows_all, dtype=jnp.int32)
    read_key = place < MEM
    live_key = place < live_count
    choose = kinds[:, None] == jnp.arange(reset_row.shape[0], dtype=jnp.int32)[None, :]
    reset_query = jnp.sum(jnp.where(choose, reset_row[None, :], 0), axis=1)
    memory_query = kinds < 0
    same_doc = kinds[:, None] == kinds[None, :]
    token_sees = same_doc | (read_key & live_key)[None, :] & (reset_query == 0)[:, None]
    memory_sees = jnp.broadcast_to((~read_key | live_key)[None, :], (rows_all, rows_all))
    return jnp.where(memory_query[:, None], memory_sees, token_sees)


def norm_forward(rows_in, gain, shift):
    center = rows_in - jnp.mean(rows_in, axis=-1, keepdims=True)
    inverse = lax.rsqrt(jnp.mean(center * center, axis=-1, keepdims=True) + NORM_EPS)
    normed = center * inverse
    return (normed * gain + shift, normed, inverse)


def norm_backward(grad, normed, inverse, gain):
    scaled = grad * gain
    back = inverse * (
        scaled
        - jnp.mean(scaled, axis=-1, keepdims=True)
        - normed * jnp.mean(scaled * normed, axis=-1, keepdims=True)
    )
    return (back, jnp.stack([jnp.sum(grad * normed, axis=0), jnp.sum(grad, axis=0)]))


def masked_scores(query, keys, allowed):
    scores = jnp.einsum("qhd,khd->hqk", query, keys, preferred_element_type=jnp.float32) * (
        1.0 / math.sqrt(HEAD)
    )
    return jnp.where(allowed[None], scores, MASKED)


def attend(inputs):
    query, keys, values, allowed = inputs
    scores = masked_scores(query, keys, allowed)
    row_top = jnp.max(scores, axis=-1, keepdims=True)
    expo = jnp.exp(scores - row_top)
    row_total = jnp.sum(expo, axis=-1, keepdims=True)
    probs = (expo / row_total).astype(jnp.bfloat16)
    context = jnp.einsum("hqk,khd->qhd", probs, values, preferred_element_type=jnp.float32)
    return (context.astype(jnp.bfloat16), row_top + jnp.log(row_total))


def attend_back(inputs):
    query, keys, values, allowed, log_total, context_grad = inputs
    probs = jnp.exp(masked_scores(query, keys, allowed) - log_total)
    value_grad = jnp.einsum(
        "hqk,qhd->khd", probs.astype(jnp.bfloat16), context_grad, preferred_element_type=jnp.float32
    )
    prob_grad = jnp.einsum("qhd,khd->hqk", context_grad, values, preferred_element_type=jnp.float32)
    score_grad = probs * (prob_grad - jnp.sum(probs * prob_grad, axis=-1, keepdims=True))
    score_grad = score_grad.astype(jnp.bfloat16)
    scale_now = 1.0 / math.sqrt(HEAD)
    query_grad = (
        jnp.einsum("hqk,khd->qhd", score_grad, keys, preferred_element_type=jnp.float32) * scale_now
    )
    key_grad = (
        jnp.einsum("hqk,qhd->khd", score_grad, query, preferred_element_type=jnp.float32)
        * scale_now
    )
    return (
        query_grad.astype(jnp.bfloat16),
        key_grad.astype(jnp.bfloat16),
        value_grad.astype(jnp.bfloat16),
    )


def adam_step(weight, moment, square, average, grad, rate, decay):
    moment = BETA_ONE * moment + (1.0 - BETA_ONE) * grad
    square = BETA_TWO * square + (1.0 - BETA_TWO) * grad * grad
    first_hat = moment / (1.0 - BETA_ONE**STEP)
    second_hat = square / (1.0 - BETA_TWO**STEP)
    weight = weight - rate * (first_hat / (jnp.sqrt(second_hat) + ADAM_EPS) + decay * weight)
    average = AVERAGE_KEEP * average + (1.0 - AVERAGE_KEEP) * weight
    return (weight, moment, square, average)


def row_scatter(terms):
    return lax.psum_scatter(terms, "narrow", scatter_dimension=0, tiled=True)


def row_gather(piece):
    return lax.all_gather(piece, "narrow", axis=0, tiled=True)


def narrow_norm(grads):
    return lax.psum(grads, "narrow")


def shared_rows(
    tokens,
    cotangent,
    doc_ids,
    reset_flags,
    mem_live,
    qkv_weight,
    qkv_moment,
    qkv_square,
    qkv_average,
    out_weight,
    out_moment,
    out_square,
    out_average,
    up_weight,
    up_moment,
    up_square,
    up_average,
    down_weight,
    down_moment,
    down_square,
    down_average,
    norm_params,
    norm_moment,
    norm_square,
    norm_average,
):
    narrow_count = lax.axis_size("narrow")
    seg_count, rows_all, width = tokens.shape
    w_qkv, w_out, w_up, w_down, norms_low = (
        lax.all_gather(qkv_weight.astype(jnp.bfloat16), "wide", axis=1, tiled=True),
        lax.all_gather(out_weight.astype(jnp.bfloat16), "wide", axis=1, tiled=True),
        lax.all_gather(up_weight.astype(jnp.bfloat16), "wide", axis=0, tiled=True),
        lax.all_gather(down_weight.astype(jnp.bfloat16), "wide", axis=1, tiled=True),
        lax.all_gather(norm_params.astype(jnp.bfloat16), "wide", axis=1, tiled=True),
    )
    norms = norms_low.astype(jnp.float32)
    local_cols = w_qkv.shape[2]
    local_heads = local_cols // HEAD
    total_rows = seg_count * rows_all
    flat_in = tokens.reshape(total_rows, width)
    flat_cot = cotangent.reshape(total_rows, width)
    allowed = jax.vmap(allowed_mask)(doc_ids, reset_flags, mem_live)
    projected = jnp.einsum(
        "md,kdc->kmc", flat_in, w_qkv, preferred_element_type=jnp.float32
    ).astype(jnp.bfloat16)
    split_heads = projected.reshape(3, seg_count, rows_all, local_heads, HEAD)
    query, keys, values = (split_heads[0], split_heads[1], split_heads[2])
    context, log_total = lax.map(attend, (query, keys, values, allowed))
    context_flat = context.reshape(total_rows, local_cols)
    attention_terms = jnp.dot(context_flat, w_out, preferred_element_type=jnp.float32)
    share = total_rows // narrow_count
    row_start = lax.axis_index("narrow") * share
    own_in = lax.dynamic_slice_in_dim(flat_in, row_start, share, 0)
    own_cot = lax.dynamic_slice_in_dim(flat_cot, row_start, share, 0)
    first_sum = own_in.astype(jnp.float32) + row_scatter(attention_terms)
    hidden, normed_one, inverse_one = norm_forward(first_sum, norms[0], norms[1])
    hidden_low = row_gather(hidden.astype(jnp.bfloat16))
    inner = jnp.dot(hidden_low, w_up, preferred_element_type=jnp.float32)
    active, gelu_pull = jax.vjp(lambda value_in: jax.nn.gelu(value_in, approximate=False), inner)
    active_low = active.astype(jnp.bfloat16)
    feed_terms = jnp.dot(active_low, w_down, preferred_element_type=jnp.float32)
    feed = row_scatter(feed_terms)
    second_sum = hidden + feed
    result, normed_two, inverse_two = norm_forward(second_sum, norms[2], norms[3])
    result_low = result.astype(jnp.bfloat16)
    second_grad, norm_two_grads = norm_backward(
        own_cot.astype(jnp.float32), normed_two, inverse_two, norms[2]
    )
    norm_two_grads = narrow_norm(norm_two_grads)
    output = row_gather(result_low)
    feed_grad = row_gather(second_grad.astype(jnp.bfloat16))
    output = output.reshape(seg_count, rows_all, width)
    down_grad = jnp.einsum("mf,md->fd", active_low, feed_grad, preferred_element_type=jnp.float32)
    active_grad = jnp.einsum("md,fd->mf", feed_grad, w_down, preferred_element_type=jnp.float32)
    inner_grad = gelu_pull(active_grad)[0].astype(jnp.bfloat16)
    up_grad = jnp.einsum("md,mf->df", hidden_low, inner_grad, preferred_element_type=jnp.float32)
    hidden_terms = jnp.einsum("mf,df->md", inner_grad, w_up, preferred_element_type=jnp.float32)
    hidden_grad = second_grad + row_scatter(hidden_terms)
    first_grad, norm_one_grads = norm_backward(hidden_grad, normed_one, inverse_one, norms[0])
    norm_one_grads = narrow_norm(norm_one_grads)
    branch_grad = row_gather(first_grad.astype(jnp.bfloat16))
    out_grad_weight = jnp.einsum(
        "mc,md->cd", context_flat, branch_grad, preferred_element_type=jnp.float32
    )
    context_grad = jnp.einsum(
        "md,cd->mc", branch_grad, w_out, preferred_element_type=jnp.float32
    ).astype(jnp.bfloat16)
    context_grad = context_grad.reshape(seg_count, rows_all, local_heads, HEAD)
    query_grad, key_grad, value_grad = lax.map(
        attend_back, (query, keys, values, allowed, log_total, context_grad)
    )
    stacked_grad = jnp.stack([query_grad, key_grad, value_grad]).reshape(3, total_rows, local_cols)
    qkv_grad = jnp.einsum("md,kmc->kdc", flat_in, stacked_grad, preferred_element_type=jnp.float32)
    input_terms = jnp.einsum("kmc,kdc->md", stacked_grad, w_qkv, preferred_element_type=jnp.float32)
    input_grad = lax.all_gather(first_grad + row_scatter(input_terms), "narrow", axis=0, tiled=True)
    input_grad = input_grad.reshape(seg_count, rows_all, width)
    norm_grads = jnp.concatenate([norm_one_grads, norm_two_grads], axis=0)
    qkv_sum, out_sum, up_sum, down_sum, norm_sum = (
        lax.psum_scatter(qkv_grad, "wide", scatter_dimension=1, tiled=True),
        lax.psum_scatter(out_grad_weight, "wide", scatter_dimension=1, tiled=True),
        lax.psum_scatter(up_grad, "wide", scatter_dimension=0, tiled=True),
        lax.psum_scatter(down_grad, "wide", scatter_dimension=1, tiled=True),
        lax.psum_scatter(norm_grads, "wide", scatter_dimension=1, tiled=True),
    )
    local_squares = (
        jnp.sum(qkv_sum * qkv_sum)
        + jnp.sum(out_sum * out_sum)
        + jnp.sum(up_sum * up_sum)
        + jnp.sum(down_sum * down_sum)
        + jnp.sum(norm_sum * norm_sum) / narrow_count
    )
    grad_norm = jnp.sqrt(lax.psum(local_squares, ("wide", "narrow")))
    threshold = math.sqrt(4 * D * D + 2 * D * FF + 4 * D)
    factor = jnp.minimum(1.0, threshold / (grad_norm + 1e-06))
    new_qkv = adam_step(
        qkv_weight, qkv_moment, qkv_square, qkv_average, qkv_sum * factor, 0.02, 0.01
    )
    new_out = adam_step(
        out_weight, out_moment, out_square, out_average, out_sum * factor, 0.06, 0.01
    )
    new_up = adam_step(up_weight, up_moment, up_square, up_average, up_sum * factor, 0.02, 0.01)
    new_down = adam_step(
        down_weight, down_moment, down_square, down_average, down_sum * factor, 0.02, 0.01
    )
    new_norm = adam_step(
        norm_params, norm_moment, norm_square, norm_average, norm_sum * factor, 0.4, 0.0
    )
    return (
        output,
        input_grad,
        grad_norm,
        new_qkv[0],
        new_qkv[1],
        new_qkv[2],
        new_qkv[3],
        new_out[0],
        new_out[1],
        new_out[2],
        new_out[3],
        new_up[0],
        new_up[1],
        new_up[2],
        new_up[3],
        new_down[0],
        new_down[1],
        new_down[2],
        new_down[3],
        new_norm[0],
        new_norm[1],
        new_norm[2],
        new_norm[3],
    )


SWAP = ((0, 1), (1, 0))
RING = ((0, 1), (1, 3), (3, 2), (2, 0))
RING_BACK = tuple((b, a) for a, b in RING)


def send(block, axes, pairs):
    return lax.ppermute(block, axes, list(pairs))


def ring_place():
    x, y = lax.axis_index("x"), lax.axis_index("y")
    return jnp.where(x == 0, y, 3 - y)


def place_xy(place):
    place = lax.rem(place + 4, 4)
    x = place // 2
    return x, jnp.where(x == 0, place, 3 - place)


def ring_near(block):
    return send(block, ("x", "y"), RING), send(block, ("x", "y"), RING_BACK)


def ring_far(left, right):
    half = left.shape[0] // 2
    return send(left[:half], ("x", "y"), RING), send(right[half:], ("x", "y"), RING_BACK)


def after(value, *others):
    return lax.optimization_barrier((value,) + others)[0]


STEP_WIDTH = 512
RING_SHIFTS = (0, -1, 1, 2, 2)
NT = (((1,), (1,)), ((), ()))
TN = (((0,), (0,)), ((), ()))
NN = (((1,), (0,)), ((), ()))
F32, LOW = jnp.float32, jnp.bfloat16
ANYWHERE = pl.BlockSpec(memory_space=pltpu.HBM)


def params(mib):
    return pltpu.CompilerParams(vmem_limit_bytes=mib << 20)


def cost(flops, moved):
    return pl.CostEstimate(flops=int(flops), bytes_accessed=int(moved), transcendentals=0)


def shaped(shape, dtype):
    return jax.ShapeDtypeStruct(shape, dtype)


def full(shape):
    return pl.BlockSpec(shape, lambda *_: (0,) * len(shape))


def mm(a, b, dims=NN):
    return lax.dot_general(a, b, dims, preferred_element_type=F32)


def join_column_kernel(count, *refs):
    out, sem = refs[-2:]
    z = lax.axis_index("z")
    copies = [pltpu.make_async_copy(ref, out.at[z ^ k], sem.at[k]) for k, ref in enumerate(refs[:count])]
    for copy in copies:
        copy.start()
    for copy in copies:
        copy.wait()


def partners(k):
    return tuple((i, i ^ k) for i in range(lax.axis_size("z")))


def line_pieces(block):
    return [block] + [send(block, "z", partners(k)) for k in range(1, lax.axis_size("z"))]


def join_column(pieces):
    count = len(pieces)
    shape = (count,) + pieces[0].shape
    return pl.pallas_call(
        functools.partial(join_column_kernel, count),
        in_specs=[ANYWHERE] * count,
        out_specs=pl.BlockSpec(memory_space=pltpu.VMEM),
        out_shape=shaped(shape, pieces[0].dtype),
        scratch_shapes=[pltpu.SemaphoreType.DMA((count,))],
        compiler_params=params(60),
        name="join_column",
    )(*pieces)


def join_pair_kernel(axis, own, other, out, sem):
    place = lax.axis_index(axis)
    copies = [pltpu.make_async_copy(own, out.at[place], sem.at[0])]
    copies.append(pltpu.make_async_copy(other, out.at[1 - place], sem.at[1]))
    for copy in copies:
        copy.start()
    for copy in copies:
        copy.wait()


def join_pair(own, other, axis):
    return pl.pallas_call(
        functools.partial(join_pair_kernel, axis),
        in_specs=[ANYWHERE] * 2,
        out_specs=pl.BlockSpec(memory_space=pltpu.VMEM),
        out_shape=shaped((2,) + own.shape, own.dtype),
        scratch_shapes=[pltpu.SemaphoreType.DMA((2,))],
        compiler_params=params(60),
        name="join_pair",
    )(own, other)


def both_cores(pieces):
    return list(pieces) + [send(p, "c", SWAP) for p in pieces]


def load_weights(pieces, w, sem, column, width, per_side):
    place, core = ring_place(), lax.axis_index("c")
    rows = w.shape[4]
    for k in range(per_side):
        for group, core_at in ((pieces[:5], core), (pieces[5:], 1 - core)):
            for i, (ref, shift) in enumerate(zip(group, RING_SHIFTS)):
                x, y = place_xy(place + shift)
                chunk = y * per_side + k
                first = ref.shape[0] if i == 4 else 0
                pltpu.make_async_copy(
                    ref.at[:, pl.ds(0, rows), pl.ds(column + k * width, width)],
                    w.at[chunk, pl.ds(first, ref.shape[0]), x, core_at],
                    sem.at[chunk],
                ).start()


def load_lines(pieces, w, sem, width, per_side):
    z, core = lax.axis_index("z"), lax.axis_index("c")
    count = len(pieces) // 2
    for k in range(per_side):
        for group, core_at in ((pieces[:count], core), (pieces[count:], 1 - core)):
            for i, ref in enumerate(group):
                for y in range(2):
                    chunk = y * per_side + k
                    pltpu.make_async_copy(
                        ref.at[:, y, :, pl.ds(k * width, width)], w.at[chunk, z ^ i, :, core_at], sem.at[chunk]
                    ).start()


def ready(w, sem, chunk):
    pltpu.make_async_copy(w.at[chunk], w.at[chunk], sem.at[chunk]).wait()


def matrix(w, chunk):
    block = w[chunk]
    return block.reshape(-1, block.shape[-1])


def chunk_buffer(shapes, chunks, width):
    z, rows = shapes
    return [pltpu.VMEM((chunks, z, 2, 2, rows, width), LOW), pltpu.SemaphoreType.DMA((chunks,))]


def alternate(per_side):
    return lambda j: (j % 2) * per_side + j // 2


def project_kernel(per_side, x_ref, *refs):
    pieces, (o_ref, w, sem) = refs[:10], refs[10:]
    j = pl.program_id(0)

    @pl.when(j == 0)
    def _():
        load_weights(pieces, w, sem, 0, o_ref.shape[2], per_side)

    chunk = alternate(per_side)(j)
    ready(w, sem, chunk)
    o_ref[0] = mm(x_ref[...], matrix(w, chunk)).astype(LOW)


def project(x, pieces, rows):
    count, width = pieces[0].shape[0], STEP_WIDTH
    per_side = pieces[0].shape[2] // width
    at = alternate(per_side)
    return pl.pallas_call(
        functools.partial(project_kernel, per_side),
        grid=(2 * per_side,),
        in_specs=[full(x.shape)] + [ANYWHERE] * 10,
        out_specs=pl.BlockSpec((1, x.shape[0], width), lambda j: (at(j), 0, 0)),
        out_shape=shaped((2 * per_side, x.shape[0], width), LOW),
        scratch_shapes=chunk_buffer((count, rows), 2 * per_side, width),
        compiler_params=params(60),
        cost_estimate=cost(6 * 1.1e9, 6 * 2e6),
        name="project",
    )(x, *pieces)


def head_parts(a, lane, scale=None):
    a = a if scale is None else a * jnp.asarray(scale, a.dtype)
    none = jnp.zeros_like(a)
    return jnp.where(lane < HEAD, a, none), jnp.where(lane < HEAD, none, a)


def attend_kernel(q_ref, k_ref, v_ref, bias_ref, o_ref, l_ref):
    k, v = k_ref[0], v_ref[0]
    lane = lax.broadcasted_iota(jnp.int32, k.shape, 1)
    outs, logs = [], []
    for q in head_parts(q_ref[0], lane, HEAD**-0.5):
        scores = mm(q, k, NT) + bias_ref[...].astype(F32)
        top = jnp.max(scores, axis=-1, keepdims=True)
        expo = jnp.exp(scores - top)
        total = jnp.sum(expo, axis=-1, keepdims=True)
        outs.append(mm((expo * (1.0 / total)).astype(LOW), v))
        logs.append(top + jnp.log(total))
    o_ref[...] = jnp.where(lane < HEAD, outs[0], outs[1]).astype(LOW)
    l_ref[...] = jnp.where(lane < HEAD, logs[0], logs[1])


def pair_specs(total, per_side):
    def spec(k):
        return pl.BlockSpec((1, total, 128), lambda g: ((g // per_side) * 3 + k, 0, g % per_side))

    return [spec(k) for k in range(3)]


def attention(qkv, bias):
    total, width = qkv.shape[1], qkv.shape[2] * 2
    pairs = width // 128
    return pl.pallas_call(
        attend_kernel,
        grid=(pairs,),
        in_specs=pair_specs(total, pairs // 2) + [full(bias.shape)],
        out_specs=[pl.BlockSpec((total, 128), lambda g: (0, g))] * 2,
        out_shape=[shaped((total, width), LOW), shaped((total, width), F32)],
        compiler_params=params(60),
        cost_estimate=cost(17 * 1.1e9, 17 * 2e6),
        name="attention",
    )(qkv, qkv, qkv, bias)


ROWS_AT_ONCE = 32


def by_rows(total, body, carry=0):
    def step(i, held):
        return body(pl.ds(pl.multiple_of(i * ROWS_AT_ONCE, ROWS_AT_ONCE), ROWS_AT_ONCE), held)

    return lax.fori_loop(0, total // ROWS_AT_ONCE, step, carry)


def normalize(v):
    center = v - jnp.mean(v, axis=-1, keepdims=True)
    inverse = lax.rsqrt(jnp.mean(center * center, axis=-1, keepdims=True) + NORM_EPS)
    return center * inverse, inverse


def unnormalize(scaled, normed, inverse):
    return inverse * (
        scaled
        - jnp.mean(scaled, axis=-1, keepdims=True)
        - normed * jnp.mean(scaled * normed, axis=-1, keepdims=True)
    )


def fold(a):
    return jnp.sum(a.reshape(-1, 8, a.shape[-1]), axis=0)


def gelu_parts(u):
    expo = jnp.exp(-0.5 * (u * u))
    t = 1.0 / (1.0 + 0.3275911 * 0.7071067811865476 * jnp.abs(u))
    poly = ((((1.061405429 * t - 1.453152027) * t + 1.421413741) * t - 0.284496736) * t + 0.254829592) * t
    tail = 0.5 * poly * expo
    phi = jnp.where(u < 0, tail, 1.0 - tail)
    return u * phi, phi + u * expo * 0.3989422804014327


def up_kernel(per_side, x_ref, ctx_ref, *refs):
    pieces = refs[:10]
    h_ref, n_ref, i_ref, norms_ref, g_ref, d_ref, wu, us, wo, os, nw, ns, acc = refs[10:]
    j = pl.program_id(0)
    width = g_ref.shape[2]

    @pl.when(j == 0)
    def _():
        first = 2 * per_side // 2 * width
        load_weights(pieces, nw, ns, first + width, 128, 1)
        load_weights(pieces, wo, os, first, width, 1)
        load_weights(pieces, wu, us, 0, width, per_side)
        ready(nw, ns, 0)
        ready(nw, ns, 1)
        cells = nw[0].reshape(-1, nw.shape[4], 128).astype(F32)
        side = x_ref.shape[1] // cells.shape[0]
        norms_ref[...] = jnp.concatenate([cells[i, :8, :side] for i in range(cells.shape[0])], axis=1)
        ready(wo, os, 0)
        acc[...] = mm(ctx_ref[:, :width], matrix(wo, 0), NT)
        ready(wo, os, 1)
        acc[...] += mm(ctx_ref[:, width:], matrix(wo, 1), NT)
        gain, shift = norms_ref[0:1], norms_ref[1:2]

        def rows(r, held):
            normed, inverse = normalize(x_ref[r].astype(F32) + acc[r])
            n_ref[r] = normed
            i_ref[r] = jnp.broadcast_to(inverse, (ROWS_AT_ONCE, 128))
            h_ref[r] = (normed * gain + shift).astype(LOW)
            return held

        by_rows(x_ref.shape[0], rows)

    chunk = alternate(per_side)(j)
    ready(wu, us, chunk)
    active, slope = gelu_parts(mm(h_ref[...], matrix(wu, chunk)))
    g_ref[0] = active.astype(LOW)
    d_ref[0] = slope.astype(LOW)


def up(x, context, pieces, rows, inner_part):
    count, width = pieces[0].shape[0], STEP_WIDTH
    per_side = inner_part // width
    at = alternate(per_side)
    total, model = x.shape
    chunks = pl.BlockSpec((1, total, width), lambda j: (at(j), 0, 0))
    return pl.pallas_call(
        functools.partial(up_kernel, per_side),
        grid=(2 * per_side,),
        in_specs=[full(x.shape)] * 2 + [ANYWHERE] * 10,
        out_specs=[full(x.shape), full(x.shape), full((total, 128)), full((8, model)), chunks, chunks],
        out_shape=[
            shaped(x.shape, LOW),
            shaped(x.shape, F32),
            shaped((total, 128), F32),
            shaped((8, model), F32),
            shaped((2 * per_side, total, width), LOW),
            shaped((2 * per_side, total, width), LOW),
        ],
        scratch_shapes=chunk_buffer((count, rows), 2 * per_side, width)
        + chunk_buffer((count, rows), 2, width)
        + chunk_buffer((count, 16), 2, 128)
        + [pltpu.VMEM(x.shape, F32)],
        compiler_params=params(60),
        cost_estimate=cost(22 * 1.1e9, 22 * 2e6),
        name="up",
    )(x, context, *pieces)


def down_kernel(per_side, pieces_count, g_ref, n_ref, norms_ref, cot_ref, *refs):
    pieces = refs[:pieces_count]
    o_ref, d_ref, f_ref, ng_ref, w, sem, acc = refs[pieces_count:]
    j = pl.program_id(0)

    @pl.when(j == 0)
    def _():
        load_lines(pieces, w, sem, g_ref.shape[2], per_side)
        acc[...] = jnp.zeros_like(acc)

    chunk = alternate(per_side)(j)
    ready(w, sem, chunk)
    acc[...] += mm(g_ref[0], matrix(w, chunk), NT)

    @pl.when(j == 2 * per_side - 1)
    def _():
        gain_one, shift_one, gain, shift = (norms_ref[i : i + 1] for i in range(4))

        def rows(r, held):
            normed, inverse = normalize(n_ref[r] * gain_one + shift_one + acc[r])
            o_ref[r] = (normed * gain + shift).astype(LOW)
            dy = cot_ref[r].astype(F32)
            back = unnormalize(dy * gain, normed, inverse)
            d_ref[r] = back
            f_ref[r] = back.astype(LOW)
            return held[0] + fold(dy * normed), held[1] + fold(dy)

        none = jnp.zeros((8, acc.shape[1]), F32)
        gains, shifts = by_rows(acc.shape[0], rows, (none, none))
        ng_ref[...] = jnp.concatenate(
            [jnp.sum(gains, axis=0, keepdims=True), jnp.sum(shifts, axis=0, keepdims=True), none[:6]], axis=0
        )


def down(active, normed, norms, cot, pieces, rows):
    width = STEP_WIDTH
    chunks, total = active.shape[0], active.shape[1]
    at = alternate(chunks // 2)
    shape = normed.shape
    count = len(pieces) // 2
    return pl.pallas_call(
        functools.partial(down_kernel, chunks // 2, len(pieces)),
        grid=(chunks,),
        in_specs=[pl.BlockSpec((1, total, width), lambda j: (at(j), 0, 0)), full(shape), full(norms.shape), full(shape)]
        + [ANYWHERE] * len(pieces),
        out_specs=[full(shape), full(shape), full(shape), full(norms.shape)],
        out_shape=[shaped(shape, LOW), shaped(shape, F32), shaped(shape, LOW), shaped(norms.shape, F32)],
        scratch_shapes=chunk_buffer((count, rows), chunks, width) + [pltpu.VMEM(shape, F32)],
        compiler_params=params(60),
        cost_estimate=cost(17 * 1.1e9, 17 * 2e6),
        name="down",
    )(active, normed, norms, cot, *pieces)


def share_out(value, own_ref, other_ref, lines_first=False):
    core = lax.axis_index("c")
    if lines_first:
        z, x, _, rows, width = own_ref.shape
        value = value.reshape(z, x, 2, rows, width)
        for parity in range(2):

            @pl.when(core == parity)
            def _(parity=parity):
                own_ref[:, :, 0] = value[:, :, parity]

            @pl.when(core != parity)
            def _(parity=parity):
                other_ref[:, :, 0] = value[:, :, parity]

        return
    squares, _, z, rows, width = own_ref.shape
    value = value.reshape(z, squares, 2, rows, width)
    for parity in range(2):

        @pl.when(core == parity)
        def _(parity=parity):
            for x in range(squares):
                own_ref[x, 0] = value[:, x, parity]

        @pl.when(core != parity)
        def _(parity=parity):
            for x in range(squares):
                other_ref[x, 0] = value[:, x, parity]


def share_specs(count, rows, per_side, columns):
    spec = pl.BlockSpec((2, 1, count, rows, STEP_WIDTH), lambda j: (0, j // per_side, 0, 0, j % per_side))
    return [spec] * 2, [shaped((2, 2, count, rows, columns), LOW)] * 2


def weight_grad_kernel(lines_first, a_ref, b_ref, own_ref, other_ref):
    share_out(mm(a_ref[...], b_ref[0], TN).astype(LOW), own_ref, other_ref, lines_first)


def weight_grad(a, b, spec, chunks, count, rows, name, lines_first=False):
    per_side = chunks // 2
    out_specs, out_shape = share_specs(count, rows, per_side, per_side * STEP_WIDTH)
    if lines_first:
        spec_out = pl.BlockSpec((count, 2, 1, rows, STEP_WIDTH), lambda j: (0, 0, j // per_side, 0, j % per_side))
        out_specs, out_shape = [spec_out] * 2, [shaped((count, 2, 2, rows, per_side * STEP_WIDTH), LOW)] * 2
    return pl.pallas_call(
        functools.partial(weight_grad_kernel, lines_first),
        grid=(chunks,),
        in_specs=[full(a.shape), spec],
        out_specs=out_specs,
        out_shape=out_shape,
        compiler_params=params(60),
        cost_estimate=cost(9 * 1.1e9, 9 * 2e6),
        name=name,
    )(a, b)


def inner_kernel(per_side, down_count, f_ref, d_ref, h_ref, r_ref, n_ref, i_ref, norms_ref, *refs):
    downs, ups = refs[:down_count], refs[down_count : down_count + 10]
    own_ref, other_ref, g_ref, a_ref, ng_ref, wd, ds, wu, us, acc = refs[down_count + 10 :]
    j = pl.program_id(0)
    width = d_ref.shape[2]

    @pl.when(j == 0)
    def _():
        load_lines(downs, wd, ds, width, per_side)
        load_weights(ups, wu, us, 0, width, per_side)
        acc[...] = r_ref[...]

    ready(wd, ds, j)
    grad = (mm(f_ref[...], matrix(wd, j)) * d_ref[0].astype(F32)).astype(LOW)
    share_out(mm(h_ref[...], grad, TN).astype(LOW), own_ref, other_ref)
    ready(wu, us, j)
    acc[...] += mm(grad, matrix(wu, j), NT)

    @pl.when(j == 2 * per_side - 1)
    def _():
        gain = norms_ref[0:1]

        def rows(r, held):
            dy, normed = acc[r], n_ref[r]
            back = unnormalize(dy * gain, normed, i_ref[r][:, :1])
            g_ref[r] = back
            a_ref[r] = back.astype(LOW)
            return held[0] + fold(dy * normed), held[1] + fold(dy)

        none = jnp.zeros((8, acc.shape[1]), F32)
        gains, shifts = by_rows(acc.shape[0], rows, (none, none))
        ng_ref[...] = jnp.concatenate(
            [jnp.sum(gains, axis=0, keepdims=True), jnp.sum(shifts, axis=0, keepdims=True), none[:6]], axis=0
        )


def inner_back(feed_grad, slope, hidden, second_grad, normed, inverse, norms, downs, ups, rows, columns):
    chunks, total, width = slope.shape
    shape = normed.shape
    count = ups[0].shape[0]
    out_specs, out_shape = share_specs(count, rows, chunks // 2, columns)
    once = pl.Buffered(1)

    def held(a):
        return pl.BlockSpec(a.shape, lambda j: (0,) * a.ndim, pipeline_mode=once)

    return pl.pallas_call(
        functools.partial(inner_kernel, chunks // 2, len(downs)),
        grid=(chunks,),
        in_specs=[held(feed_grad), pl.BlockSpec((1, total, width), lambda j: (j, 0, 0))]
        + [held(a) for a in (hidden, second_grad, normed, inverse, norms)]
        + [ANYWHERE] * (len(downs) + 10),
        out_specs=out_specs + [full(shape), full(shape), full(norms.shape)],
        out_shape=out_shape + [shaped(shape, F32), shaped(shape, LOW), shaped(norms.shape, F32)],
        scratch_shapes=chunk_buffer((count, rows), chunks, width) * 2 + [pltpu.VMEM(shape, F32)],
        compiler_params=params(60),
        cost_estimate=cost(32 * 1.1e9, 32 * 2e6),
        name="inner_back",
    )(feed_grad, slope, hidden, second_grad, normed, inverse, norms, *downs, *ups)


def out_kernel(column, a_ref, ctx_ref, one_ref, two_ref, own_in, other_in, *refs):
    pieces = refs[:10]
    own_ref, other_ref, o_ref, w, sem, tiles, out_sem = refs[10:]
    _, _, x, z, rows, _ = tiles.shape
    width = w.shape[5]
    core = lax.axis_index("c")
    load_weights(pieces, w, sem, column, width, 1)
    norm_grads = jnp.concatenate([one_ref[0:2], two_ref[0:2], one_ref[2:6]], axis=0)
    for y in range(2):
        grad = mm(a_ref[...], ctx_ref[:, y * width : (y + 1) * width], TN).astype(LOW).reshape(z, x, 2, rows, width)
        for parity in range(2):
            slot = (parity + core) % 2
            for at_x in range(x):
                tiles[slot, y, at_x, :, :, :width] = grad[:, at_x, parity]
            for at in range(z * x):
                cell = norm_grads[:, (at * 2 + parity) * rows : (at * 2 + parity + 1) * rows]
                cell = jnp.concatenate([cell, jnp.zeros((8, 128 - rows), F32)], axis=1)
                cell = jnp.concatenate([cell, jnp.zeros((rows - 8, 128), F32)], axis=0)
                tiles[slot, y, at % x, at // x, :, width:] = cell.astype(LOW)
    copies = []
    for slot, ref in enumerate((own_ref, other_ref)):
        for y in range(2):
            copies.append(
                pltpu.make_async_copy(
                    tiles.at[slot, y], ref.at[:, y, :, :, pl.ds(column, width + 128)], out_sem.at[slot, y]
                )
            )
    for copy in copies:
        copy.start()
    for y in range(2):
        ready(w, sem, y)
        o_ref[:, y * width : (y + 1) * width] = mm(a_ref[...], matrix(w, y)).astype(LOW)
    for copy in copies:
        copy.wait()


def out_back(branch_grad, context, one, two, own, other, pieces, rows, column):
    count, width = pieces[0].shape[0], STEP_WIDTH
    inside = pl.BlockSpec(memory_space=pltpu.VMEM)
    return pl.pallas_call(
        functools.partial(out_kernel, column),
        in_specs=[inside] * 4 + [ANYWHERE] * 12,
        out_specs=[ANYWHERE, ANYWHERE, inside],
        out_shape=[shaped(own.shape, LOW), shaped(other.shape, LOW), shaped(context.shape, LOW)],
        scratch_shapes=chunk_buffer((count, rows), 2, width)
        + [pltpu.VMEM((2, 2, 2, count, rows, width + 128), LOW), pltpu.SemaphoreType.DMA((2, 2))],
        input_output_aliases={4: 0, 5: 1},
        compiler_params=params(60),
        cost_estimate=cost(4 * 1.1e9, 4 * 2e6),
        name="out_back",
    )(branch_grad, context, one, two, own, other, *pieces)


def attend_back_kernel(q_ref, k_ref, v_ref, bias_ref, l_ref, g_ref, o_ref):
    k, v, grad = k_ref[0], v_ref[0], g_ref[...]
    lane = lax.broadcasted_iota(jnp.int32, k.shape, 1)
    scale = HEAD**-0.5
    queries = q_ref[0]
    outs = []
    for h, (q, own_grad) in enumerate(zip(head_parts(queries, lane, scale), head_parts(grad, lane))):
        log_total = l_ref[:, h * HEAD : h * HEAD + 1]
        probs = jnp.exp(mm(q, k, NT) + bias_ref[...].astype(F32) - log_total)
        prob_grad = mm(own_grad, v, NT)
        score_grad = probs * (prob_grad - jnp.sum(probs * prob_grad, axis=-1, keepdims=True))
        score_grad = score_grad.astype(LOW)
        outs.append(
            (mm(score_grad, k) * scale, mm(score_grad, queries, TN) * scale, mm(probs.astype(LOW), grad, TN))
        )
    for i in range(3):
        o_ref[i] = jnp.where(lane < HEAD, outs[0][i], outs[1][i]).astype(LOW)


def final_rows_kernel(own_ref, other_ref, o_ref):
    y = lax.axis_index("y")
    for place in range(2):

        @pl.when(y == place)
        def _(place=place):
            o_ref[:, place] = own_ref[...]
            o_ref[:, 1 - place] = other_ref[...]


def final_rows(own, other):
    total, width = own.shape
    block = pl.BlockSpec((ROWS_AT_ONCE, width), lambda i: (i, 0))
    both = pl.pallas_call(
        final_rows_kernel,
        grid=(pl.cdiv(total, ROWS_AT_ONCE),),
        in_specs=[block, block],
        out_specs=pl.BlockSpec((ROWS_AT_ONCE, 2, width), lambda i: (i, 0, 0)),
        out_shape=shaped((total, 2, width), own.dtype),
        compiler_params=params(60),
        name="final_rows",
    )(own, other)
    return both.transpose(1, 0, 2)


def attention_back(qkv, bias, logs, grad):
    total, width = grad.shape
    pairs = width // 128
    column = pl.BlockSpec((total, 128), lambda g: (0, g))
    return pl.pallas_call(
        attend_back_kernel,
        grid=(pairs,),
        in_specs=pair_specs(total, pairs // 2) + [full(bias.shape), column, column],
        out_specs=pl.BlockSpec((3, total, 128), lambda g: (0, 0, g)),
        out_shape=shaped((3, total, width), LOW),
        compiler_params=params(60),
        cost_estimate=cost(25 * 1.1e9, 25 * 2e6),
        name="attention_back",
    )(qkv, qkv, qkv, bias, logs, grad)


def qkv_back_kernel(per_side, x_ref, g_ref, r_ref, *refs):
    pieces, (own_ref, other_ref, o_ref, w, sem, acc) = refs[:10], refs[10:]
    j = pl.program_id(0)

    @pl.when(j == 0)
    def _():
        load_weights(pieces, w, sem, 0, g_ref.shape[2], per_side)

    grad = g_ref[0]
    share_out(mm(x_ref[...], grad, TN).astype(LOW), own_ref, other_ref)
    ready(w, sem, j)
    term = mm(grad, matrix(w, j), NT)

    @pl.when(j == 0)
    def _():
        acc[...] = r_ref[...] + term

    @pl.when(j > 0)
    def _():
        acc[...] += term

    @pl.when(j == 2 * per_side - 1)
    def _():
        o_ref[...] = acc[...].astype(LOW)


def qkv_back(x, grads, first_grad, pieces, rows):
    count, width = pieces[0].shape[0], STEP_WIDTH
    per_side = grads.shape[0]
    shape = first_grad.shape
    out_specs, out_shape = share_specs(count, rows, per_side, per_side * width)
    return pl.pallas_call(
        functools.partial(qkv_back_kernel, per_side),
        grid=(2 * per_side,),
        in_specs=[full(shape), pl.BlockSpec((1, shape[0], width), lambda j: (j % per_side, 0, j // per_side)), full(shape)]
        + [ANYWHERE] * 10,
        out_specs=out_specs + [full(shape)],
        out_shape=out_shape + [shaped(shape, LOW)],
        scratch_shapes=chunk_buffer((count, rows), 2 * per_side, width) + [pltpu.VMEM(shape, F32)],
        compiler_params=params(60),
        cost_estimate=cost(16 * 1.1e9, 16 * 2e6),
        name="qkv_back",
    )(x, grads, first_grad, *pieces)


def at(a, index, axis):
    return lax.dynamic_index_in_dim(a, index, axis, keepdims=False)


def chip_term(own, other, shift):
    x, y = place_xy(ring_place() + shift)
    return at(at(own, x, 0), y, 0).astype(F32) + at(at(other, x, 0), y, 0).astype(F32)


def ring_pair(to_right, to_left):
    return send(to_right, ("x", "y"), RING), send(to_left, ("x", "y"), RING_BACK)


def far_terms(take):
    far = take(2).astype(LOW)
    half = far.shape[0] // 2
    return far[:half], far[half:]


def near_terms(take, from_left, from_right):
    half = from_left.shape[0]
    right, left = take(1).astype(F32), take(-1).astype(F32)
    to_right = jnp.concatenate([right[:half] + from_left.astype(F32), right[half:]]).astype(LOW)
    to_left = jnp.concatenate([left[:half], left[half:] + from_right.astype(F32)]).astype(LOW)
    return to_right, to_left


def chip_terms(own, other):
    return lambda shift: chip_term(own, other, shift)


def square_terms(square):
    def take(shift):
        x, y = place_xy(ring_place() + shift)
        return at(at(square, x, 0), y, 0)

    return take


def line_terms(own, other, from_left, from_right):
    column = chip_term(own, other, 0) + from_left.astype(F32) + from_right.astype(F32)
    z = lax.axis_index("z")
    return [at(column, z, 0)] + [at(column, z ^ k, 0).astype(LOW) for k in range(1, column.shape[0])]


def line_send(terms):
    return [send(term, "z", partners(k + 1)) for k, term in enumerate(terms[1:])]


def total_of(own, others):
    for other in others:
        own = own + other.astype(F32)
    return own


def sum_over_all(value):
    value = value + send(value, "c", SWAP)
    square = [send(value, ("x", "y"), tuple((i, i ^ k) for i in range(4))) for k in (1, 2, 3)]
    value = (value + square[0]) + (square[1] + square[2])
    count, k = lax.axis_size("z"), 1
    while k < count:
        value = value + send(value, "z", tuple((i, i ^ k) for i in range(count)))
        k *= 2
    return value


def pad_rows(a, total):
    return jnp.pad(a, ((0, total - a.shape[0]), (0, 0)))


def mask_bias(doc_row, reset_row, live, total):
    kinds = jnp.concatenate([jnp.full((MEM,), -1, jnp.int32), doc_row, jnp.full((MEM,), -2, jnp.int32)])
    real = kinds.shape[0]
    kinds = jnp.pad(kinds, (0, total - real), constant_values=-3)
    place = jnp.arange(total, dtype=jnp.int32)
    choose = kinds[:, None] == jnp.arange(reset_row.shape[0], dtype=jnp.int32)[None, :]
    reset_query = jnp.sum(jnp.where(choose, reset_row[None, :], 0), axis=1)
    same = kinds[:, None] == kinds[None, :]
    live_key = place < jnp.minimum(live, MEM)
    token_sees = same | (live_key[None, :] & (reset_query == 0)[:, None])
    memory_sees = ((place >= MEM) | live_key)[None, :]
    sees = jnp.where((kinds < 0)[:, None], memory_sees, token_sees) & (place < real)[None, :]
    return jnp.where(sees, 0.0, MASKED).astype(LOW)


def whole_segment(
    tokens,
    cotangent,
    doc_ids,
    reset_flags,
    mem_live,
    qkv_weight,
    qkv_moment,
    qkv_square,
    qkv_average,
    out_weight,
    out_moment,
    out_square,
    out_average,
    up_weight,
    up_moment,
    up_square,
    up_average,
    down_weight,
    down_moment,
    down_square,
    down_average,
    norm_params,
    norm_moment,
    norm_square,
    norm_average,
):
    y = lax.axis_index("y")
    rows, inner_part = up_weight.shape
    count = lax.axis_size("z")
    width = tokens.shape[2]
    part = qkv_weight.shape[2]
    real = tokens.shape[1]
    total = -(-real // ROWS_AT_ONCE) * ROWS_AT_ONCE

    def mine(a):
        return lax.dynamic_index_in_dim(a, y, 0, keepdims=False)

    qkv_block = jnp.concatenate([qkv_weight[k] for k in range(3)], axis=1).astype(LOW)
    norm_block = jnp.pad(norm_params.astype(LOW), ((0, rows - 4), (0, 128 - rows)))
    second_block = jnp.concatenate([up_weight.astype(LOW), out_weight.T.astype(LOW), norm_block], axis=1)
    down_block = down_weight.T.astype(LOW)

    pair_down = join_pair(down_block, send(down_block, "y", SWAP), "y")
    qkv_block = after(qkv_block, down_block)
    tokens, cotangent, doc_ids = after((tokens, cotangent, doc_ids), pair_down)
    x = pad_rows(mine(tokens), total)
    cot = pad_rows(mine(cotangent), total)
    bias = mask_bias(mine(doc_ids), mine(reset_flags), mine(mem_live), total)

    z_qkv = line_pieces(qkv_block)
    other_pair = send(pair_down, "x", SWAP)
    z_second = line_pieces(after(second_block, *z_qkv))
    column_qkv = join_column(after(tuple(z_qkv), x, cot, bias, other_pair))
    square_down = join_pair(pair_down, other_pair, "x")
    near_qkv = ring_near(column_qkv)
    far_qkv = ring_far(*near_qkv)
    w_qkv = both_cores((column_qkv,) + near_qkv + far_qkv)
    column_second = after(join_column(z_second), *far_qkv)
    near_second = ring_near(column_second)
    square_down = after(square_down, column_second)
    down_one, down_two = send(square_down, "z", partners(1)), send(square_down, "z", partners(2))

    qkv = project(after(x, column_second), w_qkv, rows)
    context, logs = attention(qkv, bias)

    near_second = after(near_second, context)
    far_second = ring_far(*near_second)
    w_second = both_cores((column_second,) + near_second + far_second)
    down_two = after(down_two, near_second[0])
    down_three = send(down_two, "z", partners(1))

    hidden, normed, inverse, norms, active, slope = up(x, after(context, down_two), w_second, rows, inner_part)

    w_down = both_cores((square_down, down_one, down_two, after(down_three, active)))
    result, second_grad, feed_grad, norm_two = down(active, normed, norms, cot, w_down, rows)

    chunks = active.shape[0]
    own_down, other = weight_grad(
        feed_grad,
        active,
        pl.BlockSpec((1, total, STEP_WIDTH), lambda j: (j, 0, 0)),
        chunks,
        count,
        rows,
        "down_grad",
        lines_first=True,
    )
    z, place_x = lax.axis_index("z"), lax.axis_index("x")

    def pair(own, other):
        own, other = jnp.where(y == 0, own, other), jnp.where(y == 0, other, own)
        return jnp.stack([own, other], axis=1).transpose(1, 0, 2)

    def term(own, other):
        return lambda k: at(own, z ^ k, 0).astype(F32) + at(other, z ^ k, 0).astype(F32)

    other_down = send(other, "c", SWAP)
    down_term = term(own_down, other_down)
    crossing = down_term(3).astype(LOW)
    crossed = send(crossing, "z", partners(1))
    own_result = result[:real]
    shared_result = send(own_result, "y", SWAP)
    columns = inner_part + part + 128
    own, other, first_grad, branch_grad, norm_one = inner_back(
        after(feed_grad, crossing, own_result),
        slope,
        hidden,
        second_grad,
        normed,
        inverse,
        norms,
        w_down,
        w_second,
        rows,
        columns,
    )
    crossed, shared_result = after(crossed, branch_grad), after(shared_result, branch_grad)
    one, two = down_term(1).astype(LOW), (down_term(2) + crossed.astype(F32)).astype(LOW)
    from_one, from_two = send(one, "z", partners(1)), send(two, "z", partners(2))
    own_second, other, context_grad = out_back(
        after(branch_grad, one, two, shared_result),
        context,
        norm_one,
        norm_two,
        own,
        other,
        w_second,
        rows,
        inner_part,
    )
    other_second = send(other, "c", SWAP)
    take_second = chip_terms(own_second, other_second)
    far = far_terms(take_second)
    far_second = ring_pair(*far)
    grads = attention_back(qkv, bias, logs, after(context_grad, *far))

    far_second = after(far_second, grads)
    near = near_terms(take_second, *far_second)
    near_second = ring_pair(*near)
    from_one, from_two = after(from_one, *near), after(from_two, *near)
    square = down_term(0) + from_one.astype(F32) + from_two.astype(F32)
    to_x = at(square, 1 - place_x, 0).astype(LOW)
    own_qkv, other, own_grad = qkv_back(after(x, to_x), grads, first_grad, w_qkv, rows)
    near_second = after(near_second, own_qkv)
    from_x = send(after(to_x, *near_second), "x", SWAP)
    other_qkv = send(after(other, *near_second), "c", SWAP)
    shared_grad = send(after(own_grad[: total // 2], *near_second), "y", SWAP)
    column = chip_term(own_second, other_second, 0) + near_second[0].astype(F32) + near_second[1].astype(F32)
    crossing = at(column, z ^ 3, 0).astype(LOW)
    crossed = send(crossing, "z", partners(1))
    take_qkv = chip_terms(own_qkv, after(other_qkv, crossing))
    far = far_terms(take_qkv)
    far_qkv = ring_pair(*far)
    from_x, shared_grad = after(from_x, *far), after(shared_grad, *far)
    half = at(square, place_x, 0) + from_x.astype(F32)
    to_y = at(half, 1 - y, 0).astype(LOW)
    crossed = after(crossed, *far)
    one, two = at(column, z ^ 1, 0).astype(LOW), (at(column, z ^ 2, 0) + crossed.astype(F32)).astype(LOW)
    from_one, from_two = send(one, "z", partners(1)), send(two, "z", partners(2))
    far_qkv = after(far_qkv, one, two, to_y, shared_grad)
    near = near_terms(take_qkv, *far_qkv)
    near_qkv = ring_pair(*near)
    output = final_rows(own_result, after(shared_result, *near))
    near_qkv = after(near_qkv, output)
    from_one, from_two = after(from_one, *near), after(from_two, *near)
    second_sum = at(column, z, 0) + from_one.astype(F32) + from_two.astype(F32)
    line_qkv = line_terms(own_qkv, other_qkv, *after(near_qkv, second_sum))
    others_qkv = line_send(line_qkv)
    from_y = send(after(to_y, *line_qkv), "y", SWAP)
    last_rows = after(own_grad[total // 2 : real], *line_qkv)
    shared_grad = jnp.concatenate([shared_grad, send(last_rows, "y", SWAP)])
    down_sum = at(half, y, 0) + from_y.astype(F32)
    others_qkv = after(tuple(others_qkv), down_sum, shared_grad)
    input_grad = pair(own_grad[:real], shared_grad).astype(F32)
    qkv_sum = total_of(line_qkv[0], others_qkv)

    qkv_sum = qkv_sum.reshape(rows, 3, part).transpose(1, 0, 2)
    up_sum = second_sum[:, :inner_part]
    out_sum = second_sum[:, inner_part : inner_part + part].T
    norm_sum = second_sum[:4, inner_part + part : inner_part + part + rows]
    down_sum = down_sum.T
    local_squares = (
        jnp.sum(qkv_sum * qkv_sum)
        + jnp.sum(out_sum * out_sum)
        + jnp.sum(up_sum * up_sum)
        + jnp.sum(down_sum * down_sum)
        + jnp.sum(norm_sum * norm_sum) / lax.axis_size("y")
    )
    grad_norm = jnp.sqrt(sum_over_all(jnp.full((8, 128), local_squares))[0, 0])
    threshold = math.sqrt(4 * D * D + 2 * D * FF + 4 * D)
    factor = jnp.minimum(1.0, threshold / (grad_norm + 1e-06))
    new_qkv = adam_step(qkv_weight, qkv_moment, qkv_square, qkv_average, qkv_sum * factor, 0.02, 0.01)
    new_out = adam_step(out_weight, out_moment, out_square, out_average, out_sum * factor, 0.06, 0.01)
    new_up = adam_step(up_weight, up_moment, up_square, up_average, up_sum * factor, 0.02, 0.01)
    new_down = adam_step(down_weight, down_moment, down_square, down_average, down_sum * factor, 0.02, 0.01)
    new_norm = adam_step(norm_params, norm_moment, norm_square, norm_average, norm_sum * factor, 0.4, 0.0)
    return (output, input_grad, grad_norm) + new_qkv + new_out + new_up + new_down + new_norm


def solution(mesh):
    wide, narrow = mesh.shape["wide"], mesh.shape["narrow"]

    def placed(w, n):
        state = [P(None, w, n)] * 4 + [P(n, w)] * 4 + [P(w, n)] * 4 + [P(n, w)] * 4 + [P(None, w)] * 4
        return (
            tuple([P(w, None, None)] * 2 + [P(w, None)] * 2 + [P(w)] + state),
            tuple([P(w, None, None)] * 2 + [P()] + state),
        )

    def run(*args):
        if narrow == 2 and wide == 16 and args[0].shape[0] == wide * narrow:
            body = whole_segment
            grid = jax.sharding.Mesh(mesh.devices.reshape(wide // 4, 2, 2, 2), ("z", "x", "c", "y"))
            ins, outs = placed(("z", "x", "c"), "y")
        else:
            body, grid = shared_rows, mesh
            ins, outs = placed("wide", "narrow")
        return jax.shard_map(body, mesh=grid, in_specs=ins, out_specs=outs, check_vma=False)(*args)

    return run
```

```python
import functools
import math

import jax
import jax.numpy as jnp
from jax import lax
from jax.experimental import pallas as pl
from jax.experimental.pallas import tpu as pltpu
from jax.sharding import PartitionSpec as P

D = 1024
HEAD = 64
FF = 4096
MEM = 10
STEP = 10


NORM_EPS = 1e-12
BETA_ONE = 0.9
BETA_TWO = 0.98
ADAM_EPS = 1e-06
AVERAGE_KEEP = 0.75
MASKED = -1e30


def allowed_mask(doc_row, reset_row, live_count):
    rows_all = doc_row.shape[0] + 2 * MEM
    kinds = jnp.concatenate(
        [jnp.full((MEM,), -1, jnp.int32), doc_row, jnp.full((MEM,), -2, jnp.int32)]
    )
    place = jnp.arange(rows_all, dtype=jnp.int32)
    read_key = place < MEM
    live_key = place < live_count
    choose = kinds[:, None] == jnp.arange(reset_row.shape[0], dtype=jnp.int32)[None, :]
    reset_query = jnp.sum(jnp.where(choose, reset_row[None, :], 0), axis=1)
    memory_query = kinds < 0
    same_doc = kinds[:, None] == kinds[None, :]
    token_sees = same_doc | (read_key & live_key)[None, :] & (reset_query == 0)[:, None]
    memory_sees = jnp.broadcast_to((~read_key | live_key)[None, :], (rows_all, rows_all))
    return jnp.where(memory_query[:, None], memory_sees, token_sees)


def norm_forward(rows_in, gain, shift):
    center = rows_in - jnp.mean(rows_in, axis=-1, keepdims=True)
    inverse = lax.rsqrt(jnp.mean(center * center, axis=-1, keepdims=True) + NORM_EPS)
    normed = center * inverse
    return (normed * gain + shift, normed, inverse)


def norm_backward(grad, normed, inverse, gain):
    scaled = grad * gain
    back = inverse * (
        scaled
        - jnp.mean(scaled, axis=-1, keepdims=True)
        - normed * jnp.mean(scaled * normed, axis=-1, keepdims=True)
    )
    return (back, jnp.stack([jnp.sum(grad * normed, axis=0), jnp.sum(grad, axis=0)]))


def masked_scores(query, keys, allowed):
    scores = jnp.einsum("qhd,khd->hqk", query, keys, preferred_element_type=jnp.float32) * (
        1.0 / math.sqrt(HEAD)
    )
    return jnp.where(allowed[None], scores, MASKED)


def attend(inputs):
    query, keys, values, allowed = inputs
    scores = masked_scores(query, keys, allowed)
    row_top = jnp.max(scores, axis=-1, keepdims=True)
    expo = jnp.exp(scores - row_top)
    row_total = jnp.sum(expo, axis=-1, keepdims=True)
    probs = (expo / row_total).astype(jnp.bfloat16)
    context = jnp.einsum("hqk,khd->qhd", probs, values, preferred_element_type=jnp.float32)
    return (context.astype(jnp.bfloat16), row_top + jnp.log(row_total))


def attend_back(inputs):
    query, keys, values, allowed, log_total, context_grad = inputs
    probs = jnp.exp(masked_scores(query, keys, allowed) - log_total)
    value_grad = jnp.einsum(
        "hqk,qhd->khd", probs.astype(jnp.bfloat16), context_grad, preferred_element_type=jnp.float32
    )
    prob_grad = jnp.einsum("qhd,khd->hqk", context_grad, values, preferred_element_type=jnp.float32)
    score_grad = probs * (prob_grad - jnp.sum(probs * prob_grad, axis=-1, keepdims=True))
    score_grad = score_grad.astype(jnp.bfloat16)
    scale_now = 1.0 / math.sqrt(HEAD)
    query_grad = (
        jnp.einsum("hqk,khd->qhd", score_grad, keys, preferred_element_type=jnp.float32) * scale_now
    )
    key_grad = (
        jnp.einsum("hqk,qhd->khd", score_grad, query, preferred_element_type=jnp.float32)
        * scale_now
    )
    return (
        query_grad.astype(jnp.bfloat16),
        key_grad.astype(jnp.bfloat16),
        value_grad.astype(jnp.bfloat16),
    )


def adam_step(weight, moment, square, average, grad, rate, decay):
    moment = BETA_ONE * moment + (1.0 - BETA_ONE) * grad
    square = BETA_TWO * square + (1.0 - BETA_TWO) * grad * grad
    first_hat = moment / (1.0 - BETA_ONE**STEP)
    second_hat = square / (1.0 - BETA_TWO**STEP)
    weight = weight - rate * (first_hat / (jnp.sqrt(second_hat) + ADAM_EPS) + decay * weight)
    average = AVERAGE_KEEP * average + (1.0 - AVERAGE_KEEP) * weight
    return (weight, moment, square, average)


def row_scatter(terms):
    return lax.psum_scatter(terms, "narrow", scatter_dimension=0, tiled=True)


def row_gather(piece):
    return lax.all_gather(piece, "narrow", axis=0, tiled=True)


def narrow_norm(grads):
    return lax.psum(grads, "narrow")


def shared_rows(
    tokens,
    cotangent,
    doc_ids,
    reset_flags,
    mem_live,
    qkv_weight,
    qkv_moment,
    qkv_square,
    qkv_average,
    out_weight,
    out_moment,
    out_square,
    out_average,
    up_weight,
    up_moment,
    up_square,
    up_average,
    down_weight,
    down_moment,
    down_square,
    down_average,
    norm_params,
    norm_moment,
    norm_square,
    norm_average,
):
    narrow_count = lax.axis_size("narrow")
    seg_count, rows_all, width = tokens.shape
    w_qkv, w_out, w_up, w_down, norms_low = (
        lax.all_gather(qkv_weight.astype(jnp.bfloat16), "wide", axis=1, tiled=True),
        lax.all_gather(out_weight.astype(jnp.bfloat16), "wide", axis=1, tiled=True),
        lax.all_gather(up_weight.astype(jnp.bfloat16), "wide", axis=0, tiled=True),
        lax.all_gather(down_weight.astype(jnp.bfloat16), "wide", axis=1, tiled=True),
        lax.all_gather(norm_params.astype(jnp.bfloat16), "wide", axis=1, tiled=True),
    )
    norms = norms_low.astype(jnp.float32)
    local_cols = w_qkv.shape[2]
    local_heads = local_cols // HEAD
    total_rows = seg_count * rows_all
    flat_in = tokens.reshape(total_rows, width)
    flat_cot = cotangent.reshape(total_rows, width)
    allowed = jax.vmap(allowed_mask)(doc_ids, reset_flags, mem_live)
    projected = jnp.einsum(
        "md,kdc->kmc", flat_in, w_qkv, preferred_element_type=jnp.float32
    ).astype(jnp.bfloat16)
    split_heads = projected.reshape(3, seg_count, rows_all, local_heads, HEAD)
    query, keys, values = (split_heads[0], split_heads[1], split_heads[2])
    context, log_total = lax.map(attend, (query, keys, values, allowed))
    context_flat = context.reshape(total_rows, local_cols)
    attention_terms = jnp.dot(context_flat, w_out, preferred_element_type=jnp.float32)
    share = total_rows // narrow_count
    row_start = lax.axis_index("narrow") * share
    own_in = lax.dynamic_slice_in_dim(flat_in, row_start, share, 0)
    own_cot = lax.dynamic_slice_in_dim(flat_cot, row_start, share, 0)
    first_sum = own_in.astype(jnp.float32) + row_scatter(attention_terms)
    hidden, normed_one, inverse_one = norm_forward(first_sum, norms[0], norms[1])
    hidden_low = row_gather(hidden.astype(jnp.bfloat16))
    inner = jnp.dot(hidden_low, w_up, preferred_element_type=jnp.float32)
    active, gelu_pull = jax.vjp(lambda value_in: jax.nn.gelu(value_in, approximate=False), inner)
    active_low = active.astype(jnp.bfloat16)
    feed_terms = jnp.dot(active_low, w_down, preferred_element_type=jnp.float32)
    feed = row_scatter(feed_terms)
    second_sum = hidden + feed
    result, normed_two, inverse_two = norm_forward(second_sum, norms[2], norms[3])
    result_low = result.astype(jnp.bfloat16)
    second_grad, norm_two_grads = norm_backward(
        own_cot.astype(jnp.float32), normed_two, inverse_two, norms[2]
    )
    norm_two_grads = narrow_norm(norm_two_grads)
    output = row_gather(result_low)
    feed_grad = row_gather(second_grad.astype(jnp.bfloat16))
    output = output.reshape(seg_count, rows_all, width)
    down_grad = jnp.einsum("mf,md->fd", active_low, feed_grad, preferred_element_type=jnp.float32)
    active_grad = jnp.einsum("md,fd->mf", feed_grad, w_down, preferred_element_type=jnp.float32)
    inner_grad = gelu_pull(active_grad)[0].astype(jnp.bfloat16)
    up_grad = jnp.einsum("md,mf->df", hidden_low, inner_grad, preferred_element_type=jnp.float32)
    hidden_terms = jnp.einsum("mf,df->md", inner_grad, w_up, preferred_element_type=jnp.float32)
    hidden_grad = second_grad + row_scatter(hidden_terms)
    first_grad, norm_one_grads = norm_backward(hidden_grad, normed_one, inverse_one, norms[0])
    norm_one_grads = narrow_norm(norm_one_grads)
    branch_grad = row_gather(first_grad.astype(jnp.bfloat16))
    out_grad_weight = jnp.einsum(
        "mc,md->cd", context_flat, branch_grad, preferred_element_type=jnp.float32
    )
    context_grad = jnp.einsum(
        "md,cd->mc", branch_grad, w_out, preferred_element_type=jnp.float32
    ).astype(jnp.bfloat16)
    context_grad = context_grad.reshape(seg_count, rows_all, local_heads, HEAD)
    query_grad, key_grad, value_grad = lax.map(
        attend_back, (query, keys, values, allowed, log_total, context_grad)
    )
    stacked_grad = jnp.stack([query_grad, key_grad, value_grad]).reshape(3, total_rows, local_cols)
    qkv_grad = jnp.einsum("md,kmc->kdc", flat_in, stacked_grad, preferred_element_type=jnp.float32)
    input_terms = jnp.einsum("kmc,kdc->md", stacked_grad, w_qkv, preferred_element_type=jnp.float32)
    input_grad = lax.all_gather(first_grad + row_scatter(input_terms), "narrow", axis=0, tiled=True)
    input_grad = input_grad.reshape(seg_count, rows_all, width)
    norm_grads = jnp.concatenate([norm_one_grads, norm_two_grads], axis=0)
    qkv_sum, out_sum, up_sum, down_sum, norm_sum = (
        lax.psum_scatter(qkv_grad, "wide", scatter_dimension=1, tiled=True),
        lax.psum_scatter(out_grad_weight, "wide", scatter_dimension=1, tiled=True),
        lax.psum_scatter(up_grad, "wide", scatter_dimension=0, tiled=True),
        lax.psum_scatter(down_grad, "wide", scatter_dimension=1, tiled=True),
        lax.psum_scatter(norm_grads, "wide", scatter_dimension=1, tiled=True),
    )
    local_squares = (
        jnp.sum(qkv_sum * qkv_sum)
        + jnp.sum(out_sum * out_sum)
        + jnp.sum(up_sum * up_sum)
        + jnp.sum(down_sum * down_sum)
        + jnp.sum(norm_sum * norm_sum) / narrow_count
    )
    grad_norm = jnp.sqrt(lax.psum(local_squares, ("wide", "narrow")))
    threshold = math.sqrt(4 * D * D + 2 * D * FF + 4 * D)
    factor = jnp.minimum(1.0, threshold / (grad_norm + 1e-06))
    new_qkv = adam_step(
        qkv_weight, qkv_moment, qkv_square, qkv_average, qkv_sum * factor, 0.02, 0.01
    )
    new_out = adam_step(
        out_weight, out_moment, out_square, out_average, out_sum * factor, 0.06, 0.01
    )
    new_up = adam_step(up_weight, up_moment, up_square, up_average, up_sum * factor, 0.02, 0.01)
    new_down = adam_step(
        down_weight, down_moment, down_square, down_average, down_sum * factor, 0.02, 0.01
    )
    new_norm = adam_step(
        norm_params, norm_moment, norm_square, norm_average, norm_sum * factor, 0.4, 0.0
    )
    return (
        output,
        input_grad,
        grad_norm,
        new_qkv[0],
        new_qkv[1],
        new_qkv[2],
        new_qkv[3],
        new_out[0],
        new_out[1],
        new_out[2],
        new_out[3],
        new_up[0],
        new_up[1],
        new_up[2],
        new_up[3],
        new_down[0],
        new_down[1],
        new_down[2],
        new_down[3],
        new_norm[0],
        new_norm[1],
        new_norm[2],
        new_norm[3],
    )


SWAP = ((0, 1), (1, 0))
RING = ((0, 1), (1, 3), (3, 2), (2, 0))
RING_BACK = tuple((b, a) for a, b in RING)


def send(block, axes, pairs):
    return lax.ppermute(block, axes, list(pairs))


def ring_place():
    x, y = lax.axis_index("x"), lax.axis_index("y")
    return jnp.where(x == 0, y, 3 - y)


def place_xy(place):
    place = lax.rem(place + 4, 4)
    x = place // 2
    return x, jnp.where(x == 0, place, 3 - place)


def ring_near(block):
    return send(block, ("x", "y"), RING), send(block, ("x", "y"), RING_BACK)


def ring_far(left, right):
    half = left.shape[0] // 2
    return send(left[:half], ("x", "y"), RING), send(right[half:], ("x", "y"), RING_BACK)


def after(value, *others):
    return lax.optimization_barrier((value,) + others)[0]


STEP_WIDTH = 512
RING_SHIFTS = (0, -1, 1, 2, 2)
NT = (((1,), (1,)), ((), ()))
TN = (((0,), (0,)), ((), ()))
NN = (((1,), (0,)), ((), ()))
F32, LOW = jnp.float32, jnp.bfloat16
ANYWHERE = pl.BlockSpec(memory_space=pltpu.HBM)


def params(mib):
    return pltpu.CompilerParams(vmem_limit_bytes=mib << 20)


def cost(flops, moved):
    return pl.CostEstimate(flops=int(flops), bytes_accessed=int(moved), transcendentals=0)


def shaped(shape, dtype):
    return jax.ShapeDtypeStruct(shape, dtype)


def full(shape):
    return pl.BlockSpec(shape, lambda *_: (0,) * len(shape))


def mm(a, b, dims=NN):
    return lax.dot_general(a, b, dims, preferred_element_type=F32)


def join_column_kernel(count, *refs):
    out, sem = refs[-2:]
    z = lax.axis_index("z")
    copies = [pltpu.make_async_copy(ref, out.at[z ^ k], sem.at[k]) for k, ref in enumerate(refs[:count])]
    for copy in copies:
        copy.start()
    for copy in copies:
        copy.wait()


def partners(k):
    return tuple((i, i ^ k) for i in range(lax.axis_size("z")))


def line_pieces(block):
    return [block] + [send(block, "z", partners(k)) for k in range(1, lax.axis_size("z"))]


def join_column(pieces):
    count = len(pieces)
    shape = (count,) + pieces[0].shape
    return pl.pallas_call(
        functools.partial(join_column_kernel, count),
        in_specs=[ANYWHERE] * count,
        out_specs=pl.BlockSpec(memory_space=pltpu.VMEM),
        out_shape=shaped(shape, pieces[0].dtype),
        scratch_shapes=[pltpu.SemaphoreType.DMA((count,))],
        compiler_params=params(60),
        name="join_column",
    )(*pieces)


def join_pair_kernel(axis, own, other, out, sem):
    place = lax.axis_index(axis)
    copies = [pltpu.make_async_copy(own, out.at[place], sem.at[0])]
    copies.append(pltpu.make_async_copy(other, out.at[1 - place], sem.at[1]))
    for copy in copies:
        copy.start()
    for copy in copies:
        copy.wait()


def join_pair(own, other, axis):
    return pl.pallas_call(
        functools.partial(join_pair_kernel, axis),
        in_specs=[ANYWHERE] * 2,
        out_specs=pl.BlockSpec(memory_space=pltpu.VMEM),
        out_shape=shaped((2,) + own.shape, own.dtype),
        scratch_shapes=[pltpu.SemaphoreType.DMA((2,))],
        compiler_params=params(60),
        name="join_pair",
    )(own, other)


def both_cores(pieces):
    return list(pieces) + [send(p, "c", SWAP) for p in pieces]


def load_weights(pieces, w, sem, column, width, per_side):
    place, core = ring_place(), lax.axis_index("c")
    rows = w.shape[4]
    for k in range(per_side):
        for group, core_at in ((pieces[:5], core), (pieces[5:], 1 - core)):
            for i, (ref, shift) in enumerate(zip(group, RING_SHIFTS)):
                x, y = place_xy(place + shift)
                chunk = y * per_side + k
                first = ref.shape[0] if i == 4 else 0
                pltpu.make_async_copy(
                    ref.at[:, pl.ds(0, rows), pl.ds(column + k * width, width)],
                    w.at[chunk, pl.ds(first, ref.shape[0]), x, core_at],
                    sem.at[chunk],
                ).start()


def load_lines(pieces, w, sem, width, per_side):
    z, core = lax.axis_index("z"), lax.axis_index("c")
    count = len(pieces) // 2
    for k in range(per_side):
        for group, core_at in ((pieces[:count], core), (pieces[count:], 1 - core)):
            for i, ref in enumerate(group):
                for y in range(2):
                    chunk = y * per_side + k
                    pltpu.make_async_copy(
                        ref.at[:, y, :, pl.ds(k * width, width)], w.at[chunk, z ^ i, :, core_at], sem.at[chunk]
                    ).start()


def ready(w, sem, chunk):
    pltpu.make_async_copy(w.at[chunk], w.at[chunk], sem.at[chunk]).wait()


def matrix(w, chunk):
    block = w[chunk]
    return block.reshape(-1, block.shape[-1])


def chunk_buffer(shapes, chunks, width):
    z, rows = shapes
    return [pltpu.VMEM((chunks, z, 2, 2, rows, width), LOW), pltpu.SemaphoreType.DMA((chunks,))]


def alternate(per_side):
    return lambda j: (j % 2) * per_side + j // 2


def project_kernel(per_side, x_ref, *refs):
    pieces, (o_ref, w, sem) = refs[:10], refs[10:]
    j = pl.program_id(0)

    @pl.when(j == 0)
    def _():
        load_weights(pieces, w, sem, 0, o_ref.shape[2], per_side)

    chunk = alternate(per_side)(j)
    ready(w, sem, chunk)
    o_ref[0] = mm(x_ref[...], matrix(w, chunk)).astype(LOW)


def project(x, pieces, rows):
    count, width = pieces[0].shape[0], STEP_WIDTH
    per_side = pieces[0].shape[2] // width
    at = alternate(per_side)
    return pl.pallas_call(
        functools.partial(project_kernel, per_side),
        grid=(2 * per_side,),
        in_specs=[full(x.shape)] + [ANYWHERE] * 10,
        out_specs=pl.BlockSpec((1, x.shape[0], width), lambda j: (at(j), 0, 0)),
        out_shape=shaped((2 * per_side, x.shape[0], width), LOW),
        scratch_shapes=chunk_buffer((count, rows), 2 * per_side, width),
        compiler_params=params(60),
        cost_estimate=cost(6 * 1.1e9, 6 * 2e6),
        name="project",
    )(x, *pieces)


def head_parts(a, lane, scale=None):
    a = a if scale is None else a * jnp.asarray(scale, a.dtype)
    none = jnp.zeros_like(a)
    return jnp.where(lane < HEAD, a, none), jnp.where(lane < HEAD, none, a)


def attend_kernel(q_ref, k_ref, v_ref, bias_ref, o_ref, l_ref):
    k, v = k_ref[0], v_ref[0]
    lane = lax.broadcasted_iota(jnp.int32, k.shape, 1)
    outs, logs = [], []
    for q in head_parts(q_ref[0], lane, HEAD**-0.5):
        scores = mm(q, k, NT) + bias_ref[...].astype(F32)
        top = jnp.max(scores, axis=-1, keepdims=True)
        expo = jnp.exp(scores - top)
        total = jnp.sum(expo, axis=-1, keepdims=True)
        outs.append(mm((expo * (1.0 / total)).astype(LOW), v))
        logs.append(top + jnp.log(total))
    o_ref[...] = jnp.where(lane < HEAD, outs[0], outs[1]).astype(LOW)
    l_ref[...] = jnp.where(lane < HEAD, logs[0], logs[1])


def pair_specs(total, per_side):
    def spec(k):
        return pl.BlockSpec((1, total, 128), lambda g: ((g // per_side) * 3 + k, 0, g % per_side))

    return [spec(k) for k in range(3)]


def attention(qkv, bias):
    total, width = qkv.shape[1], qkv.shape[2] * 2
    pairs = width // 128
    return pl.pallas_call(
        attend_kernel,
        grid=(pairs,),
        in_specs=pair_specs(total, pairs // 2) + [full(bias.shape)],
        out_specs=[pl.BlockSpec((total, 128), lambda g: (0, g))] * 2,
        out_shape=[shaped((total, width), LOW), shaped((total, width), F32)],
        compiler_params=params(60),
        cost_estimate=cost(17 * 1.1e9, 17 * 2e6),
        name="attention",
    )(qkv, qkv, qkv, bias)


ROWS_AT_ONCE = 32


def by_rows(total, body, carry=0):
    def step(i, held):
        return body(pl.ds(pl.multiple_of(i * ROWS_AT_ONCE, ROWS_AT_ONCE), ROWS_AT_ONCE), held)

    return lax.fori_loop(0, total // ROWS_AT_ONCE, step, carry, unroll=True)


def normalize(v):
    center = v - jnp.mean(v, axis=-1, keepdims=True)
    inverse = lax.rsqrt(jnp.mean(center * center, axis=-1, keepdims=True) + NORM_EPS)
    return center * inverse, inverse


def unnormalize(scaled, normed, inverse):
    return inverse * (
        scaled
        - jnp.mean(scaled, axis=-1, keepdims=True)
        - normed * jnp.mean(scaled * normed, axis=-1, keepdims=True)
    )


def fold(a):
    return jnp.sum(a.reshape(-1, 8, a.shape[-1]), axis=0)


def gelu_parts(u):
    phi = 0.5 + 0.5 * lax.erf(u * math.sqrt(0.5))
    return u * phi, phi + u * (jnp.exp(-0.5 * (u * u)) * (1.0 / math.sqrt(2.0 * math.pi)))


def up_kernel(per_side, x_ref, ctx_ref, *refs):
    pieces = refs[:10]
    h_ref, n_ref, i_ref, norms_ref, g_ref, d_ref, wu, us, wo, os, nw, ns, acc = refs[10:]
    j = pl.program_id(0)
    width = g_ref.shape[2]

    @pl.when(j == 0)
    def _():
        first = 2 * per_side // 2 * width
        load_weights(pieces, nw, ns, first + width, 128, 1)
        load_weights(pieces, wo, os, first, width, 1)
        load_weights(pieces, wu, us, 0, width, per_side)
        ready(nw, ns, 0)
        ready(nw, ns, 1)
        cells = nw[0].reshape(-1, nw.shape[4], 128).astype(F32)
        side = x_ref.shape[1] // cells.shape[0]
        norms_ref[...] = jnp.concatenate([cells[i, :8, :side] for i in range(cells.shape[0])], axis=1)
        ready(wo, os, 0)
        acc[...] = mm(ctx_ref[:, :width], matrix(wo, 0), NT)
        ready(wo, os, 1)
        acc[...] += mm(ctx_ref[:, width:], matrix(wo, 1), NT)
        gain, shift = norms_ref[0:1], norms_ref[1:2]

        def rows(r, held):
            normed, inverse = normalize(x_ref[r].astype(F32) + acc[r])
            n_ref[r] = normed
            i_ref[r] = jnp.broadcast_to(inverse, (ROWS_AT_ONCE, 128))
            h_ref[r] = (normed * gain + shift).astype(LOW)
            return held

        by_rows(x_ref.shape[0], rows)

    chunk = alternate(per_side)(j)
    ready(wu, us, chunk)
    active, slope = gelu_parts(mm(h_ref[...], matrix(wu, chunk)))
    g_ref[0] = active.astype(LOW)
    d_ref[0] = slope.astype(LOW)


def up(x, context, pieces, rows, inner_part):
    count, width = pieces[0].shape[0], STEP_WIDTH
    per_side = inner_part // width
    at = alternate(per_side)
    total, model = x.shape
    chunks = pl.BlockSpec((1, total, width), lambda j: (at(j), 0, 0))
    return pl.pallas_call(
        functools.partial(up_kernel, per_side),
        grid=(2 * per_side,),
        in_specs=[full(x.shape)] * 2 + [ANYWHERE] * 10,
        out_specs=[full(x.shape), full(x.shape), full((total, 128)), full((8, model)), chunks, chunks],
        out_shape=[
            shaped(x.shape, LOW),
            shaped(x.shape, F32),
            shaped((total, 128), F32),
            shaped((8, model), F32),
            shaped((2 * per_side, total, width), LOW),
            shaped((2 * per_side, total, width), LOW),
        ],
        scratch_shapes=chunk_buffer((count, rows), 2 * per_side, width)
        + chunk_buffer((count, rows), 2, width)
        + chunk_buffer((count, 16), 2, 128)
        + [pltpu.VMEM(x.shape, F32)],
        compiler_params=params(60),
        cost_estimate=cost(22 * 1.1e9, 22 * 2e6),
        name="up",
    )(x, context, *pieces)


def down_kernel(per_side, pieces_count, g_ref, n_ref, norms_ref, cot_ref, *refs):
    pieces = refs[:pieces_count]
    o_ref, d_ref, f_ref, ng_ref, w, sem, acc = refs[pieces_count:]
    j = pl.program_id(0)

    @pl.when(j == 0)
    def _():
        load_lines(pieces, w, sem, g_ref.shape[2], per_side)
        acc[...] = jnp.zeros_like(acc)

    chunk = alternate(per_side)(j)
    ready(w, sem, chunk)
    acc[...] += mm(g_ref[0], matrix(w, chunk), NT)

    @pl.when(j == 2 * per_side - 1)
    def _():
        gain_one, shift_one, gain, shift = (norms_ref[i : i + 1] for i in range(4))

        def rows(r, held):
            normed, inverse = normalize(n_ref[r] * gain_one + shift_one + acc[r])
            o_ref[r] = (normed * gain + shift).astype(LOW)
            dy = cot_ref[r].astype(F32)
            back = unnormalize(dy * gain, normed, inverse)
            d_ref[r] = back
            f_ref[r] = back.astype(LOW)
            return held[0] + fold(dy * normed), held[1] + fold(dy)

        none = jnp.zeros((8, acc.shape[1]), F32)
        gains, shifts = by_rows(acc.shape[0], rows, (none, none))
        ng_ref[...] = jnp.concatenate(
            [jnp.sum(gains, axis=0, keepdims=True), jnp.sum(shifts, axis=0, keepdims=True), none[:6]], axis=0
        )


def down(active, normed, norms, cot, pieces, rows):
    width = STEP_WIDTH
    chunks, total = active.shape[0], active.shape[1]
    at = alternate(chunks // 2)
    shape = normed.shape
    count = len(pieces) // 2
    return pl.pallas_call(
        functools.partial(down_kernel, chunks // 2, len(pieces)),
        grid=(chunks,),
        in_specs=[pl.BlockSpec((1, total, width), lambda j: (at(j), 0, 0)), full(shape), full(norms.shape), full(shape)]
        + [ANYWHERE] * len(pieces),
        out_specs=[full(shape), full(shape), full(shape), full(norms.shape)],
        out_shape=[shaped(shape, LOW), shaped(shape, F32), shaped(shape, LOW), shaped(norms.shape, F32)],
        scratch_shapes=chunk_buffer((count, rows), chunks, width) + [pltpu.VMEM(shape, F32)],
        compiler_params=params(60),
        cost_estimate=cost(17 * 1.1e9, 17 * 2e6),
        name="down",
    )(active, normed, norms, cot, *pieces)


def share_out(value, own_ref, other_ref, lines_first=False):
    core = lax.axis_index("c")
    if lines_first:
        z, x, _, rows, width = own_ref.shape
        value = value.reshape(z, x, 2, rows, width)
        for parity in range(2):

            @pl.when(core == parity)
            def _(parity=parity):
                own_ref[:, :, 0] = value[:, :, parity]

            @pl.when(core != parity)
            def _(parity=parity):
                other_ref[:, :, 0] = value[:, :, parity]

        return
    squares, _, z, rows, width = own_ref.shape
    value = value.reshape(z, squares, 2, rows, width)
    for parity in range(2):

        @pl.when(core == parity)
        def _(parity=parity):
            for x in range(squares):
                own_ref[x, 0] = value[:, x, parity]

        @pl.when(core != parity)
        def _(parity=parity):
            for x in range(squares):
                other_ref[x, 0] = value[:, x, parity]


def share_specs(count, rows, per_side, columns):
    spec = pl.BlockSpec((2, 1, count, rows, STEP_WIDTH), lambda j: (0, j // per_side, 0, 0, j % per_side))
    return [spec] * 2, [shaped((2, 2, count, rows, columns), LOW)] * 2


def weight_grad_kernel(lines_first, a_ref, b_ref, own_ref, other_ref):
    share_out(mm(a_ref[...], b_ref[0], TN).astype(LOW), own_ref, other_ref, lines_first)


def weight_grad(a, b, spec, chunks, count, rows, name, lines_first=False):
    per_side = chunks // 2
    out_specs, out_shape = share_specs(count, rows, per_side, per_side * STEP_WIDTH)
    if lines_first:
        spec_out = pl.BlockSpec((count, 2, 1, rows, STEP_WIDTH), lambda j: (0, 0, j // per_side, 0, j % per_side))
        out_specs, out_shape = [spec_out] * 2, [shaped((count, 2, 2, rows, per_side * STEP_WIDTH), LOW)] * 2
    return pl.pallas_call(
        functools.partial(weight_grad_kernel, lines_first),
        grid=(chunks,),
        in_specs=[full(a.shape), spec],
        out_specs=out_specs,
        out_shape=out_shape,
        compiler_params=params(60),
        cost_estimate=cost(9 * 1.1e9, 9 * 2e6),
        name=name,
    )(a, b)


def inner_kernel(per_side, down_count, f_ref, d_ref, h_ref, r_ref, n_ref, i_ref, norms_ref, *refs):
    downs, ups = refs[:down_count], refs[down_count : down_count + 10]
    own_ref, other_ref, g_ref, a_ref, ng_ref, wd, ds, wu, us, acc = refs[down_count + 10 :]
    j = pl.program_id(0)
    width = d_ref.shape[2]

    @pl.when(j == 0)
    def _():
        load_lines(downs, wd, ds, width, per_side)
        load_weights(ups, wu, us, 0, width, per_side)
        acc[...] = r_ref[...]

    ready(wd, ds, j)
    grad = (mm(f_ref[...], matrix(wd, j)) * d_ref[0].astype(F32)).astype(LOW)
    share_out(mm(h_ref[...], grad, TN).astype(LOW), own_ref, other_ref)
    ready(wu, us, j)
    acc[...] += mm(grad, matrix(wu, j), NT)

    @pl.when(j == 2 * per_side - 1)
    def _():
        gain = norms_ref[0:1]

        def rows(r, held):
            dy, normed = acc[r], n_ref[r]
            back = unnormalize(dy * gain, normed, i_ref[r][:, :1])
            g_ref[r] = back
            a_ref[r] = back.astype(LOW)
            return held[0] + fold(dy * normed), held[1] + fold(dy)

        none = jnp.zeros((8, acc.shape[1]), F32)
        gains, shifts = by_rows(acc.shape[0], rows, (none, none))
        ng_ref[...] = jnp.concatenate(
            [jnp.sum(gains, axis=0, keepdims=True), jnp.sum(shifts, axis=0, keepdims=True), none[:6]], axis=0
        )


def inner_back(feed_grad, slope, hidden, second_grad, normed, inverse, norms, downs, ups, rows, columns):
    chunks, total, width = slope.shape
    shape = normed.shape
    count = ups[0].shape[0]
    out_specs, out_shape = share_specs(count, rows, chunks // 2, columns)
    once = pl.Buffered(1)

    def held(a):
        return pl.BlockSpec(a.shape, lambda j: (0,) * a.ndim, pipeline_mode=once)

    return pl.pallas_call(
        functools.partial(inner_kernel, chunks // 2, len(downs)),
        grid=(chunks,),
        in_specs=[held(feed_grad), pl.BlockSpec((1, total, width), lambda j: (j, 0, 0))]
        + [held(a) for a in (hidden, second_grad, normed, inverse, norms)]
        + [ANYWHERE] * (len(downs) + 10),
        out_specs=out_specs + [full(shape), full(shape), full(norms.shape)],
        out_shape=out_shape + [shaped(shape, F32), shaped(shape, LOW), shaped(norms.shape, F32)],
        scratch_shapes=chunk_buffer((count, rows), chunks, width) * 2 + [pltpu.VMEM(shape, F32)],
        compiler_params=params(60),
        cost_estimate=cost(32 * 1.1e9, 32 * 2e6),
        name="inner_back",
    )(feed_grad, slope, hidden, second_grad, normed, inverse, norms, *downs, *ups)


def out_kernel(column, a_ref, ctx_ref, one_ref, two_ref, own_in, other_in, *refs):
    pieces = refs[:10]
    own_ref, other_ref, o_ref, w, sem, tiles, out_sem = refs[10:]
    _, _, x, z, rows, _ = tiles.shape
    width = w.shape[5]
    core = lax.axis_index("c")
    load_weights(pieces, w, sem, column, width, 1)
    norm_grads = jnp.concatenate([one_ref[0:2], two_ref[0:2], one_ref[2:6]], axis=0)
    for y in range(2):
        grad = mm(a_ref[...], ctx_ref[:, y * width : (y + 1) * width], TN).astype(LOW).reshape(z, x, 2, rows, width)
        for parity in range(2):
            slot = (parity + core) % 2
            for at_x in range(x):
                tiles[slot, y, at_x, :, :, :width] = grad[:, at_x, parity]
            for at in range(z * x):
                cell = norm_grads[:, (at * 2 + parity) * rows : (at * 2 + parity + 1) * rows]
                cell = jnp.concatenate([cell, jnp.zeros((8, 128 - rows), F32)], axis=1)
                cell = jnp.concatenate([cell, jnp.zeros((rows - 8, 128), F32)], axis=0)
                tiles[slot, y, at % x, at // x, :, width:] = cell.astype(LOW)
    copies = []
    for slot, ref in enumerate((own_ref, other_ref)):
        for y in range(2):
            copies.append(
                pltpu.make_async_copy(
                    tiles.at[slot, y], ref.at[:, y, :, :, pl.ds(column, width + 128)], out_sem.at[slot, y]
                )
            )
    for copy in copies:
        copy.start()
    for y in range(2):
        ready(w, sem, y)
        o_ref[:, y * width : (y + 1) * width] = mm(a_ref[...], matrix(w, y)).astype(LOW)
    for copy in copies:
        copy.wait()


def out_back(branch_grad, context, one, two, own, other, pieces, rows, column):
    count, width = pieces[0].shape[0], STEP_WIDTH
    inside = pl.BlockSpec(memory_space=pltpu.VMEM)
    return pl.pallas_call(
        functools.partial(out_kernel, column),
        in_specs=[inside] * 4 + [ANYWHERE] * 12,
        out_specs=[ANYWHERE, ANYWHERE, inside],
        out_shape=[shaped(own.shape, LOW), shaped(other.shape, LOW), shaped(context.shape, LOW)],
        scratch_shapes=chunk_buffer((count, rows), 2, width)
        + [pltpu.VMEM((2, 2, 2, count, rows, width + 128), LOW), pltpu.SemaphoreType.DMA((2, 2))],
        input_output_aliases={4: 0, 5: 1},
        compiler_params=params(60),
        cost_estimate=cost(4 * 1.1e9, 4 * 2e6),
        name="out_back",
    )(branch_grad, context, one, two, own, other, *pieces)


def attend_back_kernel(q_ref, k_ref, v_ref, bias_ref, l_ref, g_ref, o_ref):
    k, v, grad = k_ref[0], v_ref[0], g_ref[...]
    lane = lax.broadcasted_iota(jnp.int32, k.shape, 1)
    scale = HEAD**-0.5
    queries = q_ref[0]
    outs = []
    for h, (q, own_grad) in enumerate(zip(head_parts(queries, lane, scale), head_parts(grad, lane))):
        log_total = l_ref[:, h * HEAD : h * HEAD + 1]
        probs = jnp.exp(mm(q, k, NT) + bias_ref[...].astype(F32) - log_total)
        prob_grad = mm(own_grad, v, NT)
        score_grad = probs * (prob_grad - jnp.sum(probs * prob_grad, axis=-1, keepdims=True))
        score_grad = score_grad.astype(LOW)
        outs.append(
            (mm(score_grad, k) * scale, mm(score_grad, queries, TN) * scale, mm(probs.astype(LOW), grad, TN))
        )
    for i in range(3):
        o_ref[i] = jnp.where(lane < HEAD, outs[0][i], outs[1][i]).astype(LOW)


def final_rows_kernel(own_ref, other_ref, o_ref):
    y = lax.axis_index("y")
    for place in range(2):

        @pl.when(y == place)
        def _(place=place):
            o_ref[:, place] = own_ref[...]
            o_ref[:, 1 - place] = other_ref[...]


def final_rows(own, other):
    total, width = own.shape
    block = pl.BlockSpec((ROWS_AT_ONCE, width), lambda i: (i, 0))
    both = pl.pallas_call(
        final_rows_kernel,
        grid=(pl.cdiv(total, ROWS_AT_ONCE),),
        in_specs=[block, block],
        out_specs=pl.BlockSpec((ROWS_AT_ONCE, 2, width), lambda i: (i, 0, 0)),
        out_shape=shaped((total, 2, width), own.dtype),
        compiler_params=params(60),
        name="final_rows",
    )(own, other)
    return both.transpose(1, 0, 2)


def attention_back(qkv, bias, logs, grad):
    total, width = grad.shape
    pairs = width // 128
    column = pl.BlockSpec((total, 128), lambda g: (0, g))
    return pl.pallas_call(
        attend_back_kernel,
        grid=(pairs,),
        in_specs=pair_specs(total, pairs // 2) + [full(bias.shape), column, column],
        out_specs=pl.BlockSpec((3, total, 128), lambda g: (0, 0, g)),
        out_shape=shaped((3, total, width), LOW),
        compiler_params=params(60),
        cost_estimate=cost(25 * 1.1e9, 25 * 2e6),
        name="attention_back",
    )(qkv, qkv, qkv, bias, logs, grad)


def qkv_back_kernel(per_side, x_ref, g_ref, r_ref, *refs):
    pieces, (own_ref, other_ref, o_ref, w, sem, acc) = refs[:10], refs[10:]
    j = pl.program_id(0)

    @pl.when(j == 0)
    def _():
        load_weights(pieces, w, sem, 0, g_ref.shape[2], per_side)

    grad = g_ref[0]
    share_out(mm(x_ref[...], grad, TN).astype(LOW), own_ref, other_ref)
    ready(w, sem, j)
    term = mm(grad, matrix(w, j), NT)

    @pl.when(j == 0)
    def _():
        acc[...] = r_ref[...] + term

    @pl.when(j > 0)
    def _():
        acc[...] += term

    @pl.when(j == 2 * per_side - 1)
    def _():
        o_ref[...] = acc[...].astype(LOW)


def qkv_back(x, grads, first_grad, pieces, rows):
    count, width = pieces[0].shape[0], STEP_WIDTH
    per_side = grads.shape[0]
    shape = first_grad.shape
    out_specs, out_shape = share_specs(count, rows, per_side, per_side * width)
    return pl.pallas_call(
        functools.partial(qkv_back_kernel, per_side),
        grid=(2 * per_side,),
        in_specs=[full(shape), pl.BlockSpec((1, shape[0], width), lambda j: (j % per_side, 0, j // per_side)), full(shape)]
        + [ANYWHERE] * 10,
        out_specs=out_specs + [full(shape)],
        out_shape=out_shape + [shaped(shape, LOW)],
        scratch_shapes=chunk_buffer((count, rows), 2 * per_side, width) + [pltpu.VMEM(shape, F32)],
        compiler_params=params(60),
        cost_estimate=cost(16 * 1.1e9, 16 * 2e6),
        name="qkv_back",
    )(x, grads, first_grad, *pieces)


def at(a, index, axis):
    return lax.dynamic_index_in_dim(a, index, axis, keepdims=False)


def chip_term(own, other, shift):
    x, y = place_xy(ring_place() + shift)
    return at(at(own, x, 0), y, 0).astype(F32) + at(at(other, x, 0), y, 0).astype(F32)


def ring_pair(to_right, to_left):
    return send(to_right, ("x", "y"), RING), send(to_left, ("x", "y"), RING_BACK)


def far_terms(take):
    far = take(2).astype(LOW)
    half = far.shape[0] // 2
    return far[:half], far[half:]


def near_terms(take, from_left, from_right):
    half = from_left.shape[0]
    right, left = take(1).astype(F32), take(-1).astype(F32)
    to_right = jnp.concatenate([right[:half] + from_left.astype(F32), right[half:]]).astype(LOW)
    to_left = jnp.concatenate([left[:half], left[half:] + from_right.astype(F32)]).astype(LOW)
    return to_right, to_left


def chip_terms(own, other):
    return lambda shift: chip_term(own, other, shift)


def square_terms(square):
    def take(shift):
        x, y = place_xy(ring_place() + shift)
        return at(at(square, x, 0), y, 0)

    return take


def line_terms(own, other, from_left, from_right):
    column = chip_term(own, other, 0) + from_left.astype(F32) + from_right.astype(F32)
    z = lax.axis_index("z")
    return [at(column, z, 0)] + [at(column, z ^ k, 0).astype(LOW) for k in range(1, column.shape[0])]


def line_send(terms):
    return [send(term, "z", partners(k + 1)) for k, term in enumerate(terms[1:])]


def total_of(own, others):
    for other in others:
        own = own + other.astype(F32)
    return own


def sum_over_all(value):
    value = value + send(value, "c", SWAP)
    square = [send(value, ("x", "y"), tuple((i, i ^ k) for i in range(4))) for k in (1, 2, 3)]
    value = (value + square[0]) + (square[1] + square[2])
    column = [send(value, "z", partners(k)) for k in (1, 2, 3)]
    return (value + column[0]) + (column[1] + column[2])


def pad_rows(a, total):
    return jnp.pad(a, ((0, total - a.shape[0]), (0, 0)))


def mask_bias(doc_row, reset_row, live, total):
    kinds = jnp.concatenate([jnp.full((MEM,), -1, jnp.int32), doc_row, jnp.full((MEM,), -2, jnp.int32)])
    real = kinds.shape[0]
    kinds = jnp.pad(kinds, (0, total - real), constant_values=-3)
    place = jnp.arange(total, dtype=jnp.int32)
    choose = kinds[:, None] == jnp.arange(reset_row.shape[0], dtype=jnp.int32)[None, :]
    reset_query = jnp.sum(jnp.where(choose, reset_row[None, :], 0), axis=1)
    same = kinds[:, None] == kinds[None, :]
    live_key = place < jnp.minimum(live, MEM)
    token_sees = same | (live_key[None, :] & (reset_query == 0)[:, None])
    memory_sees = ((place >= MEM) | live_key)[None, :]
    sees = jnp.where((kinds < 0)[:, None], memory_sees, token_sees) & (place < real)[None, :]
    return jnp.where(sees, 0.0, MASKED).astype(LOW)


def whole_segment(
    tokens,
    cotangent,
    doc_ids,
    reset_flags,
    mem_live,
    qkv_weight,
    qkv_moment,
    qkv_square,
    qkv_average,
    out_weight,
    out_moment,
    out_square,
    out_average,
    up_weight,
    up_moment,
    up_square,
    up_average,
    down_weight,
    down_moment,
    down_square,
    down_average,
    norm_params,
    norm_moment,
    norm_square,
    norm_average,
):
    y = lax.axis_index("y")
    rows, inner_part = up_weight.shape
    count = lax.axis_size("z")
    width = tokens.shape[2]
    part = qkv_weight.shape[2]
    real = tokens.shape[1]
    total = -(-real // ROWS_AT_ONCE) * ROWS_AT_ONCE

    def mine(a):
        return lax.dynamic_index_in_dim(a, y, 0, keepdims=False)

    qkv_block = jnp.concatenate([qkv_weight[k] for k in range(3)], axis=1).astype(LOW)
    norm_block = jnp.pad(norm_params.astype(LOW), ((0, rows - 4), (0, 128 - rows)))
    second_block = jnp.concatenate([up_weight.astype(LOW), out_weight.T.astype(LOW), norm_block], axis=1)
    down_block = down_weight.T.astype(LOW)

    pair_down = join_pair(down_block, send(down_block, "y", SWAP), "y")
    qkv_block = after(qkv_block, down_block)
    tokens, cotangent, doc_ids = after((tokens, cotangent, doc_ids), pair_down)
    x = pad_rows(mine(tokens), total)
    cot = pad_rows(mine(cotangent), total)
    bias = mask_bias(mine(doc_ids), mine(reset_flags), mine(mem_live), total)

    z_qkv = line_pieces(qkv_block)
    other_pair = send(pair_down, "x", SWAP)
    z_second = line_pieces(after(second_block, *z_qkv))
    column_qkv = join_column(after(tuple(z_qkv), x, cot, bias, other_pair))
    square_down = join_pair(pair_down, other_pair, "x")
    near_qkv = ring_near(column_qkv)
    far_qkv = ring_far(*near_qkv)
    w_qkv = both_cores((column_qkv,) + near_qkv + far_qkv)
    column_second = after(join_column(after(tuple(z_second), square_down)), *far_qkv)
    near_second = ring_near(column_second)
    square_down = after(square_down, *z_second)
    down_one, down_two = send(square_down, "z", partners(1)), send(square_down, "z", partners(2))

    qkv = project(after(x, column_second), w_qkv, rows)
    context, logs = attention(qkv, bias)

    near_second = after(near_second, context)
    far_second = ring_far(*near_second)
    w_second = both_cores((column_second,) + near_second + far_second)
    down_two = after(down_two, near_second[0])
    down_three = send(down_two, "z", partners(1))

    hidden, normed, inverse, norms, active, slope = up(x, after(context, down_two), w_second, rows, inner_part)

    w_down = both_cores((square_down, down_one, down_two, after(down_three, active)))
    result, second_grad, feed_grad, norm_two = down(active, normed, norms, cot, w_down, rows)

    chunks = active.shape[0]
    own_down, other = weight_grad(
        feed_grad,
        active,
        pl.BlockSpec((1, total, STEP_WIDTH), lambda j: (j, 0, 0)),
        chunks,
        count,
        rows,
        "down_grad",
        lines_first=True,
    )
    z, place_x = lax.axis_index("z"), lax.axis_index("x")

    def pair(own, other):
        own, other = jnp.where(y == 0, own, other), jnp.where(y == 0, other, own)
        return jnp.stack([own, other], axis=1).transpose(1, 0, 2)

    def term(own, other):
        return lambda k: at(own, z ^ k, 0).astype(F32) + at(other, z ^ k, 0).astype(F32)

    other_down = send(other, "c", SWAP)
    down_term = term(own_down, other_down)
    crossing = down_term(3).astype(LOW)
    crossed = send(crossing, "z", partners(1))
    own_result = result[:real]
    shared_result = send(own_result, "y", SWAP)
    columns = inner_part + part + 128
    own, other, first_grad, branch_grad, norm_one = inner_back(
        after(feed_grad, crossing, own_result),
        slope,
        hidden,
        second_grad,
        normed,
        inverse,
        norms,
        w_down,
        w_second,
        rows,
        columns,
    )
    crossed, shared_result = after(crossed, branch_grad), after(shared_result, branch_grad)
    own_second, other, context_grad = out_back(
        after(branch_grad, crossed, shared_result),
        context,
        norm_one,
        norm_two,
        own,
        other,
        w_second,
        rows,
        inner_part,
    )
    other_second = send(other, "c", SWAP)
    crossed = after(crossed, own_second)
    one, two = down_term(1).astype(LOW), (down_term(2) + crossed.astype(F32)).astype(LOW)
    from_one, from_two = send(one, "z", partners(1)), send(two, "z", partners(2))
    take_second = chip_terms(own_second, after(other_second, one, two))
    far = far_terms(take_second)
    far_second = ring_pair(*far)
    grads = attention_back(qkv, bias, logs, after(context_grad, *far))

    far_second = after(far_second, grads)
    near = near_terms(take_second, *far_second)
    near_second = ring_pair(*near)
    from_one, from_two = after(from_one, *near), after(from_two, *near)
    square = down_term(0) + from_one.astype(F32) + from_two.astype(F32)
    to_x = at(square, 1 - place_x, 0).astype(LOW)
    own_qkv, other, own_grad = qkv_back(after(x, to_x), grads, first_grad, w_qkv, rows)
    near_second = after(near_second, own_qkv)
    from_x = send(after(to_x, *near_second), "x", SWAP)
    other_qkv = send(after(other, *near_second), "c", SWAP)
    shared_grad = send(after(own_grad[: total // 2], *near_second), "y", SWAP)
    column = chip_term(own_second, other_second, 0) + near_second[0].astype(F32) + near_second[1].astype(F32)
    crossing = at(column, z ^ 3, 0).astype(LOW)
    crossed = send(crossing, "z", partners(1))
    take_qkv = chip_terms(own_qkv, after(other_qkv, crossing))
    far = far_terms(take_qkv)
    far_qkv = ring_pair(*far)
    from_x, shared_grad = after(from_x, *far), after(shared_grad, *far)
    half = at(square, place_x, 0) + from_x.astype(F32)
    to_y = at(half, 1 - y, 0).astype(LOW)
    crossed = after(crossed, *far)
    one, two = at(column, z ^ 1, 0).astype(LOW), (at(column, z ^ 2, 0) + crossed.astype(F32)).astype(LOW)
    from_one, from_two = send(one, "z", partners(1)), send(two, "z", partners(2))
    far_qkv = after(far_qkv, one, two, to_y, shared_grad)
    near = near_terms(take_qkv, *far_qkv)
    near_qkv = ring_pair(*near)
    output = final_rows(own_result, after(shared_result, *near))
    near_qkv = after(near_qkv, output)
    from_one, from_two = after(from_one, *near), after(from_two, *near)
    second_sum = at(column, z, 0) + from_one.astype(F32) + from_two.astype(F32)
    line_qkv = line_terms(own_qkv, other_qkv, *after(near_qkv, second_sum))
    others_qkv = line_send(line_qkv)
    from_y = send(after(to_y, *line_qkv), "y", SWAP)
    last_rows = after(own_grad[total // 2 : real], *line_qkv)
    shared_grad = jnp.concatenate([shared_grad, send(last_rows, "y", SWAP)])
    down_sum = at(half, y, 0) + from_y.astype(F32)
    others_qkv = after(tuple(others_qkv), down_sum, shared_grad)
    input_grad = pair(own_grad[:real], shared_grad).astype(F32)
    qkv_sum = total_of(line_qkv[0], others_qkv)

    qkv_sum = qkv_sum.reshape(rows, 3, part).transpose(1, 0, 2)
    up_sum = second_sum[:, :inner_part]
    out_sum = second_sum[:, inner_part : inner_part + part].T
    norm_sum = second_sum[:4, inner_part + part : inner_part + part + rows]
    down_sum = down_sum.T
    local_squares = (
        jnp.sum(qkv_sum * qkv_sum)
        + jnp.sum(out_sum * out_sum)
        + jnp.sum(up_sum * up_sum)
        + jnp.sum(down_sum * down_sum)
        + jnp.sum(norm_sum * norm_sum) / lax.axis_size("y")
    )
    grad_norm = jnp.sqrt(sum_over_all(jnp.full((8, 128), local_squares))[0, 0])
    threshold = math.sqrt(4 * D * D + 2 * D * FF + 4 * D)
    factor = jnp.minimum(1.0, threshold / (grad_norm + 1e-06))
    new_qkv = adam_step(qkv_weight, qkv_moment, qkv_square, qkv_average, qkv_sum * factor, 0.02, 0.01)
    new_out = adam_step(out_weight, out_moment, out_square, out_average, out_sum * factor, 0.06, 0.01)
    new_up = adam_step(up_weight, up_moment, up_square, up_average, up_sum * factor, 0.02, 0.01)
    new_down = adam_step(down_weight, down_moment, down_square, down_average, down_sum * factor, 0.02, 0.01)
    new_norm = adam_step(norm_params, norm_moment, norm_square, norm_average, norm_sum * factor, 0.4, 0.0)
    return (output, input_grad, grad_norm) + new_qkv + new_out + new_up + new_down + new_norm


def solution(mesh):
    wide, narrow = mesh.shape["wide"], mesh.shape["narrow"]

    def placed(w, n):
        state = [P(None, w, n)] * 4 + [P(n, w)] * 4 + [P(w, n)] * 4 + [P(n, w)] * 4 + [P(None, w)] * 4
        return (
            tuple([P(w, None, None)] * 2 + [P(w, None)] * 2 + [P(w)] + state),
            tuple([P(w, None, None)] * 2 + [P()] + state),
        )

    def run(*args):
        if narrow == 2 and wide == 16 and args[0].shape[0] == wide * narrow:
            body = whole_segment
            grid = jax.sharding.Mesh(mesh.devices.reshape(wide // 4, 2, 2, 2), ("z", "x", "c", "y"))
            ins, outs = placed(("z", "x", "c"), "y")
        else:
            body, grid = shared_rows, mesh
            ins, outs = placed("wide", "narrow")
        return jax.shard_map(body, mesh=grid, in_specs=ins, out_specs=outs, check_vma=False)(*args)

    return run
```

```python
import functools
import math

import jax
import jax.numpy as jnp
from jax import lax
from jax.experimental import pallas as pl
from jax.experimental.pallas import tpu as pltpu
from jax.sharding import PartitionSpec as P

D = 1024
HEAD = 64
FF = 4096
MEM = 10
STEP = 10


NORM_EPS = 1e-12
BETA_ONE = 0.9
BETA_TWO = 0.98
ADAM_EPS = 1e-06
AVERAGE_KEEP = 0.75
MASKED = -1e30


def allowed_mask(doc_row, reset_row, live_count):
    rows_all = doc_row.shape[0] + 2 * MEM
    kinds = jnp.concatenate(
        [jnp.full((MEM,), -1, jnp.int32), doc_row, jnp.full((MEM,), -2, jnp.int32)]
    )
    place = jnp.arange(rows_all, dtype=jnp.int32)
    read_key = place < MEM
    live_key = place < live_count
    choose = kinds[:, None] == jnp.arange(reset_row.shape[0], dtype=jnp.int32)[None, :]
    reset_query = jnp.sum(jnp.where(choose, reset_row[None, :], 0), axis=1)
    memory_query = kinds < 0
    same_doc = kinds[:, None] == kinds[None, :]
    token_sees = same_doc | (read_key & live_key)[None, :] & (reset_query == 0)[:, None]
    memory_sees = jnp.broadcast_to((~read_key | live_key)[None, :], (rows_all, rows_all))
    return jnp.where(memory_query[:, None], memory_sees, token_sees)


def norm_forward(rows_in, gain, shift):
    center = rows_in - jnp.mean(rows_in, axis=-1, keepdims=True)
    inverse = lax.rsqrt(jnp.mean(center * center, axis=-1, keepdims=True) + NORM_EPS)
    normed = center * inverse
    return (normed * gain + shift, normed, inverse)


def norm_backward(grad, normed, inverse, gain):
    scaled = grad * gain
    back = inverse * (
        scaled
        - jnp.mean(scaled, axis=-1, keepdims=True)
        - normed * jnp.mean(scaled * normed, axis=-1, keepdims=True)
    )
    return (back, jnp.stack([jnp.sum(grad * normed, axis=0), jnp.sum(grad, axis=0)]))


def masked_scores(query, keys, allowed):
    scores = jnp.einsum("qhd,khd->hqk", query, keys, preferred_element_type=jnp.float32) * (
        1.0 / math.sqrt(HEAD)
    )
    return jnp.where(allowed[None], scores, MASKED)


def attend(inputs):
    query, keys, values, allowed = inputs
    scores = masked_scores(query, keys, allowed)
    row_top = jnp.max(scores, axis=-1, keepdims=True)
    expo = jnp.exp(scores - row_top)
    row_total = jnp.sum(expo, axis=-1, keepdims=True)
    probs = (expo / row_total).astype(jnp.bfloat16)
    context = jnp.einsum("hqk,khd->qhd", probs, values, preferred_element_type=jnp.float32)
    return (context.astype(jnp.bfloat16), row_top + jnp.log(row_total))


def attend_back(inputs):
    query, keys, values, allowed, log_total, context_grad = inputs
    probs = jnp.exp(masked_scores(query, keys, allowed) - log_total)
    value_grad = jnp.einsum(
        "hqk,qhd->khd", probs.astype(jnp.bfloat16), context_grad, preferred_element_type=jnp.float32
    )
    prob_grad = jnp.einsum("qhd,khd->hqk", context_grad, values, preferred_element_type=jnp.float32)
    score_grad = probs * (prob_grad - jnp.sum(probs * prob_grad, axis=-1, keepdims=True))
    score_grad = score_grad.astype(jnp.bfloat16)
    scale_now = 1.0 / math.sqrt(HEAD)
    query_grad = (
        jnp.einsum("hqk,khd->qhd", score_grad, keys, preferred_element_type=jnp.float32) * scale_now
    )
    key_grad = (
        jnp.einsum("hqk,qhd->khd", score_grad, query, preferred_element_type=jnp.float32)
        * scale_now
    )
    return (
        query_grad.astype(jnp.bfloat16),
        key_grad.astype(jnp.bfloat16),
        value_grad.astype(jnp.bfloat16),
    )


def adam_step(weight, moment, square, average, grad, rate, decay):
    moment = BETA_ONE * moment + (1.0 - BETA_ONE) * grad
    square = BETA_TWO * square + (1.0 - BETA_TWO) * grad * grad
    first_hat = moment / (1.0 - BETA_ONE**STEP)
    second_hat = square / (1.0 - BETA_TWO**STEP)
    weight = weight - rate * (first_hat / (jnp.sqrt(second_hat) + ADAM_EPS) + decay * weight)
    average = AVERAGE_KEEP * average + (1.0 - AVERAGE_KEEP) * weight
    return (weight, moment, square, average)


def row_scatter(terms):
    return lax.psum_scatter(terms, "narrow", scatter_dimension=0, tiled=True)


def row_gather(piece):
    return lax.all_gather(piece, "narrow", axis=0, tiled=True)


def narrow_norm(grads):
    return lax.psum(grads, "narrow")


def shared_rows(
    tokens,
    cotangent,
    doc_ids,
    reset_flags,
    mem_live,
    qkv_weight,
    qkv_moment,
    qkv_square,
    qkv_average,
    out_weight,
    out_moment,
    out_square,
    out_average,
    up_weight,
    up_moment,
    up_square,
    up_average,
    down_weight,
    down_moment,
    down_square,
    down_average,
    norm_params,
    norm_moment,
    norm_square,
    norm_average,
):
    narrow_count = lax.axis_size("narrow")
    seg_count, rows_all, width = tokens.shape
    w_qkv, w_out, w_up, w_down, norms_low = (
        lax.all_gather(qkv_weight.astype(jnp.bfloat16), "wide", axis=1, tiled=True),
        lax.all_gather(out_weight.astype(jnp.bfloat16), "wide", axis=1, tiled=True),
        lax.all_gather(up_weight.astype(jnp.bfloat16), "wide", axis=0, tiled=True),
        lax.all_gather(down_weight.astype(jnp.bfloat16), "wide", axis=1, tiled=True),
        lax.all_gather(norm_params.astype(jnp.bfloat16), "wide", axis=1, tiled=True),
    )
    norms = norms_low.astype(jnp.float32)
    local_cols = w_qkv.shape[2]
    local_heads = local_cols // HEAD
    total_rows = seg_count * rows_all
    flat_in = tokens.reshape(total_rows, width)
    flat_cot = cotangent.reshape(total_rows, width)
    allowed = jax.vmap(allowed_mask)(doc_ids, reset_flags, mem_live)
    projected = jnp.einsum(
        "md,kdc->kmc", flat_in, w_qkv, preferred_element_type=jnp.float32
    ).astype(jnp.bfloat16)
    split_heads = projected.reshape(3, seg_count, rows_all, local_heads, HEAD)
    query, keys, values = (split_heads[0], split_heads[1], split_heads[2])
    context, log_total = lax.map(attend, (query, keys, values, allowed))
    context_flat = context.reshape(total_rows, local_cols)
    attention_terms = jnp.dot(context_flat, w_out, preferred_element_type=jnp.float32)
    share = total_rows // narrow_count
    row_start = lax.axis_index("narrow") * share
    own_in = lax.dynamic_slice_in_dim(flat_in, row_start, share, 0)
    own_cot = lax.dynamic_slice_in_dim(flat_cot, row_start, share, 0)
    first_sum = own_in.astype(jnp.float32) + row_scatter(attention_terms)
    hidden, normed_one, inverse_one = norm_forward(first_sum, norms[0], norms[1])
    hidden_low = row_gather(hidden.astype(jnp.bfloat16))
    inner = jnp.dot(hidden_low, w_up, preferred_element_type=jnp.float32)
    active, gelu_pull = jax.vjp(lambda value_in: jax.nn.gelu(value_in, approximate=False), inner)
    active_low = active.astype(jnp.bfloat16)
    feed_terms = jnp.dot(active_low, w_down, preferred_element_type=jnp.float32)
    feed = row_scatter(feed_terms)
    second_sum = hidden + feed
    result, normed_two, inverse_two = norm_forward(second_sum, norms[2], norms[3])
    result_low = result.astype(jnp.bfloat16)
    second_grad, norm_two_grads = norm_backward(
        own_cot.astype(jnp.float32), normed_two, inverse_two, norms[2]
    )
    norm_two_grads = narrow_norm(norm_two_grads)
    output = row_gather(result_low)
    feed_grad = row_gather(second_grad.astype(jnp.bfloat16))
    output = output.reshape(seg_count, rows_all, width)
    down_grad = jnp.einsum("mf,md->fd", active_low, feed_grad, preferred_element_type=jnp.float32)
    active_grad = jnp.einsum("md,fd->mf", feed_grad, w_down, preferred_element_type=jnp.float32)
    inner_grad = gelu_pull(active_grad)[0].astype(jnp.bfloat16)
    up_grad = jnp.einsum("md,mf->df", hidden_low, inner_grad, preferred_element_type=jnp.float32)
    hidden_terms = jnp.einsum("mf,df->md", inner_grad, w_up, preferred_element_type=jnp.float32)
    hidden_grad = second_grad + row_scatter(hidden_terms)
    first_grad, norm_one_grads = norm_backward(hidden_grad, normed_one, inverse_one, norms[0])
    norm_one_grads = narrow_norm(norm_one_grads)
    branch_grad = row_gather(first_grad.astype(jnp.bfloat16))
    out_grad_weight = jnp.einsum(
        "mc,md->cd", context_flat, branch_grad, preferred_element_type=jnp.float32
    )
    context_grad = jnp.einsum(
        "md,cd->mc", branch_grad, w_out, preferred_element_type=jnp.float32
    ).astype(jnp.bfloat16)
    context_grad = context_grad.reshape(seg_count, rows_all, local_heads, HEAD)
    query_grad, key_grad, value_grad = lax.map(
        attend_back, (query, keys, values, allowed, log_total, context_grad)
    )
    stacked_grad = jnp.stack([query_grad, key_grad, value_grad]).reshape(3, total_rows, local_cols)
    qkv_grad = jnp.einsum("md,kmc->kdc", flat_in, stacked_grad, preferred_element_type=jnp.float32)
    input_terms = jnp.einsum("kmc,kdc->md", stacked_grad, w_qkv, preferred_element_type=jnp.float32)
    input_grad = lax.all_gather(first_grad + row_scatter(input_terms), "narrow", axis=0, tiled=True)
    input_grad = input_grad.reshape(seg_count, rows_all, width)
    norm_grads = jnp.concatenate([norm_one_grads, norm_two_grads], axis=0)
    qkv_sum, out_sum, up_sum, down_sum, norm_sum = (
        lax.psum_scatter(qkv_grad, "wide", scatter_dimension=1, tiled=True),
        lax.psum_scatter(out_grad_weight, "wide", scatter_dimension=1, tiled=True),
        lax.psum_scatter(up_grad, "wide", scatter_dimension=0, tiled=True),
        lax.psum_scatter(down_grad, "wide", scatter_dimension=1, tiled=True),
        lax.psum_scatter(norm_grads, "wide", scatter_dimension=1, tiled=True),
    )
    local_squares = (
        jnp.sum(qkv_sum * qkv_sum)
        + jnp.sum(out_sum * out_sum)
        + jnp.sum(up_sum * up_sum)
        + jnp.sum(down_sum * down_sum)
        + jnp.sum(norm_sum * norm_sum) / narrow_count
    )
    grad_norm = jnp.sqrt(lax.psum(local_squares, ("wide", "narrow")))
    threshold = math.sqrt(4 * D * D + 2 * D * FF + 4 * D)
    factor = jnp.minimum(1.0, threshold / (grad_norm + 1e-06))
    new_qkv = adam_step(
        qkv_weight, qkv_moment, qkv_square, qkv_average, qkv_sum * factor, 0.02, 0.01
    )
    new_out = adam_step(
        out_weight, out_moment, out_square, out_average, out_sum * factor, 0.06, 0.01
    )
    new_up = adam_step(up_weight, up_moment, up_square, up_average, up_sum * factor, 0.02, 0.01)
    new_down = adam_step(
        down_weight, down_moment, down_square, down_average, down_sum * factor, 0.02, 0.01
    )
    new_norm = adam_step(
        norm_params, norm_moment, norm_square, norm_average, norm_sum * factor, 0.4, 0.0
    )
    return (
        output,
        input_grad,
        grad_norm,
        new_qkv[0],
        new_qkv[1],
        new_qkv[2],
        new_qkv[3],
        new_out[0],
        new_out[1],
        new_out[2],
        new_out[3],
        new_up[0],
        new_up[1],
        new_up[2],
        new_up[3],
        new_down[0],
        new_down[1],
        new_down[2],
        new_down[3],
        new_norm[0],
        new_norm[1],
        new_norm[2],
        new_norm[3],
    )


SWAP = ((0, 1), (1, 0))
RING = ((0, 1), (1, 3), (3, 2), (2, 0))
RING_BACK = tuple((b, a) for a, b in RING)


def send(block, axes, pairs):
    return lax.ppermute(block, axes, list(pairs))


def ring_place():
    x, y = lax.axis_index("x"), lax.axis_index("y")
    return jnp.where(x == 0, y, 3 - y)


def place_xy(place):
    place = lax.rem(place + 4, 4)
    x = place // 2
    return x, jnp.where(x == 0, place, 3 - place)


def ring_near(block):
    return send(block, ("x", "y"), RING), send(block, ("x", "y"), RING_BACK)


def ring_far(left, right):
    half = left.shape[0] // 2
    return send(left[:half], ("x", "y"), RING), send(right[half:], ("x", "y"), RING_BACK)


def after(value, *others):
    return lax.optimization_barrier((value,) + others)[0]


STEP_WIDTH = 512
RING_SHIFTS = (0, -1, 1, 2, 2)
NT = (((1,), (1,)), ((), ()))
TN = (((0,), (0,)), ((), ()))
NN = (((1,), (0,)), ((), ()))
F32, LOW = jnp.float32, jnp.bfloat16
ANYWHERE = pl.BlockSpec(memory_space=pltpu.HBM)


def params(mib):
    return pltpu.CompilerParams(vmem_limit_bytes=mib << 20)


def cost(flops, moved):
    return pl.CostEstimate(flops=int(flops), bytes_accessed=int(moved), transcendentals=0)


def shaped(shape, dtype):
    return jax.ShapeDtypeStruct(shape, dtype)


def full(shape):
    return pl.BlockSpec(shape, lambda *_: (0,) * len(shape))


def mm(a, b, dims=NN):
    return lax.dot_general(a, b, dims, preferred_element_type=F32)


def join_column_kernel(count, *refs):
    out, sem = refs[-2:]
    z = lax.axis_index("z")
    copies = [pltpu.make_async_copy(ref, out.at[z ^ k], sem.at[k]) for k, ref in enumerate(refs[:count])]
    for copy in copies:
        copy.start()
    for copy in copies:
        copy.wait()


def partners(k):
    return tuple((i, i ^ k) for i in range(lax.axis_size("z")))


def line_pieces(block):
    return [block] + [send(block, "z", partners(k)) for k in range(1, lax.axis_size("z"))]


def join_column(pieces):
    count = len(pieces)
    shape = (count,) + pieces[0].shape
    return pl.pallas_call(
        functools.partial(join_column_kernel, count),
        in_specs=[ANYWHERE] * count,
        out_specs=pl.BlockSpec(memory_space=pltpu.VMEM),
        out_shape=shaped(shape, pieces[0].dtype),
        scratch_shapes=[pltpu.SemaphoreType.DMA((count,))],
        compiler_params=params(60),
        name="join_column",
    )(*pieces)


def join_pair_kernel(axis, own, other, out, sem):
    place = lax.axis_index(axis)
    copies = [pltpu.make_async_copy(own, out.at[place], sem.at[0])]
    copies.append(pltpu.make_async_copy(other, out.at[1 - place], sem.at[1]))
    for copy in copies:
        copy.start()
    for copy in copies:
        copy.wait()


def join_pair(own, other, axis):
    return pl.pallas_call(
        functools.partial(join_pair_kernel, axis),
        in_specs=[ANYWHERE] * 2,
        out_specs=pl.BlockSpec(memory_space=pltpu.VMEM),
        out_shape=shaped((2,) + own.shape, own.dtype),
        scratch_shapes=[pltpu.SemaphoreType.DMA((2,))],
        compiler_params=params(60),
        name="join_pair",
    )(own, other)


def both_cores(pieces):
    return list(pieces) + [send(p, "c", SWAP) for p in pieces]


def load_weights(pieces, w, sem, column, width, per_side):
    place, core = ring_place(), lax.axis_index("c")
    rows = w.shape[4]
    for k in range(per_side):
        for group, core_at in ((pieces[:5], core), (pieces[5:], 1 - core)):
            for i, (ref, shift) in enumerate(zip(group, RING_SHIFTS)):
                x, y = place_xy(place + shift)
                chunk = y * per_side + k
                first = ref.shape[0] if i == 4 else 0
                pltpu.make_async_copy(
                    ref.at[:, pl.ds(0, rows), pl.ds(column + k * width, width)],
                    w.at[chunk, pl.ds(first, ref.shape[0]), x, core_at],
                    sem.at[chunk],
                ).start()


def load_lines(pieces, w, sem, width, per_side):
    z, core = lax.axis_index("z"), lax.axis_index("c")
    count = len(pieces) // 2
    for k in range(per_side):
        for group, core_at in ((pieces[:count], core), (pieces[count:], 1 - core)):
            for i, ref in enumerate(group):
                for y in range(2):
                    chunk = y * per_side + k
                    pltpu.make_async_copy(
                        ref.at[:, y, :, pl.ds(k * width, width)], w.at[chunk, z ^ i, :, core_at], sem.at[chunk]
                    ).start()


def ready(w, sem, chunk):
    pltpu.make_async_copy(w.at[chunk], w.at[chunk], sem.at[chunk]).wait()


def matrix(w, chunk):
    block = w[chunk]
    return block.reshape(-1, block.shape[-1])


def chunk_buffer(shapes, chunks, width):
    z, rows = shapes
    return [pltpu.VMEM((chunks, z, 2, 2, rows, width), LOW), pltpu.SemaphoreType.DMA((chunks,))]


def alternate(per_side):
    return lambda j: (j % 2) * per_side + j // 2


def project_kernel(per_side, x_ref, *refs):
    pieces, (o_ref, w, sem) = refs[:10], refs[10:]
    j = pl.program_id(0)

    @pl.when(j == 0)
    def _():
        load_weights(pieces, w, sem, 0, o_ref.shape[2], per_side)

    chunk = alternate(per_side)(j)
    ready(w, sem, chunk)
    o_ref[0] = mm(x_ref[...], matrix(w, chunk)).astype(LOW)


def project(x, pieces, rows):
    count, width = pieces[0].shape[0], STEP_WIDTH
    per_side = pieces[0].shape[2] // width
    at = alternate(per_side)
    return pl.pallas_call(
        functools.partial(project_kernel, per_side),
        grid=(2 * per_side,),
        in_specs=[full(x.shape)] + [ANYWHERE] * 10,
        out_specs=pl.BlockSpec((1, x.shape[0], width), lambda j: (at(j), 0, 0)),
        out_shape=shaped((2 * per_side, x.shape[0], width), LOW),
        scratch_shapes=chunk_buffer((count, rows), 2 * per_side, width),
        compiler_params=params(60),
        cost_estimate=cost(6 * 1.1e9, 6 * 2e6),
        name="project",
    )(x, *pieces)


def head_parts(a, lane, scale=None):
    a = a if scale is None else a * jnp.asarray(scale, a.dtype)
    none = jnp.zeros_like(a)
    return jnp.where(lane < HEAD, a, none), jnp.where(lane < HEAD, none, a)


def attend_kernel(q_ref, k_ref, v_ref, bias_ref, o_ref, l_ref):
    k, v = k_ref[0], v_ref[0]
    lane = lax.broadcasted_iota(jnp.int32, k.shape, 1)
    outs, logs = [], []
    for q in head_parts(q_ref[0], lane, HEAD**-0.5):
        scores = mm(q, k, NT) + bias_ref[...].astype(F32)
        top = jnp.max(scores, axis=-1, keepdims=True)
        expo = jnp.exp(scores - top)
        total = jnp.sum(expo, axis=-1, keepdims=True)
        outs.append(mm((expo * (1.0 / total)).astype(LOW), v))
        logs.append(top + jnp.log(total))
    o_ref[...] = jnp.where(lane < HEAD, outs[0], outs[1]).astype(LOW)
    l_ref[...] = jnp.where(lane < HEAD, logs[0], logs[1])


def pair_specs(total, per_side):
    def spec(k):
        return pl.BlockSpec((1, total, 128), lambda g: ((g // per_side) * 3 + k, 0, g % per_side))

    return [spec(k) for k in range(3)]


def attention(qkv, bias):
    total, width = qkv.shape[1], qkv.shape[2] * 2
    pairs = width // 128
    return pl.pallas_call(
        attend_kernel,
        grid=(pairs,),
        in_specs=pair_specs(total, pairs // 2) + [full(bias.shape)],
        out_specs=[pl.BlockSpec((total, 128), lambda g: (0, g))] * 2,
        out_shape=[shaped((total, width), LOW), shaped((total, width), F32)],
        compiler_params=params(60),
        cost_estimate=cost(17 * 1.1e9, 17 * 2e6),
        name="attention",
    )(qkv, qkv, qkv, bias)


ROWS_AT_ONCE = 32


def by_rows(total, body, carry=0):
    def step(i, held):
        return body(pl.ds(pl.multiple_of(i * ROWS_AT_ONCE, ROWS_AT_ONCE), ROWS_AT_ONCE), held)

    return lax.fori_loop(0, total // ROWS_AT_ONCE, step, carry, unroll=True)


def normalize(v):
    center = v - jnp.mean(v, axis=-1, keepdims=True)
    inverse = lax.rsqrt(jnp.mean(center * center, axis=-1, keepdims=True) + NORM_EPS)
    return center * inverse, inverse


def unnormalize(scaled, normed, inverse):
    return inverse * (
        scaled
        - jnp.mean(scaled, axis=-1, keepdims=True)
        - normed * jnp.mean(scaled * normed, axis=-1, keepdims=True)
    )


def fold(a):
    return jnp.sum(a.reshape(-1, 8, a.shape[-1]), axis=0)


def gelu_parts(u):
    phi = 0.5 + 0.5 * lax.erf(u * math.sqrt(0.5))
    return u * phi, phi + u * (jnp.exp(-0.5 * (u * u)) * (1.0 / math.sqrt(2.0 * math.pi)))


def up_kernel(per_side, x_ref, ctx_ref, *refs):
    pieces = refs[:10]
    h_ref, n_ref, i_ref, norms_ref, g_ref, d_ref, wu, us, wo, os, nw, ns, acc = refs[10:]
    j = pl.program_id(0)
    width = g_ref.shape[2]

    @pl.when(j == 0)
    def _():
        first = 2 * per_side // 2 * width
        load_weights(pieces, nw, ns, first + width, 128, 1)
        load_weights(pieces, wo, os, first, width, 1)
        load_weights(pieces, wu, us, 0, width, per_side)
        ready(nw, ns, 0)
        ready(nw, ns, 1)
        cells = nw[0].reshape(-1, nw.shape[4], 128).astype(F32)
        side = x_ref.shape[1] // cells.shape[0]
        norms_ref[...] = jnp.concatenate([cells[i, :8, :side] for i in range(cells.shape[0])], axis=1)
        ready(wo, os, 0)
        acc[...] = mm(ctx_ref[:, :width], matrix(wo, 0), NT)
        ready(wo, os, 1)
        acc[...] += mm(ctx_ref[:, width:], matrix(wo, 1), NT)
        gain, shift = norms_ref[0:1], norms_ref[1:2]

        def rows(r, held):
            normed, inverse = normalize(x_ref[r].astype(F32) + acc[r])
            n_ref[r] = normed
            i_ref[r] = jnp.broadcast_to(inverse, (ROWS_AT_ONCE, 128))
            h_ref[r] = (normed * gain + shift).astype(LOW)
            return held

        by_rows(x_ref.shape[0], rows)

    chunk = alternate(per_side)(j)
    ready(wu, us, chunk)
    active, slope = gelu_parts(mm(h_ref[...], matrix(wu, chunk)))
    g_ref[0] = active.astype(LOW)
    d_ref[0] = slope.astype(LOW)


def up(x, context, pieces, rows, inner_part):
    count, width = pieces[0].shape[0], STEP_WIDTH
    per_side = inner_part // width
    at = alternate(per_side)
    total, model = x.shape
    chunks = pl.BlockSpec((1, total, width), lambda j: (at(j), 0, 0))
    return pl.pallas_call(
        functools.partial(up_kernel, per_side),
        grid=(2 * per_side,),
        in_specs=[full(x.shape)] * 2 + [ANYWHERE] * 10,
        out_specs=[full(x.shape), full(x.shape), full((total, 128)), full((8, model)), chunks, chunks],
        out_shape=[
            shaped(x.shape, LOW),
            shaped(x.shape, F32),
            shaped((total, 128), F32),
            shaped((8, model), F32),
            shaped((2 * per_side, total, width), LOW),
            shaped((2 * per_side, total, width), LOW),
        ],
        scratch_shapes=chunk_buffer((count, rows), 2 * per_side, width)
        + chunk_buffer((count, rows), 2, width)
        + chunk_buffer((count, 16), 2, 128)
        + [pltpu.VMEM(x.shape, F32)],
        compiler_params=params(60),
        cost_estimate=cost(22 * 1.1e9, 22 * 2e6),
        name="up",
    )(x, context, *pieces)


def down_kernel(per_side, pieces_count, g_ref, n_ref, norms_ref, cot_ref, *refs):
    pieces = refs[:pieces_count]
    o_ref, d_ref, f_ref, ng_ref, w, sem, acc = refs[pieces_count:]
    j = pl.program_id(0)

    @pl.when(j == 0)
    def _():
        load_lines(pieces, w, sem, g_ref.shape[2], per_side)
        acc[...] = jnp.zeros_like(acc)

    chunk = alternate(per_side)(j)
    ready(w, sem, chunk)
    acc[...] += mm(g_ref[0], matrix(w, chunk), NT)

    @pl.when(j == 2 * per_side - 1)
    def _():
        gain_one, shift_one, gain, shift = (norms_ref[i : i + 1] for i in range(4))

        def rows(r, held):
            normed, inverse = normalize(n_ref[r] * gain_one + shift_one + acc[r])
            o_ref[r] = (normed * gain + shift).astype(LOW)
            dy = cot_ref[r].astype(F32)
            back = unnormalize(dy * gain, normed, inverse)
            d_ref[r] = back
            f_ref[r] = back.astype(LOW)
            return held[0] + fold(dy * normed), held[1] + fold(dy)

        none = jnp.zeros((8, acc.shape[1]), F32)
        gains, shifts = by_rows(acc.shape[0], rows, (none, none))
        ng_ref[...] = jnp.concatenate(
            [jnp.sum(gains, axis=0, keepdims=True), jnp.sum(shifts, axis=0, keepdims=True), none[:6]], axis=0
        )


def down(active, normed, norms, cot, pieces, rows):
    width = STEP_WIDTH
    chunks, total = active.shape[0], active.shape[1]
    at = alternate(chunks // 2)
    shape = normed.shape
    count = len(pieces) // 2
    return pl.pallas_call(
        functools.partial(down_kernel, chunks // 2, len(pieces)),
        grid=(chunks,),
        in_specs=[pl.BlockSpec((1, total, width), lambda j: (at(j), 0, 0)), full(shape), full(norms.shape), full(shape)]
        + [ANYWHERE] * len(pieces),
        out_specs=[full(shape), full(shape), full(shape), full(norms.shape)],
        out_shape=[shaped(shape, LOW), shaped(shape, F32), shaped(shape, LOW), shaped(norms.shape, F32)],
        scratch_shapes=chunk_buffer((count, rows), chunks, width) + [pltpu.VMEM(shape, F32)],
        compiler_params=params(60),
        cost_estimate=cost(17 * 1.1e9, 17 * 2e6),
        name="down",
    )(active, normed, norms, cot, *pieces)


def share_out(value, own_ref, other_ref, lines_first=False):
    core = lax.axis_index("c")
    if lines_first:
        z, x, _, rows, width = own_ref.shape
        value = value.reshape(z, x, 2, rows, width)
        for parity in range(2):

            @pl.when(core == parity)
            def _(parity=parity):
                own_ref[:, :, 0] = value[:, :, parity]

            @pl.when(core != parity)
            def _(parity=parity):
                other_ref[:, :, 0] = value[:, :, parity]

        return
    squares, _, z, rows, width = own_ref.shape
    value = value.reshape(z, squares, 2, rows, width)
    for parity in range(2):

        @pl.when(core == parity)
        def _(parity=parity):
            for x in range(squares):
                own_ref[x, 0] = value[:, x, parity]

        @pl.when(core != parity)
        def _(parity=parity):
            for x in range(squares):
                other_ref[x, 0] = value[:, x, parity]


def share_specs(count, rows, per_side, columns):
    spec = pl.BlockSpec((2, 1, count, rows, STEP_WIDTH), lambda j: (0, j // per_side, 0, 0, j % per_side))
    return [spec] * 2, [shaped((2, 2, count, rows, columns), LOW)] * 2


def weight_grad_kernel(lines_first, a_ref, b_ref, own_ref, other_ref):
    share_out(mm(a_ref[...], b_ref[0], TN).astype(LOW), own_ref, other_ref, lines_first)


def weight_grad(a, b, spec, chunks, count, rows, name, lines_first=False):
    per_side = chunks // 2
    out_specs, out_shape = share_specs(count, rows, per_side, per_side * STEP_WIDTH)
    if lines_first:
        spec_out = pl.BlockSpec((count, 2, 1, rows, STEP_WIDTH), lambda j: (0, 0, j // per_side, 0, j % per_side))
        out_specs, out_shape = [spec_out] * 2, [shaped((count, 2, 2, rows, per_side * STEP_WIDTH), LOW)] * 2
    return pl.pallas_call(
        functools.partial(weight_grad_kernel, lines_first),
        grid=(chunks,),
        in_specs=[full(a.shape), spec],
        out_specs=out_specs,
        out_shape=out_shape,
        compiler_params=params(60),
        cost_estimate=cost(9 * 1.1e9, 9 * 2e6),
        name=name,
    )(a, b)


def inner_kernel(per_side, down_count, f_ref, d_ref, h_ref, r_ref, n_ref, i_ref, norms_ref, *refs):
    downs, ups = refs[:down_count], refs[down_count : down_count + 10]
    own_ref, other_ref, g_ref, a_ref, ng_ref, wd, ds, wu, us, acc = refs[down_count + 10 :]
    j = pl.program_id(0)
    width = d_ref.shape[2]

    @pl.when(j == 0)
    def _():
        load_lines(downs, wd, ds, width, per_side)
        load_weights(ups, wu, us, 0, width, per_side)
        acc[...] = r_ref[...]

    ready(wd, ds, j)
    grad = (mm(f_ref[...], matrix(wd, j)) * d_ref[0].astype(F32)).astype(LOW)
    share_out(mm(h_ref[...], grad, TN).astype(LOW), own_ref, other_ref)
    ready(wu, us, j)
    acc[...] += mm(grad, matrix(wu, j), NT)

    @pl.when(j == 2 * per_side - 1)
    def _():
        gain = norms_ref[0:1]

        def rows(r, held):
            dy, normed = acc[r], n_ref[r]
            back = unnormalize(dy * gain, normed, i_ref[r][:, :1])
            g_ref[r] = back
            a_ref[r] = back.astype(LOW)
            return held[0] + fold(dy * normed), held[1] + fold(dy)

        none = jnp.zeros((8, acc.shape[1]), F32)
        gains, shifts = by_rows(acc.shape[0], rows, (none, none))
        ng_ref[...] = jnp.concatenate(
            [jnp.sum(gains, axis=0, keepdims=True), jnp.sum(shifts, axis=0, keepdims=True), none[:6]], axis=0
        )


def inner_back(feed_grad, slope, hidden, second_grad, normed, inverse, norms, downs, ups, rows, columns):
    chunks, total, width = slope.shape
    shape = normed.shape
    count = ups[0].shape[0]
    out_specs, out_shape = share_specs(count, rows, chunks // 2, columns)
    once = pl.Buffered(1)

    def held(a):
        return pl.BlockSpec(a.shape, lambda j: (0,) * a.ndim, pipeline_mode=once)

    return pl.pallas_call(
        functools.partial(inner_kernel, chunks // 2, len(downs)),
        grid=(chunks,),
        in_specs=[held(feed_grad), pl.BlockSpec((1, total, width), lambda j: (j, 0, 0))]
        + [held(a) for a in (hidden, second_grad, normed, inverse, norms)]
        + [ANYWHERE] * (len(downs) + 10),
        out_specs=out_specs + [full(shape), full(shape), full(norms.shape)],
        out_shape=out_shape + [shaped(shape, F32), shaped(shape, LOW), shaped(norms.shape, F32)],
        scratch_shapes=chunk_buffer((count, rows), chunks, width) * 2 + [pltpu.VMEM(shape, F32)],
        compiler_params=params(60),
        cost_estimate=cost(32 * 1.1e9, 32 * 2e6),
        name="inner_back",
    )(feed_grad, slope, hidden, second_grad, normed, inverse, norms, *downs, *ups)


def out_kernel(column, a_ref, ctx_ref, one_ref, two_ref, own_in, other_in, *refs):
    pieces = refs[:10]
    own_ref, other_ref, o_ref, w, sem, tiles, out_sem = refs[10:]
    _, _, x, z, rows, _ = tiles.shape
    width = w.shape[5]
    core = lax.axis_index("c")
    load_weights(pieces, w, sem, column, width, 1)
    norm_grads = jnp.concatenate([one_ref[0:2], two_ref[0:2], one_ref[2:6]], axis=0)
    for y in range(2):
        grad = mm(a_ref[...], ctx_ref[:, y * width : (y + 1) * width], TN).astype(LOW).reshape(z, x, 2, rows, width)
        for parity in range(2):
            slot = (parity + core) % 2
            for at_x in range(x):
                tiles[slot, y, at_x, :, :, :width] = grad[:, at_x, parity]
            for at in range(z * x):
                cell = norm_grads[:, (at * 2 + parity) * rows : (at * 2 + parity + 1) * rows]
                cell = jnp.concatenate([cell, jnp.zeros((8, 128 - rows), F32)], axis=1)
                cell = jnp.concatenate([cell, jnp.zeros((rows - 8, 128), F32)], axis=0)
                tiles[slot, y, at % x, at // x, :, width:] = cell.astype(LOW)
    copies = []
    for slot, ref in enumerate((own_ref, other_ref)):
        for y in range(2):
            copies.append(
                pltpu.make_async_copy(
                    tiles.at[slot, y], ref.at[:, y, :, :, pl.ds(column, width + 128)], out_sem.at[slot, y]
                )
            )
    for copy in copies:
        copy.start()
    for y in range(2):
        ready(w, sem, y)
        o_ref[:, y * width : (y + 1) * width] = mm(a_ref[...], matrix(w, y)).astype(LOW)
    for copy in copies:
        copy.wait()


def out_back(branch_grad, context, one, two, own, other, pieces, rows, column):
    count, width = pieces[0].shape[0], STEP_WIDTH
    inside = pl.BlockSpec(memory_space=pltpu.VMEM)
    return pl.pallas_call(
        functools.partial(out_kernel, column),
        in_specs=[inside] * 4 + [ANYWHERE] * 12,
        out_specs=[ANYWHERE, ANYWHERE, inside],
        out_shape=[shaped(own.shape, LOW), shaped(other.shape, LOW), shaped(context.shape, LOW)],
        scratch_shapes=chunk_buffer((count, rows), 2, width)
        + [pltpu.VMEM((2, 2, 2, count, rows, width + 128), LOW), pltpu.SemaphoreType.DMA((2, 2))],
        input_output_aliases={4: 0, 5: 1},
        compiler_params=params(60),
        cost_estimate=cost(4 * 1.1e9, 4 * 2e6),
        name="out_back",
    )(branch_grad, context, one, two, own, other, *pieces)


def attend_back_kernel(q_ref, k_ref, v_ref, bias_ref, l_ref, g_ref, o_ref):
    k, v, grad = k_ref[0], v_ref[0], g_ref[...]
    lane = lax.broadcasted_iota(jnp.int32, k.shape, 1)
    scale = HEAD**-0.5
    queries = q_ref[0]
    queries_turned, grad_turned = queries.T, grad.T
    outs = []
    for h, (q, own_grad) in enumerate(zip(head_parts(queries, lane, scale), head_parts(grad, lane))):
        log_total = l_ref[:, h * HEAD : h * HEAD + 1]
        probs = jnp.exp(mm(q, k, NT) + bias_ref[...].astype(F32) - log_total)
        prob_grad = mm(own_grad, v, NT)
        score_grad = probs * (prob_grad - jnp.sum(probs * prob_grad, axis=-1, keepdims=True))
        score_grad = score_grad.astype(LOW)
        mine = slice(h * HEAD, (h + 1) * HEAD)
        outs.append(
            (mm(score_grad, k) * scale, mm(queries_turned[mine], score_grad) * scale, mm(grad_turned[mine], probs.astype(LOW)))
        )
    o_ref[0] = jnp.where(lane < HEAD, outs[0][0], outs[1][0]).astype(LOW)
    for i in (1, 2):
        o_ref[i] = jnp.concatenate([outs[0][i], outs[1][i]], axis=0).T.astype(LOW)


def final_rows_kernel(own_ref, other_ref, o_ref):
    y = lax.axis_index("y")
    for place in range(2):

        @pl.when(y == place)
        def _(place=place):
            o_ref[:, place] = own_ref[...]
            o_ref[:, 1 - place] = other_ref[...]


def final_rows(own, other):
    total, width = own.shape
    block = pl.BlockSpec((ROWS_AT_ONCE, width), lambda i: (i, 0))
    both = pl.pallas_call(
        final_rows_kernel,
        grid=(pl.cdiv(total, ROWS_AT_ONCE),),
        in_specs=[block, block],
        out_specs=pl.BlockSpec((ROWS_AT_ONCE, 2, width), lambda i: (i, 0, 0)),
        out_shape=shaped((total, 2, width), own.dtype),
        compiler_params=params(60),
        name="final_rows",
    )(own, other)
    return both.transpose(1, 0, 2)


def attention_back(qkv, bias, logs, grad):
    total, width = grad.shape
    pairs = width // 128
    column = pl.BlockSpec((total, 128), lambda g: (0, g))
    return pl.pallas_call(
        attend_back_kernel,
        grid=(pairs,),
        in_specs=pair_specs(total, pairs // 2) + [full(bias.shape), column, column],
        out_specs=pl.BlockSpec((3, total, 128), lambda g: (0, 0, g)),
        out_shape=shaped((3, total, width), LOW),
        compiler_params=params(60),
        cost_estimate=cost(25 * 1.1e9, 25 * 2e6),
        name="attention_back",
    )(qkv, qkv, qkv, bias, logs, grad)


def qkv_back_kernel(per_side, x_ref, g_ref, r_ref, *refs):
    pieces, (own_ref, other_ref, o_ref, w, sem, acc) = refs[:10], refs[10:]
    j = pl.program_id(0)

    @pl.when(j == 0)
    def _():
        load_weights(pieces, w, sem, 0, g_ref.shape[2], per_side)

    grad = g_ref[0]
    share_out(mm(x_ref[...], grad, TN).astype(LOW), own_ref, other_ref)
    ready(w, sem, j)
    term = mm(grad, matrix(w, j), NT)

    @pl.when(j == 0)
    def _():
        acc[...] = r_ref[...] + term

    @pl.when(j > 0)
    def _():
        acc[...] += term

    @pl.when(j == 2 * per_side - 1)
    def _():
        o_ref[...] = acc[...].astype(LOW)


def qkv_back(x, grads, first_grad, pieces, rows):
    count, width = pieces[0].shape[0], STEP_WIDTH
    per_side = grads.shape[0]
    shape = first_grad.shape
    out_specs, out_shape = share_specs(count, rows, per_side, per_side * width)
    return pl.pallas_call(
        functools.partial(qkv_back_kernel, per_side),
        grid=(2 * per_side,),
        in_specs=[full(shape), pl.BlockSpec((1, shape[0], width), lambda j: (j % per_side, 0, j // per_side)), full(shape)]
        + [ANYWHERE] * 10,
        out_specs=out_specs + [full(shape)],
        out_shape=out_shape + [shaped(shape, LOW)],
        scratch_shapes=chunk_buffer((count, rows), 2 * per_side, width) + [pltpu.VMEM(shape, F32)],
        compiler_params=params(60),
        cost_estimate=cost(16 * 1.1e9, 16 * 2e6),
        name="qkv_back",
    )(x, grads, first_grad, *pieces)


def at(a, index, axis):
    return lax.dynamic_index_in_dim(a, index, axis, keepdims=False)


def chip_term(own, other, shift):
    x, y = place_xy(ring_place() + shift)
    return at(at(own, x, 0), y, 0).astype(F32) + at(at(other, x, 0), y, 0).astype(F32)


def ring_pair(to_right, to_left):
    return send(to_right, ("x", "y"), RING), send(to_left, ("x", "y"), RING_BACK)


def far_terms(take):
    far = take(2).astype(LOW)
    half = far.shape[0] // 2
    return far[:half], far[half:]


def near_terms(take, from_left, from_right):
    half = from_left.shape[0]
    right, left = take(1).astype(F32), take(-1).astype(F32)
    to_right = jnp.concatenate([right[:half] + from_left.astype(F32), right[half:]]).astype(LOW)
    to_left = jnp.concatenate([left[:half], left[half:] + from_right.astype(F32)]).astype(LOW)
    return to_right, to_left


def chip_terms(own, other):
    return lambda shift: chip_term(own, other, shift)


def square_terms(square):
    def take(shift):
        x, y = place_xy(ring_place() + shift)
        return at(at(square, x, 0), y, 0)

    return take


def line_terms(own, other, from_left, from_right):
    column = chip_term(own, other, 0) + from_left.astype(F32) + from_right.astype(F32)
    z = lax.axis_index("z")
    return [at(column, z, 0)] + [at(column, z ^ k, 0).astype(LOW) for k in range(1, column.shape[0])]


def line_send(terms):
    return [send(term, "z", partners(k + 1)) for k, term in enumerate(terms[1:])]


def total_of(own, others):
    for other in others:
        own = own + other.astype(F32)
    return own


def sum_over_all(value):
    value = value + send(value, "c", SWAP)
    square = [send(value, ("x", "y"), tuple((i, i ^ k) for i in range(4))) for k in (1, 2, 3)]
    value = (value + square[0]) + (square[1] + square[2])
    column = [send(value, "z", partners(k)) for k in (1, 2, 3)]
    return (value + column[0]) + (column[1] + column[2])


def pad_rows(a, total):
    return jnp.pad(a, ((0, total - a.shape[0]), (0, 0)))


def mask_bias(doc_row, reset_row, live, total):
    kinds = jnp.concatenate([jnp.full((MEM,), -1, jnp.int32), doc_row, jnp.full((MEM,), -2, jnp.int32)])
    real = kinds.shape[0]
    kinds = jnp.pad(kinds, (0, total - real), constant_values=-3)
    place = jnp.arange(total, dtype=jnp.int32)
    choose = kinds[:, None] == jnp.arange(reset_row.shape[0], dtype=jnp.int32)[None, :]
    reset_query = jnp.sum(jnp.where(choose, reset_row[None, :], 0), axis=1)
    same = kinds[:, None] == kinds[None, :]
    live_key = place < jnp.minimum(live, MEM)
    token_sees = same | (live_key[None, :] & (reset_query == 0)[:, None])
    memory_sees = ((place >= MEM) | live_key)[None, :]
    sees = jnp.where((kinds < 0)[:, None], memory_sees, token_sees) & (place < real)[None, :]
    return jnp.where(sees, 0.0, MASKED).astype(LOW)


def whole_segment(
    tokens,
    cotangent,
    doc_ids,
    reset_flags,
    mem_live,
    qkv_weight,
    qkv_moment,
    qkv_square,
    qkv_average,
    out_weight,
    out_moment,
    out_square,
    out_average,
    up_weight,
    up_moment,
    up_square,
    up_average,
    down_weight,
    down_moment,
    down_square,
    down_average,
    norm_params,
    norm_moment,
    norm_square,
    norm_average,
):
    y = lax.axis_index("y")
    rows, inner_part = up_weight.shape
    count = lax.axis_size("z")
    width = tokens.shape[2]
    part = qkv_weight.shape[2]
    real = tokens.shape[1]
    total = -(-real // ROWS_AT_ONCE) * ROWS_AT_ONCE

    def mine(a):
        return lax.dynamic_index_in_dim(a, y, 0, keepdims=False)

    qkv_block = jnp.concatenate([qkv_weight[k] for k in range(3)], axis=1).astype(LOW)
    norm_block = jnp.pad(norm_params.astype(LOW), ((0, rows - 4), (0, 128 - rows)))
    second_block = jnp.concatenate([up_weight.astype(LOW), out_weight.T.astype(LOW), norm_block], axis=1)
    down_block = down_weight.T.astype(LOW)

    pair_down = join_pair(down_block, send(down_block, "y", SWAP), "y")
    qkv_block = after(qkv_block, down_block)
    tokens, cotangent, doc_ids = after((tokens, cotangent, doc_ids), pair_down)
    x = pad_rows(mine(tokens), total)
    cot = pad_rows(mine(cotangent), total)
    bias = mask_bias(mine(doc_ids), mine(reset_flags), mine(mem_live), total)

    z_qkv = line_pieces(qkv_block)
    other_pair = send(pair_down, "x", SWAP)
    z_second = line_pieces(after(second_block, *z_qkv))
    column_qkv = join_column(after(tuple(z_qkv), x, cot, bias, other_pair))
    square_down = join_pair(pair_down, other_pair, "x")
    near_qkv = ring_near(column_qkv)
    far_qkv = ring_far(*near_qkv)
    w_qkv = both_cores((column_qkv,) + near_qkv + far_qkv)
    column_second = after(join_column(after(tuple(z_second), square_down)), *far_qkv)
    near_second = ring_near(column_second)
    square_down = after(square_down, *z_second)
    down_one, down_two = send(square_down, "z", partners(1)), send(square_down, "z", partners(2))

    qkv = project(after(x, column_second), w_qkv, rows)
    context, logs = attention(qkv, bias)

    near_second = after(near_second, context)
    far_second = ring_far(*near_second)
    w_second = both_cores((column_second,) + near_second + far_second)
    down_two = after(down_two, near_second[0])
    down_three = send(down_two, "z", partners(1))

    hidden, normed, inverse, norms, active, slope = up(x, after(context, down_two), w_second, rows, inner_part)

    w_down = both_cores((square_down, down_one, down_two, after(down_three, active)))
    result, second_grad, feed_grad, norm_two = down(active, normed, norms, cot, w_down, rows)

    chunks = active.shape[0]
    own_down, other = weight_grad(
        feed_grad,
        active,
        pl.BlockSpec((1, total, STEP_WIDTH), lambda j: (j, 0, 0)),
        chunks,
        count,
        rows,
        "down_grad",
        lines_first=True,
    )
    z, place_x = lax.axis_index("z"), lax.axis_index("x")

    def pair(own, other):
        own, other = jnp.where(y == 0, own, other), jnp.where(y == 0, other, own)
        return jnp.stack([own, other], axis=1).transpose(1, 0, 2)

    def term(own, other):
        return lambda k: at(own, z ^ k, 0).astype(F32) + at(other, z ^ k, 0).astype(F32)

    other_down = send(other, "c", SWAP)
    down_term = term(own_down, other_down)
    crossing = down_term(3).astype(LOW)
    crossed = send(crossing, "z", partners(1))
    own_result = result[:real]
    shared_result = send(own_result, "y", SWAP)
    columns = inner_part + part + 128
    own, other, first_grad, branch_grad, norm_one = inner_back(
        after(feed_grad, crossing, own_result),
        slope,
        hidden,
        second_grad,
        normed,
        inverse,
        norms,
        w_down,
        w_second,
        rows,
        columns,
    )
    crossed, shared_result = after(crossed, branch_grad), after(shared_result, branch_grad)
    own_second, other, context_grad = out_back(
        after(branch_grad, crossed, shared_result),
        context,
        norm_one,
        norm_two,
        own,
        other,
        w_second,
        rows,
        inner_part,
    )
    other_second = send(other, "c", SWAP)
    crossed = after(crossed, own_second)
    one, two = down_term(1).astype(LOW), (down_term(2) + crossed.astype(F32)).astype(LOW)
    from_one, from_two = send(one, "z", partners(1)), send(two, "z", partners(2))
    take_second = chip_terms(own_second, after(other_second, one, two))
    far = far_terms(take_second)
    far_second = ring_pair(*far)
    grads = attention_back(qkv, bias, logs, after(context_grad, *far))

    far_second = after(far_second, grads)
    near = near_terms(take_second, *far_second)
    near_second = ring_pair(*near)
    from_one, from_two = after(from_one, *near), after(from_two, *near)
    square = down_term(0) + from_one.astype(F32) + from_two.astype(F32)
    to_x = at(square, 1 - place_x, 0).astype(LOW)
    own_qkv, other, own_grad = qkv_back(after(x, to_x), grads, first_grad, w_qkv, rows)
    near_second = after(near_second, own_qkv)
    from_x = send(after(to_x, *near_second), "x", SWAP)
    other_qkv = send(after(other, *near_second), "c", SWAP)
    shared_grad = send(after(own_grad[: total // 2], *near_second), "y", SWAP)
    column = chip_term(own_second, other_second, 0) + near_second[0].astype(F32) + near_second[1].astype(F32)
    crossing = at(column, z ^ 3, 0).astype(LOW)
    crossed = send(crossing, "z", partners(1))
    take_qkv = chip_terms(own_qkv, after(other_qkv, crossing))
    far = far_terms(take_qkv)
    far_qkv = ring_pair(*far)
    from_x, shared_grad = after(from_x, *far), after(shared_grad, *far)
    half = at(square, place_x, 0) + from_x.astype(F32)
    to_y = at(half, 1 - y, 0).astype(LOW)
    crossed = after(crossed, *far)
    one, two = at(column, z ^ 1, 0).astype(LOW), (at(column, z ^ 2, 0) + crossed.astype(F32)).astype(LOW)
    from_one, from_two = send(one, "z", partners(1)), send(two, "z", partners(2))
    far_qkv = after(far_qkv, one, two, to_y, shared_grad)
    near = near_terms(take_qkv, *far_qkv)
    near_qkv = ring_pair(*near)
    output = final_rows(own_result, after(shared_result, *near))
    near_qkv = after(near_qkv, output)
    from_one, from_two = after(from_one, *near), after(from_two, *near)
    second_sum = at(column, z, 0) + from_one.astype(F32) + from_two.astype(F32)
    line_qkv = line_terms(own_qkv, other_qkv, *after(near_qkv, second_sum))
    others_qkv = line_send(line_qkv)
    from_y = send(after(to_y, *line_qkv), "y", SWAP)
    last_rows = after(own_grad[total // 2 : real], *line_qkv)
    shared_grad = jnp.concatenate([shared_grad, send(last_rows, "y", SWAP)])
    down_sum = at(half, y, 0) + from_y.astype(F32)
    others_qkv = after(tuple(others_qkv), down_sum, shared_grad)
    input_grad = pair(own_grad[:real], shared_grad).astype(F32)
    qkv_sum = total_of(line_qkv[0], others_qkv)

    qkv_sum = qkv_sum.reshape(rows, 3, part).transpose(1, 0, 2)
    up_sum = second_sum[:, :inner_part]
    out_sum = second_sum[:, inner_part : inner_part + part].T
    norm_sum = second_sum[:4, inner_part + part : inner_part + part + rows]
    down_sum = down_sum.T
    local_squares = (
        jnp.sum(qkv_sum * qkv_sum)
        + jnp.sum(out_sum * out_sum)
        + jnp.sum(up_sum * up_sum)
        + jnp.sum(down_sum * down_sum)
        + jnp.sum(norm_sum * norm_sum) / lax.axis_size("y")
    )
    grad_norm = jnp.sqrt(sum_over_all(jnp.full((8, 128), local_squares))[0, 0])
    threshold = math.sqrt(4 * D * D + 2 * D * FF + 4 * D)
    factor = jnp.minimum(1.0, threshold / (grad_norm + 1e-06))
    new_qkv = adam_step(qkv_weight, qkv_moment, qkv_square, qkv_average, qkv_sum * factor, 0.02, 0.01)
    new_out = adam_step(out_weight, out_moment, out_square, out_average, out_sum * factor, 0.06, 0.01)
    new_up = adam_step(up_weight, up_moment, up_square, up_average, up_sum * factor, 0.02, 0.01)
    new_down = adam_step(down_weight, down_moment, down_square, down_average, down_sum * factor, 0.02, 0.01)
    new_norm = adam_step(norm_params, norm_moment, norm_square, norm_average, norm_sum * factor, 0.4, 0.0)
    return (output, input_grad, grad_norm) + new_qkv + new_out + new_up + new_down + new_norm


def solution(mesh):
    wide, narrow = mesh.shape["wide"], mesh.shape["narrow"]

    def placed(w, n):
        state = [P(None, w, n)] * 4 + [P(n, w)] * 4 + [P(w, n)] * 4 + [P(n, w)] * 4 + [P(None, w)] * 4
        return (
            tuple([P(w, None, None)] * 2 + [P(w, None)] * 2 + [P(w)] + state),
            tuple([P(w, None, None)] * 2 + [P()] + state),
        )

    def run(*args):
        if narrow == 2 and wide == 16 and args[0].shape[0] == wide * narrow:
            body = whole_segment
            grid = jax.sharding.Mesh(mesh.devices.reshape(wide // 4, 2, 2, 2), ("z", "x", "c", "y"))
            ins, outs = placed(("z", "x", "c"), "y")
        else:
            body, grid = shared_rows, mesh
            ins, outs = placed("wide", "narrow")
        return jax.shard_map(body, mesh=grid, in_specs=ins, out_specs=outs, check_vma=False)(*args)

    return run
```
